32 devices in a mesh: walkers: 8 (over z, y), orb: 4 (over x, core).
Axes of the slice: x: 2, y: 2, z: 4, core: 2. Of those that a mesh axis runs over, the one named last changes fastest.
Arguments:
- inverse: float32 [32, 2, 128, 128], P('walkers', None, 'orb'), as said below
- slater: float32 [32, 2, 128, 128], P('walkers', None, 'orb'), may hold values from -1 to 3, as said below
- positions: float32 [32, 3, 256], P('walkers'), may hold values from -2 to 10
- displacements: float32 [32, 3, 256], P('walkers'), may hold values from -0.6 to 0.6
- move_order: int32 [32, 2, 128], P('walkers'), may hold values from 0 to 127, each once within a row
- accepted: int32 [32, 2, 32], P('walkers'), may hold values 0 or 1
- counts: int32 [32], P('walkers'), may hold values from 0 to 2, as said below
- log_amp: float32 [32], P('walkers'), may hold values from -4 to 4
- centers: float32 [3, 1024], replicated, may hold values from 0 to 8
- exponents: float32 [1024], replicated, may hold values from 0.3 to 3
- orbitals: float32 [2, 128, 1024], P(None, 'orb'), may hold values from -0.36 to 0.36
- jastrow: float32 [4], replicated, may hold values from 0.2 to 0.6
Outputs:
- inverse_new: float32 [32, 2, 128, 128], P('walkers', None, 'orb')
- slater_new: float32 [32, 2, 128, 128], P('walkers', None, 'orb')
- positions_new: float32 [32, 3, 256], P('walkers')
- log_amp_new: float32 [32], P('walkers')
- local_energy_new: float32 [32], P('walkers')
- energy_mean: float32 [], replicated
The draws below stay inside these ranges and needn't reach their ends.
Inputs may be any that keep to these rules, and one draw needn't show every extreme that they name: For every walker and spin, inverse is the inverse of the transpose of slater: the sum over o of slater[w, s, o, e] * inverse[w, s, o, f] is 1 when e = f and 0 otherwise, up to float32 rounding. `slater`: orbital values at the current positions. All counts sum to 32; for every whole m, the counts of the first m * 4 walkers sum to a value within 2 of m * 4, and both ends of that band are reached.
All inputs are finite; a program needn't handle non-finite values. No bound on the sum of `accepted` on one device may be relied on, other than what follows from the above.
Results may differ from the reference program's by a relative error of at most 0.0003.
Values sent between devices are 32-bit elements; how exact they have to be, the bound alone decides.
No kernel may reach another device: no remote copies, remote signals or barrier semaphores. Data moves between devices by JAX's collectives and lax.ppermute only.
A program may use at most 64 MiB of HBM per device.

```python
import math
import jax
import jax.numpy as jnp
from jax import lax

NEL = 128
NB = 1024
K = 32
WINDOWS = 1
MOVES = 32
W_DEV = 4
WALKERS = 32


def slater_matrices(key):
    base = jax.random.fold_in(key, 7)
    shape = (WALKERS, 2, NEL, NEL)
    noise = jnp.clip(jax.random.normal(base, shape, jnp.float32), -4.0, 4.0)
    return 2.0 * jnp.eye(NEL, dtype=jnp.float32) + 0.5 * noise / math.sqrt(NEL)


def draw_slater(key, part):
    return slater_matrices(key)


def draw_inverse(key, part):
    return jnp.swapaxes(jnp.linalg.inv(slater_matrices(key)), 2, 3)


def draw_positions(key, part):
    walker_ids = jnp.arange(WALKERS).astype(jnp.float32)
    side = 4.0 * jnp.power(3.0, walker_ids / max(WALKERS - 1, 1))
    shape = (WALKERS, 3, 2 * NEL)
    cloud = jax.random.uniform(key, shape, jnp.float32, -0.5, 0.5)
    return 4.0 + side[:, None, None] * cloud


def draw_counts(key, part):
    devices = WALKERS // W_DEV
    half = W_DEV // 2
    keys = jax.random.split(key, 3)
    inner = jax.random.randint(keys[0], (devices - 1,), -half, half + 1)
    chosen = jax.random.randint(keys[1], (), 1, devices - 1)
    labels = jnp.arange(1, devices)
    inner = jnp.where(labels == chosen, -half, jnp.where(labels == chosen + 1, half, inner))
    edge = jnp.zeros((1,), jnp.int32)
    drift = jnp.concatenate([edge, inner.astype(jnp.int32), edge])
    totals = W_DEV + drift[1:] - drift[:-1]
    orders = jax.vmap(lambda piece: jax.random.permutation(piece, 2 * W_DEV))(jax.random.split(keys[2], devices))
    picked = (orders < totals[:, None]).astype(jnp.int32)
    return picked.reshape(devices, W_DEV, 2).sum(axis=2).reshape(WALKERS)


def touch_ends(drawn, rng, least, largest):
    spot = [jax.random.randint(jax.random.fold_in(rng, axis), (), 0, length) for axis, length in enumerate(drawn.shape)]
    widest = drawn.shape.index(max(drawn.shape))
    beside = spot[:widest] + [(spot[widest] + 1) % drawn.shape[widest]] + spot[widest + 1:]
    return drawn.at[tuple(spot)].set(least).at[tuple(beside)].set(largest)


def block_levels(key, shape, cuts, low, top_value):
    def one(axis_at, shards_of):
        steps = jax.random.uniform(jax.random.fold_in(jax.random.fold_in(key, 6), axis_at), (shards_of,), jnp.float32, low / len(cuts), top_value / len(cuts))
        return jnp.repeat(jnp.exp(steps), shape[axis_at] // shards_of).reshape((-1,) + (1,) * (len(shape) - axis_at - 1))

    loudness = one(*cuts[0])
    for cut in cuts[1:]:
        loudness = loudness * one(*cut)
    return loudness


def scatter_about(rng, shape, width, bound, cuts=(), kind=jnp.bfloat16):
    drawn = jax.random.normal(rng, shape, jnp.float32) * width
    if len(cuts) > 0:
        drawn = block_levels(rng, shape, cuts, -0.22, 0.18) * drawn
    return jnp.clip(drawn, min=-bound, max=bound).astype(kind)


def setup_inputs(seed: int = 0) -> dict:
    arg_keys = jax.random.split(jax.random.key(seed), 13)
    inverse = draw_inverse(jax.random.fold_in(arg_keys[12], 71), 0)
    slater = draw_slater(jax.random.fold_in(arg_keys[12], 71), 0)
    positions = draw_positions(jax.random.fold_in(arg_keys[12], 71), 0)
    displacements = scatter_about(arg_keys[3], (WALKERS, 3, 2 * NEL), 0.2, 0.6, ((0, 8),), jnp.float32)
    move_order = jax.vmap(lambda own: jax.random.permutation(own, NEL))(jax.random.split(arg_keys[4], WALKERS * 2)).reshape((WALKERS, 2, NEL)).astype(jnp.int32)
    accepted = touch_ends((jax.random.randint(arg_keys[5], (WALKERS, 2, MOVES), 0, 4) < 3).astype(jnp.int32), jax.random.fold_in(arg_keys[5], 1), 0, 1)
    counts = draw_counts(jax.random.fold_in(arg_keys[12], 71), 0)
    log_amp = scatter_about(arg_keys[7], (WALKERS,), 1.0, 4.0, ((0, 8),), jnp.float32)
    centers = jnp.clip(jax.random.uniform(arg_keys[8], (3, NB), jnp.float32, 0.0, 8.0), 0.0, 8.0)
    exponents = jnp.clip(jnp.exp(jax.random.uniform(arg_keys[9], (NB,), jnp.float32, math.log(0.3), math.log(3.0))), 0.3, 3.0)
    orbitals = scatter_about(arg_keys[10], (2, NEL, NB), 0.06, 0.36, ((1, 4),), jnp.float32)
    jastrow = jnp.clip(jax.random.uniform(arg_keys[11], (4,), jnp.float32, 0.2, 0.6), 0.2, 0.6)
    return dict(inverse=inverse, slater=slater, positions=positions, displacements=displacements, move_order=move_order, accepted=accepted, counts=counts, log_amp=log_amp, centers=centers, exponents=exponents, orbitals=orbitals, jastrow=jastrow)


highest = lax.Precision.HIGHEST

def basis_values(points, centers, exponents):
    squares = jnp.zeros((centers.shape[1], points.shape[1]), jnp.float32)
    for component in range(3):
        offset = points[component][None, :] - centers[component][:, None]
        squares = squares + offset * offset
    return jnp.exp(-exponents[:, None] * squares)

def orbital_change(points, steps, centers, exponents, orbitals):
    count = points.shape[1] // 2
    differ = basis_values(points + steps, centers, exponents) - basis_values(points, centers, exponents)
    spin_up = jnp.dot(orbitals[0].astype(jnp.float32), differ[:, :count].astype(jnp.float32), precision=highest, preferred_element_type=jnp.float32)
    spin_down = jnp.dot(orbitals[1].astype(jnp.float32), differ[:, count:].astype(jnp.float32), precision=highest, preferred_element_type=jnp.float32)
    return jnp.stack([spin_up, spin_down])

def pair_terms(before, after, jastrow):
    total = before.shape[1]
    old_squares = jnp.zeros((total, total), jnp.float32)
    new_squares = jnp.zeros((total, total), jnp.float32)
    for component in range(3):
        old_offset = before[component][:, None] - before[component][None, :]
        new_offset = after[component][:, None] - after[component][None, :]
        old_squares = old_squares + old_offset * old_offset
        new_squares = new_squares + new_offset * new_offset
    spins = jnp.arange(total) // (total // 2)
    same = spins[:, None] == spins[None, :]
    height = jnp.where(same, jastrow[0], jastrow[1])
    falloff = jnp.where(same, jastrow[2], jastrow[3])
    old_dist = jnp.sqrt(old_squares)
    new_dist = jnp.sqrt(new_squares)
    change = jnp.sum(height * (new_dist / (1.0 + falloff * new_dist) - old_dist / (1.0 + falloff * old_dist)))
    soft = jnp.sum(1.0 / jnp.sqrt(new_squares + 1.0))
    return (change, soft)

def eliminate(coupling, change):
    size = coupling.shape[-1]
    matrix = jnp.concatenate([coupling, change], axis=-1)
    labels = jnp.arange(size)

    def sweep(index, carry):
        matrix, logsum = carry
        pivot_row = lax.dynamic_slice_in_dim(matrix, index, 1, matrix.ndim - 2)
        pivot = lax.dynamic_slice_in_dim(pivot_row, index, 1, matrix.ndim - 1)
        pivot_row = pivot_row / pivot
        column_now = lax.dynamic_slice_in_dim(matrix, index, 1, matrix.ndim - 1)
        mine = (labels == index)[:, None]
        matrix = jnp.where(mine, pivot_row, matrix - column_now * pivot_row)
        return (matrix, logsum + jnp.log(jnp.abs(pivot[..., 0, 0])))
    start = (matrix, jnp.zeros(coupling.shape[:-2], jnp.float32))
    matrix, logsum = lax.fori_loop(0, size, sweep, start)
    return (matrix[..., size:], logsum)

def reference(inverse, slater, positions, displacements, move_order, accepted, counts, log_amp, centers, exponents, orbitals, jastrow):

    def per_walker(pair):
        return orbital_change(pair[0], pair[1], centers, exponents, orbitals)
    orbital_shift = lax.map(per_walker, (positions, displacements))
    proposed = slater + orbital_shift
    labels = jnp.arange(NEL)
    current = inverse
    logdet = jnp.zeros(inverse.shape[:2], jnp.float32)
    for window in range(WINDOWS):
        chosen = move_order[:, :, window * K:(window + 1) * K]
        flags = accepted[:, :, window * K:(window + 1) * K]
        one_hot = (labels[None, None, :, None] == chosen[:, :, None, :]).astype(jnp.float32)
        proposed_cols = jnp.einsum('wsoe,wsek->wsok', proposed, one_hot, precision=highest)
        intersection = jnp.einsum('wsok,wsoe->wske', proposed_cols, current, precision=highest)
        unit_rows = jnp.swapaxes(one_hot, 2, 3)
        effective = jnp.where(flags[..., None] == 1, intersection, unit_rows)
        coupling = jnp.einsum('wske,wsel->wskl', effective, one_hot, precision=highest)
        solved, logsum = eliminate(coupling, effective - unit_rows)
        columns = jnp.einsum('wsoe,wsek->wsok', current, one_hot, precision=highest)
        current = current - jnp.einsum('wsok,wske->wsoe', columns, solved, precision=highest)
        logdet = logdet + logsum
    placed = (move_order[:, :, :MOVES, None] == labels[None, None, None, :]).astype(jnp.float32)
    applied = jnp.einsum('wsk,wske->wse', accepted.astype(jnp.float32), placed, precision=highest)
    slater_now = slater + orbital_shift * applied[:, :, None, :]
    positions_now = positions + displacements * applied.reshape(applied.shape[0], 1, 2 * NEL)

    def walker_pairs(pair):
        return pair_terms(pair[0], pair[1], jastrow)
    jastrow_change, soft_total = lax.map(walker_pairs, (positions, positions_now))
    log_now = log_amp + lax.optimization_barrier(jnp.sum(logdet, axis=1)) + 0.5 * jastrow_change
    energy = (soft_total - 2.0 * NEL) / (2.0 * NEL * (2 * NEL - 1))
    energy_mean = jnp.sum(counts.astype(jnp.float32) * energy) / WALKERS
    limits = jnp.cumsum(counts).astype(jnp.int32)
    slot_ids = jnp.arange(WALKERS).astype(jnp.int32)
    source = lax.optimization_barrier(jnp.sum((limits[None, :] <= slot_ids[:, None]).astype(jnp.int32), axis=1))
    inverse_new = jnp.take(current, source, axis=0)
    slater_new = jnp.take(slater_now, source, axis=0)
    positions_new = jnp.take(positions_now, source, axis=0)
    log_amp_new = jnp.take(log_now, source, axis=0)
    local_energy_new = jnp.take(energy, source, axis=0)
    return (inverse_new, slater_new, positions_new, log_amp_new, local_energy_new, energy_mean)
```

```python
import jax
import jax.numpy as jnp
from jax import lax
from jax.experimental import pallas as pl
from jax.experimental.pallas import tpu as pltpu
from jax.sharding import PartitionSpec as P

F32 = jnp.float32
highest = lax.Precision.HIGHEST
VMEM = pl.BlockSpec(memory_space=pltpu.VMEM)
SMEM = pl.BlockSpec(memory_space=pltpu.SMEM)
LANES = 128
INFO = 8


def nn(a, b):
    return lax.dot_general(
        a, b, (((1,), (0,)), ((), ())), precision=highest, preferred_element_type=F32
    )


def nt(a, b):
    return lax.dot_general(
        a, b, (((1,), (1,)), ((), ())), precision=highest, preferred_element_type=F32
    )


def tn(a, b):
    return lax.dot_general(
        a, b, (((0,), (0,)), ((), ())), precision=highest, preferred_element_type=F32
    )


def turned(rows):
    short = -rows.shape[0] % 8
    if short:
        rows = jnp.concatenate([rows, jnp.zeros((short, rows.shape[1]), F32)], axis=0)
    return jnp.transpose(rows)


def moves_of(order_ref, flags_ref):
    walkers, _, moves = flags_ref.shape
    nel = order_ref.shape[2]
    order = turned(
        jnp.concatenate([order_ref[w] for w in range(walkers)], axis=0).astype(F32)
    )
    flags = jnp.concatenate([flags_ref[w] for w in range(walkers)], axis=0).astype(F32)
    flags = turned(
        jnp.concatenate([flags, jnp.zeros((2 * walkers, nel - moves), F32)], axis=1)
    )
    cols = [order[:moves, i : i + 1] for i in range(2 * walkers)]
    keep = [flags[:moves, i : i + 1] for i in range(2 * walkers)]
    return cols, keep


def one_hots(cols, nel):
    moves = cols[0].shape[0]
    lanes = lax.broadcasted_iota(jnp.int32, (moves, nel), 1).astype(F32)
    return [(c == lanes).astype(F32) for c in cols]


def pick(counts_ref, index):
    walkers = counts_ref.shape[0]
    total = jnp.int32(0)
    source = jnp.int32(0)
    for w in range(walkers):
        total = total + counts_ref[w]
        source = source + (total <= index).astype(jnp.int32)
    return jnp.minimum(source, walkers - 1)


def total_of(counts_ref):
    total = jnp.int32(0)
    for w in range(counts_ref.shape[0]):
        total = total + counts_ref[w]
    return total


def blocks_of(nel):
    return ((0, 0, 1.0), (nel, nel, 1.0), (0, nel, 2.0))


def squares_of(cols, rows, a, b, nel):
    total = None
    for c in range(3):
        offset = cols[c][a : a + nel] - rows[c][:, b : b + nel]
        total = offset * offset if total is None else total + offset * offset
    return total


def energy_kernel(pos_ref, dis_ref, order_ref, flags_ref, counts_ref, now_ref, energy_ref, info_ref):
    walkers, _, both = pos_ref.shape
    nel = both // 2
    cols, keep = moves_of(order_ref, flags_ref)
    hots = one_hots(cols, nel)
    weighted = jnp.zeros((1, 1), F32)
    for w in range(walkers):
        applied = [
            jnp.sum(hots[2 * w + s] * keep[2 * w + s], axis=0, keepdims=True) for s in (0, 1)
        ]
        now = pos_ref[w] + dis_ref[w] * jnp.concatenate(applied, axis=1)
        now_ref[w] = now
        turn = turned(jnp.concatenate([now, jnp.zeros((5, both), F32)], axis=0))
        ncols = [turn[:, c : c + 1] for c in range(3)]
        nrows = [now[c : c + 1] for c in range(3)]
        soft = jnp.zeros((8, nel), F32)
        for a, b, weight in blocks_of(nel):
            squares = squares_of(ncols, nrows, a, b, nel)
            terms = lax.rsqrt(squares + 1.0)
            part = jnp.sum(terms.reshape(nel // 8, 8, nel), axis=0)
            soft = soft + (part if weight == 1.0 else part * weight)
        whole = jnp.sum(jnp.sum(soft, axis=0, keepdims=True), axis=1, keepdims=True)
        energy = (whole - 1.0 * both) / (1.0 * both * (both - 1))
        energy_ref[w : w + 1, :] = jnp.broadcast_to(energy, (1, energy_ref.shape[1]))
        weighted = weighted + energy * counts_ref[w].astype(F32)
    me = lax.axis_index("walkers")
    lanes = lax.broadcasted_iota(jnp.int32, info_ref.shape, 1)
    rows = lax.broadcasted_iota(jnp.int32, info_ref.shape, 0)
    number = total_of(counts_ref).astype(F32)
    info_ref[...] = jnp.where(
        lanes == me,
        jnp.where(rows == 0, number, jnp.where(rows == 1, weighted, 0.0)),
        0.0,
    )


def jastrow_kernel(pos_ref, now_ref, jas_ref, out_ref):
    walkers, _, both = pos_ref.shape
    nel = both // 2
    for w in range(walkers):
        old = pos_ref[w]
        new = now_ref[w]
        turn = turned(jnp.concatenate([old, new, jnp.zeros((2, both), F32)], axis=0))
        ocols = [turn[:, c : c + 1] for c in range(3)]
        ncols = [turn[:, 3 + c : 4 + c] for c in range(3)]
        orows = [old[c : c + 1] for c in range(3)]
        nrows = [new[c : c + 1] for c in range(3)]
        total = jnp.zeros((8, nel), F32)
        for a, b, weight in blocks_of(nel):
            kind = 0 if a == b else 1
            fall = jas_ref[2 + kind]
            osq = squares_of(ocols, orows, a, b, nel)
            nsq = squares_of(ncols, nrows, a, b, nel)
            od = jnp.sqrt(osq)
            nd = jnp.sqrt(nsq)
            terms = (nd - od) / ((1.0 + fall * nd) * (1.0 + fall * od))
            part = jnp.sum(terms.reshape(nel // 8, 8, nel), axis=0)
            total = total + part * (jas_ref[kind] * weight)
        whole = jnp.sum(jnp.sum(total, axis=0, keepdims=True), axis=1, keepdims=True)
        out_ref[w : w + 1, :] = jnp.broadcast_to(0.5 * whole, (1, out_ref.shape[1]))


def partial_kernel(
    pos_ref, dis_ref, order_ref, flags_ref, counts_ref, cen_ref, exp_ref, orb_ref, inv_ref,
    sla_ref, now_ref, energy_ref, part_ref, done_ref, pair_ref, odd_ref, differ_ref,
):
    walkers, _, both = pos_ref.shape
    nel = both // 2
    moves = flags_ref.shape[2]
    basis = cen_ref.shape[1]
    orbs = inv_ref.shape[2]
    cols, keep = moves_of(order_ref, flags_ref)
    hots = one_hots(cols, nel)
    for s in (0, 1):
        table = jnp.concatenate(
            [
                jnp.concatenate(
                    [
                        pos_ref[w, :, s * nel : (s + 1) * nel],
                        dis_ref[w, :, s * nel : (s + 1) * nel],
                        jnp.zeros((2, nel), F32),
                    ],
                    axis=0,
                )
                for w in range(walkers)
            ],
            axis=0,
        )
        points = nt(jnp.concatenate([hots[2 * w + s] for w in range(walkers)], axis=0), table)
        for w in range(walkers):
            mine = points[w * moves : (w + 1) * moves]
            old = [
                jnp.broadcast_to(mine[:, 8 * w + c : 8 * w + c + 1], (moves, LANES))
                for c in range(3)
            ]
            new = [
                jnp.broadcast_to(
                    mine[:, 8 * w + c : 8 * w + c + 1] + mine[:, 8 * w + 3 + c : 8 * w + 4 + c],
                    (moves, LANES),
                )
                for c in range(3)
            ]
            for j in range(0, basis, LANES):
                osq = None
                nsq = None
                for c in range(3):
                    row = cen_ref[c : c + 1, j : j + LANES]
                    do = old[c] - row
                    dn = new[c] - row
                    osq = do * do if osq is None else osq + do * do
                    nsq = dn * dn if nsq is None else nsq + dn * dn
                rate = -exp_ref[:, j : j + LANES]
                differ_ref[s, w * moves : (w + 1) * moves, j : j + LANES] = jnp.exp(
                    rate * nsq
                ) - jnp.exp(rate * osq)
    for s in (0, 1):
        shift = nt(differ_ref[s], orb_ref[s])
        for w in range(walkers):
            i = 2 * w + s
            mine = shift[w * moves : (w + 1) * moves]
            proposed = mine + nt(hots[i], sla_ref[w, s])
            part = nn(proposed, inv_ref[w, s])
            part_ref[i * moves : (i + 1) * moves, :] = part * keep[i]
            done_ref[w, s] = sla_ref[w, s] + tn(mine, hots[i] * keep[i])
    half = walkers // 2
    per = 2 * orbs
    tail = half * per
    width = both // LANES
    parity = lax.rem(lax.axis_index("walkers"), 2)
    number = total_of(counts_ref)
    for pay, goes_up in ((pair_ref, parity == 0), (odd_ref, parity == 1)):
        pay[tail:, :] = jnp.zeros((pay.shape[0] - tail, LANES), F32)
        for j in range(half):
            index = jnp.where(goes_up, number - half + j, j)
            source = pick(counts_ref, index)
            for s in (0, 1):
                pay[j * per + s * orbs : j * per + (s + 1) * orbs, :] = done_ref[source, s]
            spot = now_ref[source]
            for h in range(width):
                at = tail + (j * width + h) * 3
                pay[at : at + 3, :] = spot[:, h * LANES : (h + 1) * LANES]
            at = tail + half * width * 3 + j
            pay[at : at + 1, :] = energy_ref[pl.ds(source, 1), :]


def add_kernel(mine_ref, other_ref, info_ref, info_other_ref, out_ref):
    rows = mine_ref.shape[0]
    out_ref[:rows, :] = mine_ref[...] + other_ref[...]
    out_ref[rows:, :] = info_ref[...] + info_other_ref[...]


def update_kernel(
    sum_ref, got_ref, inv_ref, order_ref, flags_ref, counts_ref, amp_ref, jas_ref,
    cur_ref, log_ref, info_ref, pair_ref, odd_ref,
):
    walkers, _, orbs, nel = inv_ref.shape
    moves = flags_ref.shape[2]
    count = 2 * walkers
    cols, keep = moves_of(order_ref, flags_ref)
    hots = one_hots(cols, nel)
    eye = (
        lax.broadcasted_iota(jnp.int32, (moves, moves), 0)
        == lax.broadcasted_iota(jnp.int32, (moves, moves), 1)
    ).astype(F32)
    tiles = moves // 8
    left = []
    right = []
    columns = []
    for i in range(count):
        at = slice(i * moves, (i + 1) * moves)
        change = sum_ref[at, :] + got_ref[at, :] - hots[i] * keep[i]
        coupling = nt(change, hots[i]) + eye
        columns.append(nt(inv_ref[i // 2, i % 2], hots[i]))
        left.append([coupling[8 * t : 8 * t + 8] for t in range(tiles)])
        right.append([change[8 * t : 8 * t + 8] for t in range(tiles)])
    info_ref[...] = sum_ref[count * moves :, :] + got_ref[count * moves :, :]
    lanes = lax.broadcasted_iota(jnp.int32, (1, nel), 1)
    sub = lax.broadcasted_iota(jnp.int32, (8, nel), 0)
    pivots = [jnp.ones((1, nel), F32) for _ in range(count)]
    for k in range(moves):
        own, line = k // 8, k % 8
        for i in range(count):
            wide = [
                jnp.broadcast_to(left[i][t][:, k : k + 1], (8, nel)) for t in range(tiles)
            ]
            pivot = wide[own][line : line + 1]
            pivots[i] = jnp.where(lanes == k, pivot, pivots[i])
            scale = 1.0 / pivot
            lrow = left[i][own][line : line + 1] * scale[:, :moves]
            rrow = right[i][own][line : line + 1] * scale
            for t in range(tiles):
                nl = left[i][t] - wide[t][:, :moves] * lrow
                nr = right[i][t] - wide[t] * rrow
                if t == own:
                    nl = jnp.where(sub[:, :moves] == line, lrow, nl)
                    nr = jnp.where(sub == line, rrow, nr)
                left[i][t] = nl
                right[i][t] = nr
    for i in range(count):
        solved = jnp.concatenate(right[i], axis=0)
        cur_ref[i // 2, i % 2] = inv_ref[i // 2, i % 2] - nn(columns[i], solved)
    log_ref[...] = jnp.zeros(log_ref.shape, F32)
    for w in range(walkers):
        both = jnp.log(jnp.abs(pivots[2 * w])) + jnp.log(jnp.abs(pivots[2 * w + 1]))
        log_ref[w : w + 1, :] = (
            jnp.broadcast_to(jnp.sum(both, axis=1, keepdims=True), (1, nel))
            + jas_ref[w : w + 1, :]
            + amp_ref[w]
        )
    half = walkers // 2
    per = 2 * orbs
    tail = half * per
    parity = lax.rem(lax.axis_index("walkers"), 2)
    number = total_of(counts_ref)
    for pay, goes_up in ((pair_ref, parity == 0), (odd_ref, parity == 1)):
        pay[tail : tail + INFO, :] = info_ref[...]
        pay[tail + INFO :, :] = jnp.zeros((pay.shape[0] - tail - INFO, LANES), F32)
        for j in range(half):
            index = jnp.where(goes_up, number - half + j, j)
            source = pick(counts_ref, index)
            for s in (0, 1):
                pay[j * per + s * orbs : j * per + (s + 1) * orbs, :] = cur_ref[source, s]
            at = tail + INFO + j
            pay[at : at + 1, :] = log_ref[pl.ds(source, 1), :]


def place_kernel(
    counts_ref, cur_ref, done_ref, now_ref, energy_ref, log_ref, info_ref,
    pair_s_ref, odd_s_ref, pair_i_ref, odd_i_ref,
    inv_out, sla_out, pos_out, log_out, energy_out, mean_out,
):
    walkers, _, orbs, nel = cur_ref.shape
    both = now_ref.shape[2]
    width = both // LANES
    half = walkers // 2
    per = 2 * orbs
    tail = half * per
    me = lax.axis_index("walkers")
    parity = lax.rem(me, 2)
    info = info_ref[...] + pair_i_ref[tail : tail + INFO, :]
    lanes = lax.broadcasted_iota(jnp.int32, (1, info.shape[1]), 1)
    before = jnp.sum(jnp.where(lanes < me, info[0:1], 0.0)).astype(jnp.int32)
    groups = lax.axis_size("walkers")
    mean = jnp.sum(info[1:2], axis=1, keepdims=True)
    mean_out[...] = mean / (1.0 * walkers * groups)
    number = total_of(counts_ref)
    spots = lax.broadcasted_iota(jnp.int32, (1, walkers), 1)

    def put(j, inverse, slater, spot, log, energy):
        for s in (0, 1):
            inv_out[j, s] = inverse(s)
            sla_out[j, s] = slater(s)
        for h in range(width):
            pos_out[j, :, h * LANES : (h + 1) * LANES] = spot(h)
        log_out[...] = jnp.where(spots == j, log[:, :walkers], log_out[...])
        energy_out[...] = jnp.where(spots == j, energy[:, :walkers], energy_out[...])

    log_out[...] = jnp.zeros(log_out.shape, F32)
    energy_out[...] = jnp.zeros(energy_out.shape, F32)
    for j in range(walkers):
        index = me * walkers + j - before
        low = index < 0
        high = index >= number

        @pl.when(jnp.logical_not(low | high))
        def _():
            w = pick(counts_ref, index)
            put(
                j,
                lambda s: cur_ref[w, s],
                lambda s: done_ref[w, s],
                lambda h: now_ref[w, :, h * LANES : (h + 1) * LANES],
                log_ref[pl.ds(w, 1), :],
                energy_ref[pl.ds(w, 1), :],
            )

        def received(late, early):
            i = jnp.clip(jnp.where(low, index + half, index - number), 0, half - 1)
            put(
                j,
                lambda s: late[pl.ds(i * per + s * orbs, orbs), :],
                lambda s: early[pl.ds(i * per + s * orbs, orbs), :],
                lambda h: early[pl.ds(tail + (i * width + h) * 3, 3), :],
                late[pl.ds(tail + INFO + i, 1), :],
                early[pl.ds(tail + half * width * 3 + i, 1), :],
            )

        on_pair = (low & (parity == 1)) | (high & (parity == 0))

        @pl.when(on_pair)
        def _():
            received(pair_i_ref, pair_s_ref)

        @pl.when((low | high) & jnp.logical_not(on_pair))
        def _():
            received(odd_i_ref, odd_s_ref)


def call(kernel, outs, in_specs, scratch=(), flops=0, name=None):
    return pl.pallas_call(
        kernel,
        out_shape=outs,
        in_specs=in_specs,
        out_specs=jax.tree.map(lambda _: VMEM, outs),
        scratch_shapes=list(scratch),
        compiler_params=pltpu.CompilerParams(vmem_limit_bytes=32 * 2**20),
        cost_estimate=pl.CostEstimate(flops=flops, bytes_accessed=2**18, transcendentals=0),
        name=name,
    )


def shape(*dims):
    return jax.ShapeDtypeStruct(dims, F32)


def body(
    inverse, slater, positions, displacements, move_order, accepted, counts, log_amp, centers,
    exponents, orbitals, jastrow,
):
    walkers, _, orbs, nel = inverse.shape
    moves = accepted.shape[2]
    both = positions.shape[2]
    basis = centers.shape[1]
    groups = lax.axis_size("walkers")
    members = lax.axis_size("orb")
    wide = max(LANES, groups)
    half = walkers // 2
    per = 2 * orbs
    count = 2 * walkers
    tall = half * per + 16

    pairs = [(i, i ^ 1) for i in range(groups)]
    odds = [(i, i + 1) for i in range(1, groups - 1, 2)]
    odds = odds + [(b, a) for a, b in odds]

    now, energy, info = call(
        energy_kernel,
        (shape(walkers, 3, both), shape(walkers, LANES), shape(INFO, wide)),
        [VMEM, VMEM, VMEM, VMEM, SMEM],
        flops=10**6,
        name="energy",
    )(positions, displacements, move_order, accepted, counts)

    hops = members * 2
    step = hops
    while step < groups:
        info = info + lax.ppermute(info, "walkers", [(i, i ^ step) for i in range(groups)])
        step *= 2
    joint = [
        (d * members + o, (d ^ (2 * o)) * members + o)
        for d in range(groups)
        for o in range(members)
        if 2 * o < groups
    ]
    info = lax.ppermute(info, ("walkers", "orb"), joint)

    part, done, pair_s, odd_s = call(
        partial_kernel,
        (
            shape(count * moves, nel),
            shape(walkers, 2, orbs, nel),
            shape(tall, LANES),
            shape(tall, LANES),
        ),
        [VMEM, VMEM, VMEM, VMEM, SMEM] + [VMEM] * 7,
        scratch=[pltpu.VMEM((2, walkers * moves, basis), F32)],
        flops=10**6,
        name="partial",
    )(
        positions, displacements, move_order, accepted, counts, centers,
        exponents.reshape(1, basis), orbitals, inverse, slater, now, energy,
    )

    total = part
    step = 1
    while step < members:
        partner = [(o, o ^ step) for o in range(members)]
        if step == 1:
            other = lax.ppermute(part, "orb", partner)
            info_other = lax.ppermute(info, "orb", partner)
            total = call(
                add_kernel,
                shape(count * moves + INFO, nel),
                [VMEM] * 4,
                flops=10**5,
                name="add",
            )(part, other, info, info_other)
        else:
            got = lax.ppermute(total, "orb", partner)
        step *= 2

    change = call(
        jastrow_kernel, shape(walkers, LANES), [VMEM, VMEM, SMEM], flops=10**6, name="jastrow"
    )(positions, now, jastrow)

    pair_s = lax.ppermute(pair_s, "walkers", pairs)
    odd_s = lax.ppermute(odd_s, "walkers", odds)

    current, logs, info, pair_i, odd_i = call(
        update_kernel,
        (
            shape(walkers, 2, orbs, nel),
            shape(8, nel),
            shape(INFO, wide),
            shape(tall, LANES),
            shape(tall, LANES),
        ),
        [VMEM] * 5 + [SMEM, SMEM, VMEM],
        flops=10**6,
        name="update",
    )(total, got, inverse, move_order, accepted, counts, log_amp, change)

    pair_i = lax.ppermute(pair_i, "walkers", pairs)
    odd_i = lax.ppermute(odd_i, "walkers", odds)

    inv_new, sla_new, pos_new, log_new, energy_new, mean = call(
        place_kernel,
        (
            shape(walkers, 2, orbs, nel),
            shape(walkers, 2, orbs, nel),
            shape(walkers, 3, both),
            shape(1, walkers),
            shape(1, walkers),
            shape(1, 1),
        ),
        [SMEM] + [VMEM] * 10,
        flops=10**5,
        name="place",
    )(counts, current, done, now, energy, logs, info, pair_s, odd_s, pair_i, odd_i)
    return (
        inv_new,
        sla_new,
        pos_new,
        log_new.reshape(walkers),
        energy_new.reshape(walkers),
        mean.reshape(()),
    )


def solution(mesh):
    return jax.shard_map(
        body,
        mesh=mesh,
        in_specs=(
            P("walkers", None, "orb", None),
            P("walkers", None, "orb", None),
            P("walkers", None, None),
            P("walkers", None, None),
            P("walkers", None, None),
            P("walkers", None, None),
            P("walkers"),
            P("walkers"),
            P(),
            P(),
            P(None, "orb", None),
            P(),
        ),
        out_specs=(
            P("walkers", None, "orb", None),
            P("walkers", None, "orb", None),
            P("walkers", None, None),
            P("walkers"),
            P("walkers"),
            P(),
        ),
        check_vma=False,
    )
```

```python
import jax
import jax.numpy as jnp
from jax import lax
from jax.experimental import pallas as pl
from jax.experimental.pallas import tpu as pltpu
from jax.sharding import PartitionSpec as P

F32 = jnp.float32
highest = lax.Precision.HIGHEST
VMEM = pl.BlockSpec(memory_space=pltpu.VMEM)
SMEM = pl.BlockSpec(memory_space=pltpu.SMEM)
LANES = 128
INFO = 8


def nn(a, b):
    return lax.dot_general(
        a, b, (((1,), (0,)), ((), ())), precision=highest, preferred_element_type=F32
    )


def nt(a, b):
    return lax.dot_general(
        a, b, (((1,), (1,)), ((), ())), precision=highest, preferred_element_type=F32
    )


def tn(a, b):
    return lax.dot_general(
        a, b, (((0,), (0,)), ((), ())), precision=highest, preferred_element_type=F32
    )


def turned(rows):
    short = -rows.shape[0] % 8
    if short:
        rows = jnp.concatenate([rows, jnp.zeros((short, rows.shape[1]), F32)], axis=0)
    return jnp.transpose(rows)


def moves_of(order_ref, flags_ref):
    walkers, _, moves = flags_ref.shape
    nel = order_ref.shape[2]
    order = turned(
        jnp.concatenate([order_ref[w] for w in range(walkers)], axis=0).astype(F32)
    )
    flags = jnp.concatenate([flags_ref[w] for w in range(walkers)], axis=0).astype(F32)
    flags = turned(
        jnp.concatenate([flags, jnp.zeros((2 * walkers, nel - moves), F32)], axis=1)
    )
    cols = [order[:moves, i : i + 1] for i in range(2 * walkers)]
    keep = [flags[:moves, i : i + 1] for i in range(2 * walkers)]
    return cols, keep


def one_hots(cols, nel):
    moves = cols[0].shape[0]
    lanes = lax.broadcasted_iota(jnp.int32, (moves, nel), 1).astype(F32)
    return [(c == lanes).astype(F32) for c in cols]


def pick(counts_ref, index):
    walkers = counts_ref.shape[0]
    total = jnp.int32(0)
    source = jnp.int32(0)
    for w in range(walkers):
        total = total + counts_ref[w]
        source = source + (total <= index).astype(jnp.int32)
    return jnp.minimum(source, walkers - 1)


def total_of(counts_ref):
    total = jnp.int32(0)
    for w in range(counts_ref.shape[0]):
        total = total + counts_ref[w]
    return total


def blocks_of(nel):
    return ((0, 0, 1.0), (nel, nel, 1.0), (0, nel, 2.0))


def squares_of(cols, rows, a, b, nel):
    total = None
    for c in range(3):
        offset = cols[c][a : a + nel] - rows[c][:, b : b + nel]
        total = offset * offset if total is None else total + offset * offset
    return total


def in_rows(rows):
    return [r[:, at : at + LANES] for at in range(0, rows[0].shape[1], LANES) for r in rows]


def energy_kernel(
    pos_ref, dis_ref, order_ref, flags_ref, counts_ref, spots_ref, info_ref,
):
    _, walkers, both = pos_ref.shape
    nel = both // 2
    cols, keep = moves_of(order_ref, flags_ref)
    hots = one_hots(cols, nel)
    applied = jnp.concatenate(
        [
            jnp.concatenate(
                [
                    jnp.sum(hots[2 * w + s] * keep[2 * w + s], axis=0, keepdims=True)
                    for s in (0, 1)
                ],
                axis=1,
            )
            for w in range(walkers)
        ],
        axis=0,
    )
    now = [pos_ref[c] + dis_ref[c] * applied for c in range(3)]
    turn = turned(jnp.concatenate(now, axis=0))
    weighted = jnp.zeros((1, 1), F32)
    for w in range(walkers):
        ncols = [turn[:, c * walkers + w : c * walkers + w + 1] for c in range(3)]
        nrows = [now[c][w : w + 1] for c in range(3)]
        soft = jnp.zeros((8, nel), F32)
        for a, b, weight in blocks_of(nel):
            squares = squares_of(ncols, nrows, a, b, nel)
            terms = lax.rsqrt(squares + 1.0)
            part = jnp.sum(terms.reshape(nel // 8, 8, nel), axis=0)
            soft = soft + (part if weight == 1.0 else part * weight)
        whole = jnp.sum(jnp.sum(soft, axis=0, keepdims=True), axis=1, keepdims=True)
        energy = (whole - 1.0 * both) / (1.0 * both * (both - 1))
        wide = [jnp.broadcast_to(energy, (1, LANES)), jnp.zeros((7 - 3 * (both // LANES), LANES), F32)]
        spots_ref[w, :8] = jnp.concatenate(in_rows(nrows) + wide[: 1 + (3 * (both // LANES) < 7)], axis=0)
        spots_ref[w, 8 : 8 + 3 * (both // LANES)] = jnp.concatenate(
            in_rows([pos_ref[c, w : w + 1] for c in range(3)]), axis=0
        )
        weighted = weighted + energy * counts_ref[w].astype(F32)
    me = lax.axis_index("walkers")
    lanes = lax.broadcasted_iota(jnp.int32, info_ref.shape, 1)
    rows = lax.broadcasted_iota(jnp.int32, info_ref.shape, 0)
    number = total_of(counts_ref).astype(F32)
    info_ref[...] = jnp.where(
        lanes == me,
        jnp.where(rows == 0, number, jnp.where(rows == 1, weighted, 0.0)),
        0.0,
    )


def jastrow_kernel(spots_ref, jas_ref, out_ref):
    walkers = spots_ref.shape[0]
    nel = LANES
    parts = max(lax.axis_size("orb") // 2, 1)
    share = walkers // parts
    first = lax.div(lax.axis_index("orb"), lax.axis_size("orb") // parts) * share
    out_ref[...] = jnp.zeros(out_ref.shape, F32)
    for w in range(share):
        rows = spots_ref[first + w]
        turn = turned(rows)
        new, old = (
            [
                [rows[base + 3 * h + c : base + 3 * h + c + 1] for c in range(3)]
                for h in (0, 1)
            ]
            for base in (0, 8)
        )
        newt, oldt = (
            [
                [turn[:, base + 3 * h + c : base + 3 * h + c + 1] for c in range(3)]
                for h in (0, 1)
            ]
            for base in (0, 8)
        )
        total = jnp.zeros((8, nel), F32)
        for a, b, weight in blocks_of(nel):
            kind = 0 if a == b else 1
            fall = jas_ref[2 + kind]
            osq = squares_of(oldt[a // nel], old[b // nel], 0, 0, nel)
            nsq = squares_of(newt[a // nel], new[b // nel], 0, 0, nel)
            od = jnp.sqrt(osq)
            nd = jnp.sqrt(nsq)
            terms = (nd - od) / ((1.0 + fall * nd) * (1.0 + fall * od))
            part = jnp.sum(terms.reshape(nel // 8, 8, nel), axis=0)
            total = total + part * (jas_ref[kind] * weight)
        whole = jnp.sum(jnp.sum(total, axis=0, keepdims=True), axis=1, keepdims=True)
        out_ref[pl.ds(2 + first + w, 1), :] = jnp.broadcast_to(
            0.5 * whole, (1, out_ref.shape[1])
        )


def shift_kernel(pos_ref, dis_ref, order_ref, flags_ref, cen_ref, exp_ref, orb_ref, shift_ref, differ_ref):
    _, walkers, both = pos_ref.shape
    nel = both // 2
    moves = flags_ref.shape[2]
    basis = cen_ref.shape[1]
    cols, _ = moves_of(order_ref, flags_ref)
    hots = one_hots(cols, nel)
    rows = [ref[c] for ref in (pos_ref, dis_ref) for c in range(3)]
    rows = jnp.concatenate(rows + [jnp.zeros((-6 * walkers % 8, both), F32)] * (6 * walkers % 8 > 0), axis=0)
    for s in (0, 1):
        points = nt(
            jnp.concatenate([hots[2 * w + s] for w in range(walkers)], axis=0),
            rows[:, s * nel : (s + 1) * nel],
        )
        for w in range(walkers):
            mine = points[w * moves : (w + 1) * moves]
            old = []
            new = []
            for c in range(3):
                at = c * walkers + w
                to = (3 + c) * walkers + w
                spot = mine[:, at : at + 1]
                old.append(jnp.broadcast_to(spot, (moves, LANES)))
                new.append(jnp.broadcast_to(spot + mine[:, to : to + 1], (moves, LANES)))
            for j in range(0, basis, LANES):
                osq = None
                nsq = None
                for c in range(3):
                    row = cen_ref[c : c + 1, j : j + LANES]
                    do = old[c] - row
                    dn = new[c] - row
                    osq = do * do if osq is None else osq + do * do
                    nsq = dn * dn if nsq is None else nsq + dn * dn
                rate = -exp_ref[:, j : j + LANES]
                differ_ref[s, w * moves : (w + 1) * moves, j : j + LANES] = jnp.exp(
                    rate * nsq
                ) - jnp.exp(rate * osq)
    for s in (0, 1):
        shift_ref[s] = nt(differ_ref[s], orb_ref[s])


def partial_kernel(
    shift_ref, order_ref, flags_ref, counts_ref, inv_ref, sla_ref, spots_ref, info_ref,
    part_ref, done_ref, pair_ref, odd_ref,
):
    walkers, _, orbs, nel = inv_ref.shape
    moves = flags_ref.shape[2]
    cols, keep = moves_of(order_ref, flags_ref)
    hots = one_hots(cols, nel)
    part_ref[2 * walkers * moves :, :] = info_ref[...]
    for s in (0, 1):
        for w in range(walkers):
            i = 2 * w + s
            mine = shift_ref[s, w * moves : (w + 1) * moves, :]
            proposed = mine + nt(hots[i], sla_ref[w, s])
            part = nn(proposed, inv_ref[w, s])
            part_ref[i * moves : (i + 1) * moves, :] = part * keep[i]
            done_ref[w, s] = sla_ref[w, s] + tn(mine, hots[i] * keep[i])
    half = walkers // 2
    per = 2 * orbs
    tail = half * per
    parity = lax.rem(lax.axis_index("walkers"), 2)
    number = total_of(counts_ref)
    for pay, goes_up in ((pair_ref, parity == 0), (odd_ref, parity == 1)):
        for j in range(half):
            index = jnp.where(goes_up, number - half + j, j)
            source = pick(counts_ref, index)
            for s in (0, 1):
                pay[j * per + s * orbs : j * per + (s + 1) * orbs, :] = done_ref[source, s]
            pay[tail + 8 * j : tail + 8 * j + 8, :] = spots_ref[source, :8]


def add_kernel(mine_ref, other_ref, change_ref, out_ref):
    rows = mine_ref.shape[0] - change_ref.shape[0]
    out_ref[:rows, :] = mine_ref[:rows, :] + other_ref[:rows, :]
    out_ref[rows:, :] = mine_ref[rows:, :] + other_ref[rows:, :] + change_ref[...]


def update_kernel(
    sum_ref, got_ref, inv_ref, order_ref, flags_ref, counts_ref, amp_ref,
    cur_ref, log_ref, info_ref, pair_ref, odd_ref,
):
    walkers, _, orbs, nel = inv_ref.shape
    moves = flags_ref.shape[2]
    count = 2 * walkers
    cols, keep = moves_of(order_ref, flags_ref)
    hots = one_hots(cols, nel)
    eye = (
        lax.broadcasted_iota(jnp.int32, (moves, moves), 0)
        == lax.broadcasted_iota(jnp.int32, (moves, moves), 1)
    ).astype(F32)
    tiles = moves // 8
    left = []
    right = []
    columns = []
    for i in range(count):
        at = slice(i * moves, (i + 1) * moves)
        change = sum_ref[at, :] + got_ref[at, :] - hots[i] * keep[i]
        coupling = nt(change, hots[i]) + eye
        columns.append(nt(inv_ref[i // 2, i % 2], hots[i]))
        left.append([coupling[8 * t : 8 * t + 8] for t in range(tiles)])
        right.append([change[8 * t : 8 * t + 8] for t in range(tiles)])
    info_ref[...] = sum_ref[count * moves :, :] + got_ref[count * moves :, :]
    lanes = lax.broadcasted_iota(jnp.int32, (1, nel), 1)
    sub = lax.broadcasted_iota(jnp.int32, (8, nel), 0)
    pivots = [jnp.ones((1, nel), F32) for _ in range(count)]
    for k in range(moves):
        own, line = k // 8, k % 8
        for i in range(count):
            wide = [
                jnp.broadcast_to(left[i][t][:, k : k + 1], (8, nel)) for t in range(tiles)
            ]
            pivot = wide[own][line : line + 1]
            pivots[i] = jnp.where(lanes == k, pivot, pivots[i])
            scale = 1.0 / pivot
            lrow = left[i][own][line : line + 1] * scale[:, :moves]
            rrow = right[i][own][line : line + 1] * scale
            for t in range(tiles):
                nl = left[i][t] - wide[t][:, :moves] * lrow
                nr = right[i][t] - wide[t] * rrow
                if t == own:
                    nl = jnp.where(sub[:, :moves] == line, lrow, nl)
                    nr = jnp.where(sub == line, rrow, nr)
                left[i][t] = nl
                right[i][t] = nr
    for i in range(count):
        solved = jnp.concatenate(right[i], axis=0)
        cur_ref[i // 2, i % 2] = inv_ref[i // 2, i % 2] - nn(columns[i], solved)
    log_ref[...] = jnp.zeros(log_ref.shape, F32)
    for w in range(walkers):
        both = jnp.log(jnp.abs(pivots[2 * w])) + jnp.log(jnp.abs(pivots[2 * w + 1]))
        log_ref[w : w + 1, :] = (
            jnp.broadcast_to(jnp.sum(both, axis=1, keepdims=True), (1, nel))
            + info_ref[2 + w : 3 + w, :nel]
            + amp_ref[w]
        )
    half = walkers // 2
    per = 2 * orbs
    tail = half * per
    parity = lax.rem(lax.axis_index("walkers"), 2)
    number = total_of(counts_ref)
    for pay, goes_up in ((pair_ref, parity == 0), (odd_ref, parity == 1)):
        pay[tail : tail + INFO, :] = info_ref[...]
        pay[tail + INFO :, :] = jnp.zeros((pay.shape[0] - tail - INFO, LANES), F32)
        for j in range(half):
            index = jnp.where(goes_up, number - half + j, j)
            source = pick(counts_ref, index)
            for s in (0, 1):
                pay[j * per + s * orbs : j * per + (s + 1) * orbs, :] = cur_ref[source, s]
            at = tail + INFO + j
            pay[at : at + 1, :] = log_ref[pl.ds(source, 1), :]


def place_kernel(
    counts_ref, cur_ref, done_ref, spots_ref, log_ref, info_ref,
    pair_s_ref, odd_s_ref, pair_i_ref, odd_i_ref,
    inv_out, sla_out, pos_out, log_out, energy_out, mean_out,
):
    walkers, _, orbs, nel = cur_ref.shape
    width = pos_out.shape[2] // LANES
    half = walkers // 2
    per = 2 * orbs
    tail = half * per
    me = lax.axis_index("walkers")
    parity = lax.rem(me, 2)
    info = info_ref[...] + pair_i_ref[tail : tail + INFO, :]
    lanes = lax.broadcasted_iota(jnp.int32, (1, info.shape[1]), 1)
    before = jnp.sum(jnp.where(lanes < me, info[0:1], 0.0)).astype(jnp.int32)
    groups = lax.axis_size("walkers")
    mean = jnp.sum(info[1:2], axis=1, keepdims=True)
    mean_out[...] = mean / (1.0 * walkers * groups)
    number = total_of(counts_ref)
    slots = lax.broadcasted_iota(jnp.int32, (1, walkers), 1)

    def put(j, inverse, slater, spot, log):
        for s in (0, 1):
            inv_out[j, s] = inverse(s)
            sla_out[j, s] = slater(s)
        for c in range(3):
            for h in range(width):
                pos_out[c, j : j + 1, h * LANES : (h + 1) * LANES] = spot[3 * h + c : 3 * h + c + 1]
        log_out[...] = jnp.where(slots == j, log[:, :walkers], log_out[...])
        energy_out[...] = jnp.where(
            slots == j, spot[3 * width : 3 * width + 1, :walkers], energy_out[...]
        )

    log_out[...] = jnp.zeros(log_out.shape, F32)
    energy_out[...] = jnp.zeros(energy_out.shape, F32)
    for j in range(walkers):
        index = me * walkers + j - before
        low = index < 0
        high = index >= number

        @pl.when(jnp.logical_not(low | high))
        def _():
            w = pick(counts_ref, index)
            put(
                j,
                lambda s: cur_ref[w, s],
                lambda s: done_ref[w, s],
                spots_ref[w, :8],
                log_ref[pl.ds(w, 1), :],
            )

        def received(late, early):
            i = jnp.clip(jnp.where(low, index + half, index - number), 0, half - 1)
            put(
                j,
                lambda s: late[pl.ds(pl.multiple_of(i * per + s * orbs, 8), orbs), :],
                lambda s: early[pl.ds(pl.multiple_of(i * per + s * orbs, 8), orbs), :],
                early[pl.ds(pl.multiple_of(tail + i * 8, 8), 8), :],
                late[pl.ds(tail + INFO + i, 1), :],
            )

        on_pair = (low & (parity == 1)) | (high & (parity == 0))

        @pl.when(on_pair)
        def _():
            received(pair_i_ref, pair_s_ref)

        @pl.when((low | high) & jnp.logical_not(on_pair))
        def _():
            received(odd_i_ref, odd_s_ref)


def call(kernel, outs, in_specs, scratch=(), us=1.0, name=None):
    return pl.pallas_call(
        kernel,
        out_shape=outs,
        in_specs=in_specs,
        out_specs=jax.tree.map(lambda _: VMEM, outs),
        scratch_shapes=list(scratch),
        compiler_params=pltpu.CompilerParams(vmem_limit_bytes=32 * 2**20),
        cost_estimate=pl.CostEstimate(flops=int(us * 1.1e9), bytes_accessed=2**18, transcendentals=0),
        name=name,
    )


def shape(*dims):
    return jax.ShapeDtypeStruct(dims, F32)


def body(
    inverse, slater, positions, displacements, move_order, accepted, counts, log_amp, centers,
    exponents, orbitals, jastrow,
):
    walkers, _, orbs, nel = inverse.shape
    moves = accepted.shape[2]
    both = positions.shape[2]
    basis = centers.shape[1]
    groups = lax.axis_size("walkers")
    members = lax.axis_size("orb")
    wide = max(LANES, groups)
    half = walkers // 2
    per = 2 * orbs
    count = 2 * walkers
    tall = half * per + 16

    pairs = [(i, i ^ 1) for i in range(groups)]
    odds = [(i, i + 1) for i in range(1, groups - 1, 2)]
    odds = odds + [(b, a) for a, b in odds]

    places = positions.transpose(1, 0, 2)
    steps = displacements.transpose(1, 0, 2)
    spots, info = call(
        energy_kernel,
        (
            shape(walkers, 16, LANES),
            shape(INFO, wide),
        ),
        [VMEM, VMEM, VMEM, VMEM, SMEM],
        us=2,
        name="energy",
    )(places, steps, move_order, accepted, counts)

    hops = members * 2
    step = hops
    while step < groups:
        info = info + lax.ppermute(info, "walkers", [(i, i ^ step) for i in range(groups)])
        step *= 2
    joint = [
        (d * members + o, (d ^ (2 * o)) * members + o)
        for d in range(groups)
        for o in range(members)
        if 2 * o < groups
    ]
    info = lax.ppermute(info, ("walkers", "orb"), joint)

    shift = call(
        shift_kernel,
        shape(2, walkers * moves, orbs),
        [VMEM] * 7,
        scratch=[pltpu.VMEM((2, walkers * moves, basis), F32)],
        us=3,
        name="shift",
    )(places, steps, move_order, accepted, centers, exponents.reshape(1, basis), orbitals)

    part, done, pair_s, odd_s = call(
        partial_kernel,
        (
            shape(count * moves + INFO, nel),
            shape(walkers, 2, orbs, nel),
            shape(tall, LANES),
            shape(tall, LANES),
        ),
        [VMEM, VMEM, VMEM, SMEM] + [VMEM] * 4,
        us=2,
        name="partial",
    )(shift, move_order, accepted, counts, inverse, slater, spots, info)

    change = call(
        jastrow_kernel, shape(INFO, wide), [VMEM, SMEM], us=1.2, name="jastrow"
    )(spots, jastrow)

    total = part
    got = jnp.zeros_like(part)
    step = 1
    while step < members:
        partner = [(o, o ^ step) for o in range(members)]
        got = lax.ppermute(total, "orb", partner)
        if 2 * step < members:
            total = call(
                add_kernel,
                shape(count * moves + INFO, nel),
                [VMEM] * 3,
                us=0.7,
                name="add",
            )(total, got, change if step == 1 else jnp.zeros_like(change))
        step *= 2

    pair_s = lax.ppermute(pair_s, "walkers", pairs)
    odd_s = lax.ppermute(odd_s, "walkers", odds)

    current, logs, info, pair_i, odd_i = call(
        update_kernel,
        (
            shape(walkers, 2, orbs, nel),
            shape(8, nel),
            shape(INFO, wide),
            shape(tall, LANES),
            shape(tall, LANES),
        ),
        [VMEM] * 5 + [SMEM, SMEM],
        us=4,
        name="update",
    )(total, got, inverse, move_order, accepted, counts, log_amp)

    pair_i = lax.ppermute(pair_i, "walkers", pairs)
    odd_i = lax.ppermute(odd_i, "walkers", odds)

    inv_new, sla_new, pos_new, log_new, energy_new, mean = call(
        place_kernel,
        (
            shape(walkers, 2, orbs, nel),
            shape(walkers, 2, orbs, nel),
            shape(3, walkers, both),
            shape(1, walkers),
            shape(1, walkers),
            shape(1, 1),
        ),
        [SMEM] + [VMEM] * 9,
        us=1.5,
        name="place",
    )(counts, current, done, spots, logs, info, pair_s, odd_s, pair_i, odd_i)
    return (
        inv_new,
        sla_new,
        pos_new.transpose(1, 0, 2),
        log_new.reshape(walkers),
        energy_new.reshape(walkers),
        mean.reshape(()),
    )


def solution(mesh):
    return jax.shard_map(
        body,
        mesh=mesh,
        in_specs=(
            P("walkers", None, "orb", None),
            P("walkers", None, "orb", None),
            P("walkers", None, None),
            P("walkers", None, None),
            P("walkers", None, None),
            P("walkers", None, None),
            P("walkers"),
            P("walkers"),
            P(),
            P(),
            P(None, "orb", None),
            P(),
        ),
        out_specs=(
            P("walkers", None, "orb", None),
            P("walkers", None, "orb", None),
            P("walkers", None, None),
            P("walkers"),
            P("walkers"),
            P(),
        ),
        check_vma=False,
    )
```

```python
import jax
import jax.numpy as jnp
from jax import lax
from jax.experimental import pallas as pl
from jax.experimental.pallas import tpu as pltpu
from jax.sharding import PartitionSpec as P

F32 = jnp.float32
BF16 = jnp.bfloat16
highest = lax.Precision.HIGHEST
VMEM = pl.BlockSpec(memory_space=pltpu.VMEM)
SMEM = pl.BlockSpec(memory_space=pltpu.SMEM)
LANES = 128
INFO = 8


def nn(a, b):
    return lax.dot_general(
        a, b, (((1,), (0,)), ((), ())), precision=highest, preferred_element_type=F32
    )


def nt(a, b):
    return lax.dot_general(
        a, b, (((1,), (1,)), ((), ())), precision=highest, preferred_element_type=F32
    )


def tn(a, b):
    return lax.dot_general(
        a, b, (((0,), (0,)), ((), ())), precision=highest, preferred_element_type=F32
    )


def thirds(x):
    high = x.astype(BF16)
    rest = x - high.astype(F32)
    middle = rest.astype(BF16)
    low = (rest - middle.astype(F32)).astype(BF16)
    return jnp.concatenate([high, middle, low], axis=0)


def taken(x, hot):
    rows = x.shape[0]
    parts = lax.dot_general(
        thirds(x), hot.astype(BF16), (((1,), (1,)), ((), ())), preferred_element_type=F32
    )
    return parts[:rows] + parts[rows : 2 * rows] + parts[2 * rows :]


def turned(rows):
    short = -rows.shape[0] % 8
    if short:
        rows = jnp.concatenate([rows, jnp.zeros((short, rows.shape[1]), F32)], axis=0)
    return jnp.transpose(rows)


def moves_of(order_ref, flags_ref):
    walkers, _, moves = flags_ref.shape
    nel = order_ref.shape[2]
    order = turned(
        jnp.concatenate([order_ref[w] for w in range(walkers)], axis=0).astype(F32)
    )
    flags = jnp.concatenate([flags_ref[w] for w in range(walkers)], axis=0).astype(F32)
    flags = turned(
        jnp.concatenate([flags, jnp.zeros((2 * walkers, nel - moves), F32)], axis=1)
    )
    cols = [order[:moves, i : i + 1] for i in range(2 * walkers)]
    keep = [flags[:moves, i : i + 1] for i in range(2 * walkers)]
    return cols, keep


def one_hots(cols, nel):
    moves = cols[0].shape[0]
    lanes = lax.broadcasted_iota(jnp.int32, (moves, nel), 1).astype(F32)
    return [(c == lanes).astype(F32) for c in cols]


def pick(counts_ref, index):
    walkers = counts_ref.shape[0]
    total = jnp.int32(0)
    source = jnp.int32(0)
    for w in range(walkers):
        total = total + counts_ref[w]
        source = source + (total <= index).astype(jnp.int32)
    return jnp.minimum(source, walkers - 1)


def total_of(counts_ref):
    total = jnp.int32(0)
    for w in range(counts_ref.shape[0]):
        total = total + counts_ref[w]
    return total


def pair_tiles(turns, rows, nel, kinds):
    sums = [None, None]
    for h in (0, 1):
        for t in range(nel // 8):
            wide = [
                [
                    jnp.broadcast_to(turn[h][c][8 * t : 8 * t + 8], (8, nel))
                    for c in range(3)
                ]
                for turn in turns
            ]
            for g in range(h, 2):
                squares = []
                for i, row in enumerate(rows):
                    total = None
                    for c in range(3):
                        offset = wide[i][c] - row[g][c]
                        total = offset * offset if total is None else total + offset * offset
                    squares.append(total)
                kind = int(g != h)
                term = kinds[kind](*squares)
                sums[kind] = term if sums[kind] is None else sums[kind] + term
    return sums


def summed(tile):
    return jnp.sum(jnp.sum(tile, axis=0, keepdims=True), axis=1, keepdims=True)


def jastrow_of(spots, turn, jas_ref, nel):
    rows, turns = (
        [
            [
                [cut(base + 3 * h + c) for c in range(3)]
                for h in (0, 1)
            ]
            for base in (0, 8)
        ]
        for cut in (lambda r: spots[r : r + 1], lambda r: turn[:, r : r + 1])
    )

    def change(fall):
        def term(new, old):
            nd = jnp.sqrt(new)
            od = jnp.sqrt(old)
            return (nd - od) / ((1.0 + fall * nd) * (1.0 + fall * od))

        return term

    same, other = pair_tiles(turns, rows, nel, [change(jas_ref[2]), change(jas_ref[3])])
    return summed(same * (0.5 * jas_ref[0]) + other * jas_ref[1])


def in_rows(rows):
    return [r[:, at : at + LANES] for at in range(0, rows[0].shape[1], LANES) for r in rows]


def energy_kernel(
    pos_ref, dis_ref, order_ref, flags_ref, counts_ref, spots_ref, info_ref,
):
    _, walkers, both = pos_ref.shape
    nel = both // 2
    cols, keep = moves_of(order_ref, flags_ref)
    hots = one_hots(cols, nel)
    applied = jnp.concatenate(
        [
            jnp.concatenate(
                [
                    jnp.sum(hots[2 * w + s] * keep[2 * w + s], axis=0, keepdims=True)
                    for s in (0, 1)
                ],
                axis=1,
            )
            for w in range(walkers)
        ],
        axis=0,
    )
    now = [pos_ref[c] + dis_ref[c] * applied for c in range(3)]
    turn = turned(jnp.concatenate(now, axis=0))
    weighted = jnp.zeros((1, 1), F32)
    for w in range(walkers):
        nrows = [now[c][w : w + 1] for c in range(3)]
        halves = [[r[:, h * nel : (h + 1) * nel] for r in nrows] for h in (0, 1)]
        tall = [
            [
                turn[h * nel : (h + 1) * nel, c * walkers + w : c * walkers + w + 1]
                for c in range(3)
            ]
            for h in (0, 1)
        ]
        same, other = pair_tiles([tall], [halves], nel, [lambda q: lax.rsqrt(q + 1.0)] * 2)
        whole = summed(same + 2.0 * other)
        energy = (whole - 1.0 * both) / (1.0 * both * (both - 1))
        wide = [jnp.broadcast_to(energy, (1, LANES)), jnp.zeros((7 - 3 * (both // LANES), LANES), F32)]
        spots_ref[w, :8] = jnp.concatenate(in_rows(nrows) + wide[: 1 + (3 * (both // LANES) < 7)], axis=0)
        spots_ref[w, 8 : 8 + 3 * (both // LANES)] = jnp.concatenate(
            in_rows([pos_ref[c, w : w + 1] for c in range(3)]), axis=0
        )
        weighted = weighted + energy * counts_ref[w].astype(F32)
    me = lax.axis_index("walkers")
    lanes = lax.broadcasted_iota(jnp.int32, info_ref.shape, 1)
    rows = lax.broadcasted_iota(jnp.int32, info_ref.shape, 0)
    number = total_of(counts_ref).astype(F32)
    info_ref[...] = jnp.where(
        lanes == me,
        jnp.where(rows == 0, number, jnp.where(rows == 1, weighted, 0.0)),
        0.0,
    )


def shift_kernel(pos_ref, dis_ref, order_ref, flags_ref, cen_ref, exp_ref, orb_ref, shift_ref, differ_ref):
    _, walkers, both = pos_ref.shape
    nel = both // 2
    moves = flags_ref.shape[2]
    basis = cen_ref.shape[1]
    cols, _ = moves_of(order_ref, flags_ref)
    hots = one_hots(cols, nel)
    rows = [ref[c] for ref in (pos_ref, dis_ref) for c in range(3)]
    rows = jnp.concatenate(rows + [jnp.zeros((-6 * walkers % 8, both), F32)] * (6 * walkers % 8 > 0), axis=0)
    for s in (0, 1):
        points = nt(
            jnp.concatenate([hots[2 * w + s] for w in range(walkers)], axis=0),
            rows[:, s * nel : (s + 1) * nel],
        )
        for w in range(walkers):
            mine = points[w * moves : (w + 1) * moves]
            old = []
            new = []
            for c in range(3):
                at = c * walkers + w
                to = (3 + c) * walkers + w
                spot = mine[:, at : at + 1]
                old.append(jnp.broadcast_to(spot, (moves, LANES)))
                new.append(jnp.broadcast_to(spot + mine[:, to : to + 1], (moves, LANES)))
            for j in range(0, basis, LANES):
                osq = None
                nsq = None
                for c in range(3):
                    row = cen_ref[c : c + 1, j : j + LANES]
                    do = old[c] - row
                    dn = new[c] - row
                    osq = do * do if osq is None else osq + do * do
                    nsq = dn * dn if nsq is None else nsq + dn * dn
                rate = -exp_ref[:, j : j + LANES]
                differ_ref[s, w * moves : (w + 1) * moves, j : j + LANES] = jnp.exp(
                    rate * nsq
                ) - jnp.exp(rate * osq)
    for s in (0, 1):
        shift_ref[s] = nt(differ_ref[s], orb_ref[s])


def partial_kernel(
    shift_ref, order_ref, flags_ref, counts_ref, inv_ref, sla_ref, spots_ref, info_ref, jas_ref,
    part_ref, done_ref, pair_ref, odd_ref,
):
    walkers, _, orbs, nel = inv_ref.shape
    moves = flags_ref.shape[2]
    cols, keep = moves_of(order_ref, flags_ref)
    hots = one_hots(cols, nel)
    members = lax.axis_size("orb")
    share = walkers // members
    first = lax.axis_index("orb") * share
    tail = 2 * walkers * moves
    part_ref[tail:, :] = info_ref[...]
    for w in range(share):
        mine = spots_ref[first + w]
        at = tail + 2 + first + w
        part_ref[pl.ds(at, 1), :] = jnp.broadcast_to(
            jastrow_of(mine, turned(mine), jas_ref, nel), (1, part_ref.shape[1])
        )
    for s in (0, 1):
        for w in range(walkers):
            i = 2 * w + s
            mine = shift_ref[s, w * moves : (w + 1) * moves, :]
            proposed = mine + nt(hots[i], sla_ref[w, s])
            part = nn(proposed, inv_ref[w, s])
            part_ref[i * moves : (i + 1) * moves, :] = part * keep[i]
            done_ref[w, s] = sla_ref[w, s] + tn(mine, hots[i] * keep[i])
    half = walkers // 2
    per = 2 * orbs
    tail = half * per
    parity = lax.rem(lax.axis_index("walkers"), 2)
    number = total_of(counts_ref)
    for pay, goes_up in ((pair_ref, parity == 0), (odd_ref, parity == 1)):
        for j in range(half):
            index = jnp.where(goes_up, number - half + j, j)
            source = pick(counts_ref, index)
            for s in (0, 1):
                pay[j * per + s * orbs : j * per + (s + 1) * orbs, :] = done_ref[source, s]
            pay[tail + 8 * j : tail + 8 * j + 8, :] = spots_ref[source, :8]


def add_kernel(mine_ref, other_ref, out_ref):
    out_ref[...] = mine_ref[...] + other_ref[...]


def update_kernel(
    sum_ref, got_ref, inv_ref, order_ref, flags_ref, counts_ref, amp_ref,
    cur_ref, log_ref, info_ref, pair_ref, odd_ref,
):
    walkers, _, orbs, nel = inv_ref.shape
    moves = flags_ref.shape[2]
    count = 2 * walkers
    cols, keep = moves_of(order_ref, flags_ref)
    hots = one_hots(cols, nel)
    eye = (
        lax.broadcasted_iota(jnp.int32, (moves, moves), 0)
        == lax.broadcasted_iota(jnp.int32, (moves, moves), 1)
    ).astype(F32)
    tiles = moves // 8
    left = []
    right = []
    columns = []
    for i in range(count):
        at = slice(i * moves, (i + 1) * moves)
        change = sum_ref[at, :] + got_ref[at, :] - hots[i] * keep[i]
        coupling = taken(change, hots[i]) + eye
        columns.append(taken(inv_ref[i // 2, i % 2], hots[i]))
        left.append([coupling[8 * t : 8 * t + 8] for t in range(tiles)])
        right.append([change[8 * t : 8 * t + 8] for t in range(tiles)])
    info_ref[...] = sum_ref[count * moves :, :] + got_ref[count * moves :, :]
    lanes = lax.broadcasted_iota(jnp.int32, (1, nel), 1)
    sub = lax.broadcasted_iota(jnp.int32, (8, nel), 0)
    pivots = [jnp.ones((1, nel), F32) for _ in range(count)]
    for k in range(moves):
        own, line = k // 8, k % 8
        for i in range(count):
            wide = [
                jnp.broadcast_to(left[i][t][:, k : k + 1], (8, nel)) for t in range(tiles)
            ]
            pivot = wide[own][line : line + 1]
            pivots[i] = jnp.where(lanes == k, pivot, pivots[i])
            scale = 1.0 / pivot
            lrow = left[i][own][line : line + 1] * scale[:, :moves]
            rrow = right[i][own][line : line + 1] * scale
            for t in range(tiles):
                nl = left[i][t] - wide[t][:, :moves] * lrow
                nr = right[i][t] - wide[t] * rrow
                if t == own:
                    nl = jnp.where(sub[:, :moves] == line, lrow, nl)
                    nr = jnp.where(sub == line, rrow, nr)
                left[i][t] = nl
                right[i][t] = nr
    for i in range(count):
        solved = jnp.concatenate(right[i], axis=0)
        cur_ref[i // 2, i % 2] = inv_ref[i // 2, i % 2] - nn(columns[i], solved)
    log_ref[...] = jnp.zeros(log_ref.shape, F32)
    for w in range(walkers):
        both = jnp.log(jnp.abs(pivots[2 * w])) + jnp.log(jnp.abs(pivots[2 * w + 1]))
        log_ref[w : w + 1, :] = (
            jnp.broadcast_to(jnp.sum(both, axis=1, keepdims=True), (1, nel))
            + info_ref[2 + w : 3 + w, :nel]
            + amp_ref[w]
        )
    half = walkers // 2
    per = 2 * orbs
    tail = half * per
    parity = lax.rem(lax.axis_index("walkers"), 2)
    number = total_of(counts_ref)
    for pay, goes_up in ((pair_ref, parity == 0), (odd_ref, parity == 1)):
        pay[tail : tail + INFO, :] = info_ref[...]
        pay[tail + INFO :, :] = jnp.zeros((pay.shape[0] - tail - INFO, LANES), F32)
        for j in range(half):
            index = jnp.where(goes_up, number - half + j, j)
            source = pick(counts_ref, index)
            for s in (0, 1):
                pay[j * per + s * orbs : j * per + (s + 1) * orbs, :] = cur_ref[source, s]
            at = tail + INFO + j
            pay[at : at + 1, :] = log_ref[pl.ds(source, 1), :]


def place_kernel(
    counts_ref, cur_ref, done_ref, spots_ref, log_ref, info_ref,
    pair_s_ref, odd_s_ref, pair_i_ref, odd_i_ref,
    inv_out, sla_out, pos_out, log_out, energy_out, mean_out,
):
    walkers, _, orbs, nel = cur_ref.shape
    width = pos_out.shape[2] // LANES
    half = walkers // 2
    per = 2 * orbs
    tail = half * per
    me = lax.axis_index("walkers")
    parity = lax.rem(me, 2)
    info = info_ref[...] + pair_i_ref[tail : tail + INFO, :]
    lanes = lax.broadcasted_iota(jnp.int32, (1, info.shape[1]), 1)
    before = jnp.sum(jnp.where(lanes < me, info[0:1], 0.0)).astype(jnp.int32)
    groups = lax.axis_size("walkers")
    mean = jnp.sum(info[1:2], axis=1, keepdims=True)
    mean_out[...] = mean / (1.0 * walkers * groups)
    number = total_of(counts_ref)
    slots = lax.broadcasted_iota(jnp.int32, (1, walkers), 1)

    def put(j, inverse, slater, spot, log):
        for s in (0, 1):
            inv_out[j, s] = inverse(s)
            sla_out[j, s] = slater(s)
        for c in range(3):
            for h in range(width):
                pos_out[c, j : j + 1, h * LANES : (h + 1) * LANES] = spot[3 * h + c : 3 * h + c + 1]
        log_out[...] = jnp.where(slots == j, log[:, :walkers], log_out[...])
        energy_out[...] = jnp.where(
            slots == j, spot[3 * width : 3 * width + 1, :walkers], energy_out[...]
        )

    log_out[...] = jnp.zeros(log_out.shape, F32)
    energy_out[...] = jnp.zeros(energy_out.shape, F32)
    for j in range(walkers):
        index = me * walkers + j - before
        low = index < 0
        high = index >= number

        @pl.when(jnp.logical_not(low | high))
        def _():
            w = pick(counts_ref, index)
            put(
                j,
                lambda s: cur_ref[w, s],
                lambda s: done_ref[w, s],
                spots_ref[w, :8],
                log_ref[pl.ds(w, 1), :],
            )

        def received(late, early):
            i = jnp.clip(jnp.where(low, index + half, index - number), 0, half - 1)
            put(
                j,
                lambda s: late[pl.ds(pl.multiple_of(i * per + s * orbs, 8), orbs), :],
                lambda s: early[pl.ds(pl.multiple_of(i * per + s * orbs, 8), orbs), :],
                early[pl.ds(pl.multiple_of(tail + i * 8, 8), 8), :],
                late[pl.ds(tail + INFO + i, 1), :],
            )

        on_pair = (low & (parity == 1)) | (high & (parity == 0))

        @pl.when(on_pair)
        def _():
            received(pair_i_ref, pair_s_ref)

        @pl.when((low | high) & jnp.logical_not(on_pair))
        def _():
            received(odd_i_ref, odd_s_ref)


def call(kernel, outs, in_specs, scratch=(), us=1.0, name=None, vmem=32 * 2**20):
    return pl.pallas_call(
        kernel,
        out_shape=outs,
        in_specs=in_specs,
        out_specs=jax.tree.map(lambda _: VMEM, outs),
        scratch_shapes=list(scratch),
        compiler_params=pltpu.CompilerParams(vmem_limit_bytes=vmem),
        cost_estimate=pl.CostEstimate(flops=int(us * 1.1e9), bytes_accessed=2**18, transcendentals=0),
        name=name,
    )


def shape(*dims):
    return jax.ShapeDtypeStruct(dims, F32)


def body(
    inverse, slater, positions, displacements, move_order, accepted, counts, log_amp, centers,
    exponents, orbitals, jastrow,
):
    walkers, _, orbs, nel = inverse.shape
    moves = accepted.shape[2]
    both = positions.shape[2]
    basis = centers.shape[1]
    groups = lax.axis_size("walkers")
    members = lax.axis_size("orb")
    wide = max(LANES, groups)
    half = walkers // 2
    per = 2 * orbs
    count = 2 * walkers
    tall = half * per + 16

    pairs = [(i, i ^ 1) for i in range(groups)]
    odds = [(i, i + 1) for i in range(1, groups - 1, 2)]
    odds = odds + [(b, a) for a, b in odds]

    places = positions.transpose(1, 0, 2)
    steps = displacements.transpose(1, 0, 2)
    spots, info = call(
        energy_kernel,
        (
            shape(walkers, 16, LANES),
            shape(INFO, wide),
        ),
        [VMEM, VMEM, VMEM, VMEM, SMEM],
        us=2,
        vmem=61 * 2**20,
        name="energy",
    )(places, steps, move_order, accepted, counts)

    hops = members * 2
    step = hops
    while step < groups:
        info = info + lax.ppermute(info, "walkers", [(i, i ^ step) for i in range(groups)])
        step *= 2
    joint = [
        (d * members + o, (d ^ (2 * o)) * members + o)
        for d in range(groups)
        for o in range(members)
        if 2 * o < groups
    ]
    info = lax.ppermute(info, ("walkers", "orb"), joint)

    shift = call(
        shift_kernel,
        shape(2, walkers * moves, orbs),
        [VMEM] * 7,
        scratch=[pltpu.VMEM((2, walkers * moves, basis), F32)],
        us=3,
        name="shift",
    )(places, steps, move_order, accepted, centers, exponents.reshape(1, basis), orbitals)

    part, done, pair_s, odd_s = call(
        partial_kernel,
        (
            shape(count * moves + INFO, nel),
            shape(walkers, 2, orbs, nel),
            shape(tall, LANES),
            shape(tall, LANES),
        ),
        [VMEM, VMEM, VMEM, SMEM] + [VMEM] * 4 + [SMEM],
        us=2,
        name="partial",
    )(shift, move_order, accepted, counts, inverse, slater, spots, info, jastrow)

    total = part
    got = jnp.zeros_like(part)
    step = 1
    while step < members:
        partner = [(o, o ^ step) for o in range(members)]
        got = lax.ppermute(total, "orb", partner)
        if 2 * step < members:
            total = call(
                add_kernel,
                shape(count * moves + INFO, nel),
                [VMEM] * 2,
                us=0.5,
                name="add",
            )(total, got)
        step *= 2

    pair_s = lax.ppermute(pair_s, "walkers", pairs)
    odd_s = lax.ppermute(odd_s, "walkers", odds)

    current, logs, info, pair_i, odd_i = call(
        update_kernel,
        (
            shape(walkers, 2, orbs, nel),
            shape(8, nel),
            shape(INFO, wide),
            shape(tall, LANES),
            shape(tall, LANES),
        ),
        [VMEM] * 5 + [SMEM, SMEM],
        us=4,
        name="update",
    )(total, got, inverse, move_order, accepted, counts, log_amp)

    pair_i = lax.ppermute(pair_i, "walkers", pairs)
    odd_i = lax.ppermute(odd_i, "walkers", odds)

    inv_new, sla_new, pos_new, log_new, energy_new, mean = call(
        place_kernel,
        (
            shape(walkers, 2, orbs, nel),
            shape(walkers, 2, orbs, nel),
            shape(3, walkers, both),
            shape(1, walkers),
            shape(1, walkers),
            shape(1, 1),
        ),
        [SMEM] + [VMEM] * 9,
        us=1.5,
        name="place",
    )(counts, current, done, spots, logs, info, pair_s, odd_s, pair_i, odd_i)
    return (
        inv_new,
        sla_new,
        pos_new.transpose(1, 0, 2),
        log_new.reshape(walkers),
        energy_new.reshape(walkers),
        mean.reshape(()),
    )


def solution(mesh):
    return jax.shard_map(
        body,
        mesh=mesh,
        in_specs=(
            P("walkers", None, "orb", None),
            P("walkers", None, "orb", None),
            P("walkers", None, None),
            P("walkers", None, None),
            P("walkers", None, None),
            P("walkers", None, None),
            P("walkers"),
            P("walkers"),
            P(),
            P(),
            P(None, "orb", None),
            P(),
        ),
        out_specs=(
            P("walkers", None, "orb", None),
            P("walkers", None, "orb", None),
            P("walkers", None, None),
            P("walkers"),
            P("walkers"),
            P(),
        ),
        check_vma=False,
    )
```

```python
import jax
import jax.numpy as jnp
from jax import lax
from jax.experimental import pallas as pl
from jax.experimental.pallas import tpu as pltpu
from jax.sharding import PartitionSpec as P

F32 = jnp.float32
BF16 = jnp.bfloat16
highest = lax.Precision.HIGHEST
VMEM = pl.BlockSpec(memory_space=pltpu.VMEM)
HBM = pl.BlockSpec(memory_space=pl.ANY)
SMEM = pl.BlockSpec(memory_space=pltpu.SMEM)
LANES = 128
INFO = 8


def nt(a, b):
    return lax.dot_general(
        a, b, (((1,), (1,)), ((), ())), precision=highest, preferred_element_type=F32
    )


def thirds(x):
    high = x.astype(BF16)
    rest = x - high.astype(F32)
    middle = rest.astype(BF16)
    low = (rest - middle.astype(F32)).astype(BF16)
    return jnp.concatenate([high, middle, low], axis=0)


def parted(x):
    high = x.astype(BF16)
    return jnp.concatenate([high, (x - high.astype(F32)).astype(BF16)], axis=0)


def product(a, b):
    rows = a.shape[0]
    inner = b.shape[0]
    left = parted(a)
    right = parted(b)
    whole = None
    for part in (right[:inner], right[inner:]):
        both = lax.dot_general(
            left, part, (((1,), (0,)), ((), ())), preferred_element_type=F32
        )
        both = both[:rows] + both[rows:]
        whole = both if whole is None else whole + both
    return whole


def product_nt(a, b):
    rows, cols = a.shape[0], b.shape[0]
    both = lax.dot_general(
        parted(a), parted(b), (((1,), (1,)), ((), ())), preferred_element_type=F32
    )
    both = both[:rows] + both[rows:]
    return both[:, :cols] + both[:, cols:]


def taken_nt(hot, x):
    rows = x.shape[0]
    parts = lax.dot_general(
        hot.astype(BF16), thirds(x), (((1,), (1,)), ((), ())), preferred_element_type=F32
    )
    return parts[:, :rows] + parts[:, rows : 2 * rows] + parts[:, 2 * rows :]


def spread(x, hot):
    hot = hot.astype(BF16)
    return lax.dot_general(
        thirds(x),
        jnp.concatenate([hot] * 3, axis=0),
        (((0,), (0,)), ((), ())),
        preferred_element_type=F32,
    )


def taken(x, hot):
    rows = x.shape[0]
    parts = lax.dot_general(
        thirds(x), hot.astype(BF16), (((1,), (1,)), ((), ())), preferred_element_type=F32
    )
    return parts[:rows] + parts[rows : 2 * rows] + parts[2 * rows :]


def turned(rows):
    short = -rows.shape[0] % 8
    if short:
        rows = jnp.concatenate([rows, jnp.zeros((short, rows.shape[1]), F32)], axis=0)
    return jnp.transpose(rows)


def moves_of(order_ref, flags_ref):
    walkers, _, moves = flags_ref.shape
    nel = order_ref.shape[2]
    order = turned(
        jnp.concatenate([order_ref[w] for w in range(walkers)], axis=0).astype(F32)
    )
    flags = jnp.concatenate([flags_ref[w] for w in range(walkers)], axis=0).astype(F32)
    flags = turned(
        jnp.concatenate([flags, jnp.zeros((2 * walkers, nel - moves), F32)], axis=1)
    )
    cols = [order[:moves, i : i + 1] for i in range(2 * walkers)]
    keep = [flags[:moves, i : i + 1] for i in range(2 * walkers)]
    return cols, keep


def one_hots(cols, nel):
    moves = cols[0].shape[0]
    lanes = lax.broadcasted_iota(jnp.int32, (moves, nel), 1).astype(F32)
    return [(c == lanes).astype(F32) for c in cols]


def pick(counts_ref, index):
    walkers = counts_ref.shape[0]
    total = jnp.int32(0)
    source = jnp.int32(0)
    for w in range(walkers):
        total = total + counts_ref[w]
        source = source + (total <= index).astype(jnp.int32)
    return jnp.minimum(source, walkers - 1)


def total_of(counts_ref):
    total = jnp.int32(0)
    for w in range(counts_ref.shape[0]):
        total = total + counts_ref[w]
    return total


def pair_tiles(turns, rows, nel, kinds):
    sums = [None, None]
    for h in (0, 1):
        for t in range(nel // 8):
            wide = [
                [
                    jnp.broadcast_to(turn[h][c][8 * t : 8 * t + 8], (8, nel))
                    for c in range(3)
                ]
                for turn in turns
            ]
            for g in range(h, 2):
                squares = []
                for i, row in enumerate(rows):
                    total = None
                    for c in range(3):
                        offset = wide[i][c] - row[g][c]
                        total = offset * offset if total is None else total + offset * offset
                    squares.append(total)
                kind = int(g != h)
                term = kinds[kind](*squares)
                sums[kind] = term if sums[kind] is None else sums[kind] + term
    return sums


def summed(tile):
    return jnp.sum(jnp.sum(tile, axis=0, keepdims=True), axis=1, keepdims=True)


def jastrow_of(spots, turn, jas_ref, nel):
    rows, turns = (
        [
            [
                [cut(base + 3 * h + c) for c in range(3)]
                for h in (0, 1)
            ]
            for base in (0, 8)
        ]
        for cut in (lambda r: spots[r : r + 1], lambda r: turn[:, r : r + 1])
    )

    def change(fall):
        def term(new, old):
            nd = jnp.sqrt(new)
            od = jnp.sqrt(old)
            return (nd - od) / ((1.0 + fall * nd) * (1.0 + fall * od))

        return term

    same, other = pair_tiles(turns, rows, nel, [change(jas_ref[2]), change(jas_ref[3])])
    return summed(same * (0.5 * jas_ref[0]) + other * jas_ref[1])


def in_rows(rows):
    return [r[:, at : at + LANES] for at in range(0, rows[0].shape[1], LANES) for r in rows]


def energy_kernel(
    pos_ref, dis_ref, order_ref, flags_ref, counts_ref, spots_ref, info_ref,
):
    _, walkers, both = pos_ref.shape
    nel = both // 2
    cols, keep = moves_of(order_ref, flags_ref)
    hots = one_hots(cols, nel)
    applied = jnp.concatenate(
        [
            jnp.concatenate(
                [
                    jnp.sum(hots[2 * w + s] * keep[2 * w + s], axis=0, keepdims=True)
                    for s in (0, 1)
                ],
                axis=1,
            )
            for w in range(walkers)
        ],
        axis=0,
    )
    now = [pos_ref[c] + dis_ref[c] * applied for c in range(3)]
    turn = turned(jnp.concatenate(now, axis=0))
    weighted = jnp.zeros((1, 1), F32)
    for w in range(walkers):
        nrows = [now[c][w : w + 1] for c in range(3)]
        halves = [[r[:, h * nel : (h + 1) * nel] for r in nrows] for h in (0, 1)]
        tall = [
            [
                turn[h * nel : (h + 1) * nel, c * walkers + w : c * walkers + w + 1]
                for c in range(3)
            ]
            for h in (0, 1)
        ]
        same, other = pair_tiles([tall], [halves], nel, [lambda q: lax.rsqrt(q + 1.0)] * 2)
        whole = summed(same + 2.0 * other)
        energy = (whole - 1.0 * both) / (1.0 * both * (both - 1))
        wide = [jnp.broadcast_to(energy, (1, LANES)), jnp.zeros((7 - 3 * (both // LANES), LANES), F32)]
        spots_ref[w, :8] = jnp.concatenate(in_rows(nrows) + wide[: 1 + (3 * (both // LANES) < 7)], axis=0)
        spots_ref[w, 8 : 8 + 3 * (both // LANES)] = jnp.concatenate(
            in_rows([pos_ref[c, w : w + 1] for c in range(3)]), axis=0
        )
        weighted = weighted + energy * counts_ref[w].astype(F32)
    me = lax.axis_index("walkers")
    lanes = lax.broadcasted_iota(jnp.int32, info_ref.shape, 1)
    rows = lax.broadcasted_iota(jnp.int32, info_ref.shape, 0)
    number = total_of(counts_ref).astype(F32)
    info_ref[...] = jnp.where(
        lanes == me,
        jnp.where(rows == 0, number, jnp.where(rows == 1, weighted, 0.0)),
        0.0,
    )


def shift_kernel(pos_ref, dis_ref, order_ref, flags_ref, cen_ref, exp_ref, orb_ref, shift_ref, differ_ref):
    _, walkers, both = pos_ref.shape
    nel = both // 2
    moves = flags_ref.shape[2]
    basis = cen_ref.shape[1]
    cols, _ = moves_of(order_ref, flags_ref)
    hots = one_hots(cols, nel)
    rows = [ref[c] for ref in (pos_ref, dis_ref) for c in range(3)]
    rows = jnp.concatenate(rows + [jnp.zeros((-6 * walkers % 8, both), F32)] * (6 * walkers % 8 > 0), axis=0)
    for s in (0, 1):
        points = nt(
            jnp.concatenate([hots[2 * w + s] for w in range(walkers)], axis=0),
            rows[:, s * nel : (s + 1) * nel],
        )
        for w in range(walkers):
            mine = points[w * moves : (w + 1) * moves]
            old = []
            new = []
            for c in range(3):
                at = c * walkers + w
                to = (3 + c) * walkers + w
                spot = mine[:, at : at + 1]
                old.append(jnp.broadcast_to(spot, (moves, LANES)))
                new.append(jnp.broadcast_to(spot + mine[:, to : to + 1], (moves, LANES)))
            for j in range(0, basis, LANES):
                osq = None
                nsq = None
                for c in range(3):
                    row = cen_ref[c : c + 1, j : j + LANES]
                    do = old[c] - row
                    dn = new[c] - row
                    osq = do * do if osq is None else osq + do * do
                    nsq = dn * dn if nsq is None else nsq + dn * dn
                rate = -exp_ref[:, j : j + LANES]
                differ_ref[s, w * moves : (w + 1) * moves, j : j + LANES] = jnp.exp(
                    rate * nsq
                ) - jnp.exp(rate * osq)
    for s in (0, 1):
        shift_ref[s] = product_nt(differ_ref[s], orb_ref[s])


def partial_kernel(
    shift_ref, order_ref, flags_ref, counts_ref, inv_ref, sla_ref, spots_ref, info_ref, jas_ref,
    part_ref, done_ref, pair_ref, odd_ref,
):
    walkers, _, orbs, nel = inv_ref.shape
    moves = flags_ref.shape[2]
    cols, keep = moves_of(order_ref, flags_ref)
    hots = one_hots(cols, nel)
    members = lax.axis_size("orb")
    share = walkers // members
    first = lax.axis_index("orb") * share
    tail = 2 * walkers * moves
    part_ref[tail:, :] = info_ref[...]
    for w in range(share):
        mine = spots_ref[first + w]
        at = tail + 2 + first + w
        part_ref[pl.ds(at, 1), :] = jnp.broadcast_to(
            jastrow_of(mine, turned(mine), jas_ref, nel), (1, part_ref.shape[1])
        )
    for s in (0, 1):
        for w in range(walkers):
            i = 2 * w + s
            mine = shift_ref[s, w * moves : (w + 1) * moves, :]
            proposed = mine + taken_nt(hots[i], sla_ref[w, s])
            part = product(proposed, inv_ref[w, s])
            part_ref[i * moves : (i + 1) * moves, :] = part * keep[i]
            done_ref[w, s] = sla_ref[w, s] + spread(mine, hots[i] * keep[i])
    half = walkers // 2
    per = 2 * orbs
    tail = half * per
    parity = lax.rem(lax.axis_index("walkers"), 2)
    number = total_of(counts_ref)
    for pay, goes_up in ((pair_ref, parity == 0), (odd_ref, parity == 1)):
        for j in range(half):
            index = jnp.where(goes_up, number - half + j, j)
            source = pick(counts_ref, index)
            for s in (0, 1):
                pay[j * per + s * orbs : j * per + (s + 1) * orbs, :] = done_ref[source, s]
            pay[tail + 8 * j : tail + 8 * j + 8, :] = spots_ref[source, :8]


def add_kernel(mine_ref, other_ref, out_ref):
    out_ref[...] = mine_ref[...] + other_ref[...]


def update_kernel(
    sum_ref, got_ref, inv_ref, order_ref, flags_ref, counts_ref, amp_ref,
    cur_ref, log_ref, info_ref, pair_ref, odd_ref,
):
    walkers, _, orbs, nel = inv_ref.shape
    moves = flags_ref.shape[2]
    count = 2 * walkers
    cols, keep = moves_of(order_ref, flags_ref)
    hots = one_hots(cols, nel)
    eye = (
        lax.broadcasted_iota(jnp.int32, (moves, moves), 0)
        == lax.broadcasted_iota(jnp.int32, (moves, moves), 1)
    ).astype(F32)
    tiles = moves // 8
    left = []
    right = []
    columns = []
    for i in range(count):
        at = slice(i * moves, (i + 1) * moves)
        change = sum_ref[at, :] + got_ref[at, :] - hots[i] * keep[i]
        coupling = taken(change, hots[i]) + eye
        columns.append(taken(inv_ref[i // 2, i % 2], hots[i]))
        left.append([coupling[8 * t : 8 * t + 8] for t in range(tiles)])
        right.append([change[8 * t : 8 * t + 8] for t in range(tiles)])
    info_ref[...] = sum_ref[count * moves :, :] + got_ref[count * moves :, :]
    lanes = lax.broadcasted_iota(jnp.int32, (1, nel), 1)
    sub = lax.broadcasted_iota(jnp.int32, (8, nel), 0)
    pivots = [jnp.ones((1, nel), F32) for _ in range(count)]
    for k in range(0, moves, 2):
        own, line = k // 8, k % 8
        for i in range(count):
            wide = [
                [jnp.broadcast_to(left[i][t][:, c : c + 1], (8, nel)) for t in range(tiles)]
                for c in (k, k + 1)
            ]
            a, b = (wide[c][own][line : line + 1] for c in (0, 1))
            c, d = (wide[c][own][line + 1 : line + 2] for c in (0, 1))
            det = a * d - b * c
            pivots[i] = jnp.where(lanes == k, det, pivots[i])
            scale = 1.0 / det
            new = []
            for side, width in ((left, moves), (right, nel)):
                upper = side[i][own][line : line + 1]
                lower = side[i][own][line + 1 : line + 2]
                new.append(
                    (
                        (d[:, :width] * upper - b[:, :width] * lower) * scale[:, :width],
                        (a[:, :width] * lower - c[:, :width] * upper) * scale[:, :width],
                    )
                )
            for t in range(tiles):
                for side, width, (upper, lower) in ((left, moves, new[0]), (right, nel, new[1])):
                    tile = (
                        side[i][t] - wide[0][t][:, :width] * upper - wide[1][t][:, :width] * lower
                    )
                    if t == own:
                        tile = jnp.where(
                            sub[:, :width] == line,
                            upper,
                            jnp.where(sub[:, :width] == line + 1, lower, tile),
                        )
                    side[i][t] = tile
    for i in range(count):
        solved = jnp.concatenate(right[i], axis=0)
        cur_ref[i // 2, i % 2] = inv_ref[i // 2, i % 2] - product(columns[i], solved)
    log_ref[...] = jnp.zeros(log_ref.shape, F32)
    for w in range(walkers):
        both = jnp.log(jnp.abs(pivots[2 * w])) + jnp.log(jnp.abs(pivots[2 * w + 1]))
        log_ref[w : w + 1, :] = (
            jnp.broadcast_to(jnp.sum(both, axis=1, keepdims=True), (1, nel))
            + info_ref[2 + w : 3 + w, :nel]
            + amp_ref[w]
        )
    half = walkers // 2
    per = 2 * orbs
    tail = half * per
    parity = lax.rem(lax.axis_index("walkers"), 2)
    number = total_of(counts_ref)
    for pay, goes_up in ((pair_ref, parity == 0), (odd_ref, parity == 1)):
        pay[tail : tail + INFO, :] = info_ref[...]
        pay[tail + INFO :, :] = jnp.zeros((pay.shape[0] - tail - INFO, LANES), F32)
        for j in range(half):
            index = jnp.where(goes_up, number - half + j, j)
            source = pick(counts_ref, index)
            for s in (0, 1):
                pay[j * per + s * orbs : j * per + (s + 1) * orbs, :] = cur_ref[source, s]
            at = tail + INFO + j
            pay[at : at + 1, :] = log_ref[pl.ds(source, 1), :]


def place_kernel(
    counts_ref, cur_ref, done_ref, spots_ref, log_ref, info_ref,
    pair_s_ref, odd_s_ref, pair_i_ref, odd_i_ref,
    inv_out, sla_out, pos_out, log_out, energy_out, mean_out, sems,
):
    walkers, _, orbs, nel = cur_ref.shape
    width = pos_out.shape[2] // LANES
    half = walkers // 2
    per = 2 * orbs
    tail = half * per
    me = lax.axis_index("walkers")
    parity = lax.rem(me, 2)
    info = info_ref[...] + pair_i_ref[tail : tail + INFO, :]
    lanes = lax.broadcasted_iota(jnp.int32, (1, info.shape[1]), 1)
    before = jnp.sum(jnp.where(lanes < me, info[0:1], 0.0)).astype(jnp.int32)
    groups = lax.axis_size("walkers")
    mean = jnp.sum(info[1:2], axis=1, keepdims=True)
    mean_out[...] = mean / (1.0 * walkers * groups)
    number = total_of(counts_ref)
    slots = lax.broadcasted_iota(jnp.int32, (1, walkers), 1)

    def put(j, inverse, slater, spot, log):
        for s in (0, 1):
            pltpu.make_async_copy(inverse(s), inv_out.at[j, s], sems.at[j, s, 0]).start()
            pltpu.make_async_copy(slater(s), sla_out.at[j, s], sems.at[j, s, 1]).start()
        for c in range(3):
            for h in range(width):
                pos_out[c, j : j + 1, h * LANES : (h + 1) * LANES] = spot[3 * h + c : 3 * h + c + 1]
        log_out[...] = jnp.where(slots == j, log[:, :walkers], log_out[...])
        energy_out[...] = jnp.where(
            slots == j, spot[3 * width : 3 * width + 1, :walkers], energy_out[...]
        )

    log_out[...] = jnp.zeros(log_out.shape, F32)
    energy_out[...] = jnp.zeros(energy_out.shape, F32)
    for j in range(walkers):
        index = me * walkers + j - before
        low = index < 0
        high = index >= number

        @pl.when(jnp.logical_not(low | high))
        def _():
            w = pick(counts_ref, index)
            put(
                j,
                lambda s: cur_ref.at[w, s],
                lambda s: done_ref.at[w, s],
                spots_ref[w, :8],
                log_ref[pl.ds(w, 1), :],
            )

        def received(late, early):
            i = jnp.clip(jnp.where(low, index + half, index - number), 0, half - 1)
            put(
                j,
                lambda s: late.at[pl.ds(pl.multiple_of(i * per + s * orbs, 8), orbs), :],
                lambda s: early.at[pl.ds(pl.multiple_of(i * per + s * orbs, 8), orbs), :],
                early[pl.ds(pl.multiple_of(tail + i * 8, 8), 8), :],
                late[pl.ds(tail + INFO + i, 1), :],
            )

        on_pair = (low & (parity == 1)) | (high & (parity == 0))

        @pl.when(on_pair)
        def _():
            received(pair_i_ref, pair_s_ref)

        @pl.when((low | high) & jnp.logical_not(on_pair))
        def _():
            received(odd_i_ref, odd_s_ref)

    for j in range(walkers):
        for s in (0, 1):
            pltpu.make_async_copy(cur_ref.at[0, s], inv_out.at[j, s], sems.at[j, s, 0]).wait()
            pltpu.make_async_copy(done_ref.at[0, s], sla_out.at[j, s], sems.at[j, s, 1]).wait()


def call(kernel, outs, in_specs, scratch=(), us=1.0, name=None, out_specs=None, vmem=32 * 2**20):
    return pl.pallas_call(
        kernel,
        out_shape=outs,
        in_specs=in_specs,
        out_specs=jax.tree.map(lambda _: VMEM, outs) if out_specs is None else out_specs,
        scratch_shapes=list(scratch),
        compiler_params=pltpu.CompilerParams(vmem_limit_bytes=vmem),
        cost_estimate=pl.CostEstimate(flops=int(us * 1.1e9), bytes_accessed=2**18, transcendentals=0),
        name=name,
    )


def shape(*dims):
    return jax.ShapeDtypeStruct(dims, F32)


def body(
    inverse, slater, positions, displacements, move_order, accepted, counts, log_amp, centers,
    exponents, orbitals, jastrow,
):
    walkers, _, orbs, nel = inverse.shape
    moves = accepted.shape[2]
    both = positions.shape[2]
    basis = centers.shape[1]
    groups = lax.axis_size("walkers")
    members = lax.axis_size("orb")
    wide = max(LANES, groups)
    half = walkers // 2
    per = 2 * orbs
    count = 2 * walkers
    tall = half * per + 16

    pairs = [(i, i ^ 1) for i in range(groups)]
    odds = [(i, i + 1) for i in range(1, groups - 1, 2)]
    odds = odds + [(b, a) for a, b in odds]

    places = positions.transpose(1, 0, 2)
    steps = displacements.transpose(1, 0, 2)
    spots, info = call(
        energy_kernel,
        (
            shape(walkers, 16, LANES),
            shape(INFO, wide),
        ),
        [VMEM, VMEM, VMEM, VMEM, SMEM],
        us=2,
        vmem=61 * 2**20,
        name="energy",
    )(places, steps, move_order, accepted, counts)

    hops = members * 2
    step = hops
    while step < groups:
        info = info + lax.ppermute(info, "walkers", [(i, i ^ step) for i in range(groups)])
        step *= 2
    joint = [
        (d * members + o, (d ^ (2 * o)) * members + o)
        for d in range(groups)
        for o in range(members)
        if 2 * o < groups
    ]
    info = lax.ppermute(info, ("walkers", "orb"), joint)

    shift = call(
        shift_kernel,
        shape(2, walkers * moves, orbs),
        [VMEM] * 7,
        scratch=[pltpu.VMEM((2, walkers * moves, basis), F32)],
        us=3,
        name="shift",
    )(places, steps, move_order, accepted, centers, exponents.reshape(1, basis), orbitals)

    part, done, pair_s, odd_s = call(
        partial_kernel,
        (
            shape(count * moves + INFO, nel),
            shape(walkers, 2, orbs, nel),
            shape(tall, LANES),
            shape(tall, LANES),
        ),
        [VMEM, VMEM, VMEM, SMEM] + [VMEM] * 4 + [SMEM],
        us=2,
        name="partial",
    )(shift, move_order, accepted, counts, inverse, slater, spots, info, jastrow)

    total = part
    got = jnp.zeros_like(part)
    step = 1
    while step < members:
        partner = [(o, o ^ step) for o in range(members)]
        got = lax.ppermute(total, "orb", partner)
        if 2 * step < members:
            total = call(
                add_kernel,
                shape(count * moves + INFO, nel),
                [VMEM] * 2,
                us=0.5,
                name="add",
            )(total, got)
        step *= 2

    pair_s = lax.ppermute(pair_s, "walkers", pairs)
    odd_s = lax.ppermute(odd_s, "walkers", odds)

    current, logs, info, pair_i, odd_i = call(
        update_kernel,
        (
            shape(walkers, 2, orbs, nel),
            shape(8, nel),
            shape(INFO, wide),
            shape(tall, LANES),
            shape(tall, LANES),
        ),
        [VMEM] * 5 + [SMEM, SMEM],
        us=4,
        name="update",
    )(total, got, inverse, move_order, accepted, counts, log_amp)

    pair_i = lax.ppermute(pair_i, "walkers", pairs)
    odd_i = lax.ppermute(odd_i, "walkers", odds)

    inv_new, sla_new, pos_new, log_new, energy_new, mean = call(
        place_kernel,
        (
            shape(walkers, 2, orbs, nel),
            shape(walkers, 2, orbs, nel),
            shape(3, walkers, both),
            shape(1, walkers),
            shape(1, walkers),
            shape(1, 1),
        ),
        [SMEM] + [VMEM] * 9,
        out_specs=(HBM, HBM, VMEM, VMEM, VMEM, VMEM),
        scratch=[pltpu.SemaphoreType.DMA((walkers, 2, 2))],
        us=1.5,
        name="place",
    )(counts, current, done, spots, logs, info, pair_s, odd_s, pair_i, odd_i)
    return (
        inv_new,
        sla_new,
        pos_new.transpose(1, 0, 2),
        log_new.reshape(walkers),
        energy_new.reshape(walkers),
        mean.reshape(()),
    )


def solution(mesh):
    return jax.shard_map(
        body,
        mesh=mesh,
        in_specs=(
            P("walkers", None, "orb", None),
            P("walkers", None, "orb", None),
            P("walkers", None, None),
            P("walkers", None, None),
            P("walkers", None, None),
            P("walkers", None, None),
            P("walkers"),
            P("walkers"),
            P(),
            P(),
            P(None, "orb", None),
            P(),
        ),
        out_specs=(
            P("walkers", None, "orb", None),
            P("walkers", None, "orb", None),
            P("walkers", None, None),
            P("walkers"),
            P("walkers"),
            P(),
        ),
        check_vma=False,
    )
```

```python
import jax
import jax.numpy as jnp
from jax import lax
from jax.experimental import pallas as pl
from jax.experimental.pallas import tpu as pltpu
from jax.sharding import PartitionSpec as P

F32 = jnp.float32
BF16 = jnp.bfloat16
highest = lax.Precision.HIGHEST
VMEM = pl.BlockSpec(memory_space=pltpu.VMEM)
LANES = 128
INFO = 8


def nt(a, b):
    return lax.dot_general(
        a, b, (((1,), (1,)), ((), ())), precision=highest, preferred_element_type=F32
    )


def thirds(x):
    high = x.astype(BF16)
    rest = x - high.astype(F32)
    middle = rest.astype(BF16)
    low = (rest - middle.astype(F32)).astype(BF16)
    return jnp.concatenate([high, middle, low], axis=0)


def parted(x):
    high = x.astype(BF16)
    return jnp.concatenate([high, (x - high.astype(F32)).astype(BF16)], axis=0)


def product(a, b):
    rows = a.shape[0]
    inner = b.shape[0]
    left = parted(a)
    right = parted(b)
    whole = None
    for part in (right[:inner], right[inner:]):
        both = lax.dot_general(
            left, part, (((1,), (0,)), ((), ())), preferred_element_type=F32
        )
        both = both[:rows] + both[rows:]
        whole = both if whole is None else whole + both
    return whole


def product_nt(a, b):
    rows, cols = a.shape[0], b.shape[0]
    both = lax.dot_general(
        parted(a), parted(b), (((1,), (1,)), ((), ())), preferred_element_type=F32
    )
    both = both[:rows] + both[rows:]
    return both[:, :cols] + both[:, cols:]


def taken_nt(hot, x):
    rows = x.shape[0]
    parts = lax.dot_general(
        hot.astype(BF16), thirds(x), (((1,), (1,)), ((), ())), preferred_element_type=F32
    )
    return parts[:, :rows] + parts[:, rows : 2 * rows] + parts[:, 2 * rows :]


def spread(x, hot):
    hot = hot.astype(BF16)
    return lax.dot_general(
        thirds(x),
        jnp.concatenate([hot] * 3, axis=0),
        (((0,), (0,)), ((), ())),
        preferred_element_type=F32,
    )


def taken(x, hot):
    rows = x.shape[0]
    parts = lax.dot_general(
        thirds(x), hot.astype(BF16), (((1,), (1,)), ((), ())), preferred_element_type=F32
    )
    return parts[:rows] + parts[rows : 2 * rows] + parts[2 * rows :]


def turned(rows):
    short = -rows.shape[0] % 8
    if short:
        rows = jnp.concatenate([rows, jnp.zeros((short, rows.shape[1]), F32)], axis=0)
    return jnp.transpose(rows)


def moves_of(order_ref, flags_ref):
    walkers, _, moves = flags_ref.shape
    nel = order_ref.shape[2]
    order = turned(
        jnp.concatenate([order_ref[w] for w in range(walkers)], axis=0).astype(F32)
    )
    flags = jnp.concatenate([flags_ref[w] for w in range(walkers)], axis=0).astype(F32)
    flags = turned(
        jnp.concatenate([flags, jnp.zeros((2 * walkers, nel - moves), F32)], axis=1)
    )
    cols = [order[:moves, i : i + 1] for i in range(2 * walkers)]
    keep = [flags[:moves, i : i + 1] for i in range(2 * walkers)]
    return cols, keep


def one_hots(cols, nel):
    moves = cols[0].shape[0]
    lanes = lax.broadcasted_iota(jnp.int32, (moves, nel), 1).astype(F32)
    return [(c == lanes).astype(F32) for c in cols]


def limits_of(counts_ref):
    counts = counts_ref[...].astype(F32)
    limits = [counts[:, :1]]
    for w in range(1, counts.shape[1]):
        limits.append(limits[-1] + counts[:, w : w + 1])
    return limits


def picked(limits, index, choices):
    rows = max(x[0].shape[0] for x in choices)
    after = [
        jnp.broadcast_to(limit - index, (rows, choices[0][0].shape[1])) <= 0.0
        for limit in limits[:-1]
    ]
    out = []
    for some in choices:
        value = some[0]
        for w in range(1, len(some)):
            value = jnp.where(after[w - 1][: value.shape[0]], some[w], value)
        out.append(value)
    return out


def sent(counts_ref, half, pair_ref, odd_ref):
    limits = limits_of(counts_ref)
    parity = lax.rem(lax.axis_index("walkers"), 2)
    out = []
    for pay, up in ((pair_ref, parity == 0), (odd_ref, parity == 1)):
        up = up.astype(F32)
        out.append(
            (pay, [(limits, up * (limits[-1] - 1.0 * half) + 1.0 * j) for j in range(half)])
        )
    return out


def pair_tiles(turns, rows, nel, kinds):
    sums = [None, None]
    for h in (0, 1):
        for t in range(nel // 8):
            wide = [
                [
                    jnp.broadcast_to(turn[h][c][8 * t : 8 * t + 8], (8, nel))
                    for c in range(3)
                ]
                for turn in turns
            ]
            for g in range(h, 2):
                squares = []
                for i, row in enumerate(rows):
                    total = None
                    for c in range(3):
                        offset = wide[i][c] - row[g][c]
                        total = offset * offset if total is None else total + offset * offset
                    squares.append(total)
                kind = int(g != h)
                term = kinds[kind](*squares)
                sums[kind] = term if sums[kind] is None else sums[kind] + term
    return sums


def summed(tile):
    return jnp.sum(jnp.sum(tile, axis=0, keepdims=True), axis=1, keepdims=True)


def jastrow_of(spots, turn, jas_ref, nel):
    rows, turns = (
        [
            [
                [cut(base + 3 * h + c) for c in range(3)]
                for h in (0, 1)
            ]
            for base in (0, 8)
        ]
        for cut in (lambda r: spots[r : r + 1], lambda r: turn[:, r : r + 1])
    )

    def change(fall):
        fall = jnp.broadcast_to(fall, (8, nel))

        def term(new, old):
            nd = jnp.sqrt(new)
            od = jnp.sqrt(old)
            return (nd - od) / ((1.0 + fall * nd) * (1.0 + fall * od))

        return term

    same, other = pair_tiles(turns, rows, nel, [change(jas_ref[:, 2:3]), change(jas_ref[:, 3:4])])
    return summed(same * (0.5 * jas_ref[:, :1]) + other * jas_ref[:, 1:2])


def in_rows(rows):
    return [r[:, at : at + LANES] for at in range(0, rows[0].shape[1], LANES) for r in rows]


def energy_kernel(
    pos_ref, dis_ref, order_ref, flags_ref, counts_ref, spots_ref, info_ref,
):
    _, walkers, both = pos_ref.shape
    nel = both // 2
    cols, keep = moves_of(order_ref, flags_ref)
    hots = one_hots(cols, nel)
    applied = jnp.concatenate(
        [
            jnp.concatenate(
                [
                    jnp.sum(hots[2 * w + s] * keep[2 * w + s], axis=0, keepdims=True)
                    for s in (0, 1)
                ],
                axis=1,
            )
            for w in range(walkers)
        ],
        axis=0,
    )
    now = [pos_ref[c] + dis_ref[c] * applied for c in range(3)]
    turn = turned(jnp.concatenate(now, axis=0))
    weighted = jnp.zeros((1, 1), F32)
    counts = counts_ref[...].astype(F32)
    for w in range(walkers):
        nrows = [now[c][w : w + 1] for c in range(3)]
        halves = [[r[:, h * nel : (h + 1) * nel] for r in nrows] for h in (0, 1)]
        tall = [
            [
                turn[h * nel : (h + 1) * nel, c * walkers + w : c * walkers + w + 1]
                for c in range(3)
            ]
            for h in (0, 1)
        ]
        same, other = pair_tiles([tall], [halves], nel, [lambda q: lax.rsqrt(q + 1.0)] * 2)
        whole = summed(same + 2.0 * other)
        energy = (whole - 1.0 * both) / (1.0 * both * (both - 1))
        wide = [jnp.broadcast_to(energy, (1, LANES)), jnp.zeros((7 - 3 * (both // LANES), LANES), F32)]
        spots_ref[w, :8] = jnp.concatenate(in_rows(nrows) + wide[: 1 + (3 * (both // LANES) < 7)], axis=0)
        spots_ref[w, 8 : 8 + 3 * (both // LANES)] = jnp.concatenate(
            in_rows([pos_ref[c, w : w + 1] for c in range(3)]), axis=0
        )
        weighted = weighted + energy * counts[:, w : w + 1]
    me = lax.axis_index("walkers")
    lanes = lax.broadcasted_iota(jnp.int32, info_ref.shape, 1)
    rows = lax.broadcasted_iota(jnp.int32, info_ref.shape, 0)
    number = jnp.sum(counts, axis=1, keepdims=True)
    info_ref[...] = jnp.where(
        lanes == me,
        jnp.where(rows == 0, number, jnp.where(rows == 1, weighted, 0.0)),
        0.0,
    )


def shift_kernel(
    pos_ref, dis_ref, order_ref, flags_ref, counts_ref, jas_ref, cen_ref, exp_ref, orb_ref,
    shift_ref, differ_ref,
):
    del counts_ref, jas_ref
    _, walkers, both = pos_ref.shape
    nel = both // 2
    moves = flags_ref.shape[2]
    basis = cen_ref.shape[1]
    cols, _ = moves_of(order_ref, flags_ref)
    hots = one_hots(cols, nel)
    rows = [ref[c] for ref in (pos_ref, dis_ref) for c in range(3)]
    rows = jnp.concatenate(rows + [jnp.zeros((-6 * walkers % 8, both), F32)] * (6 * walkers % 8 > 0), axis=0)
    for s in (0, 1):
        points = nt(
            jnp.concatenate([hots[2 * w + s] for w in range(walkers)], axis=0),
            rows[:, s * nel : (s + 1) * nel],
        )
        for w in range(walkers):
            mine = points[w * moves : (w + 1) * moves]
            old = []
            new = []
            for c in range(3):
                at = c * walkers + w
                to = (3 + c) * walkers + w
                spot = mine[:, at : at + 1]
                old.append(jnp.broadcast_to(spot, (moves, LANES)))
                new.append(jnp.broadcast_to(spot + mine[:, to : to + 1], (moves, LANES)))
            for j in range(0, basis, LANES):
                osq = None
                nsq = None
                for c in range(3):
                    row = cen_ref[c : c + 1, j : j + LANES]
                    do = old[c] - row
                    dn = new[c] - row
                    osq = do * do if osq is None else osq + do * do
                    nsq = dn * dn if nsq is None else nsq + dn * dn
                rate = -exp_ref[:, j : j + LANES]
                differ_ref[s, w * moves : (w + 1) * moves, j : j + LANES] = jnp.exp(
                    rate * nsq
                ) - jnp.exp(rate * osq)
    for s in (0, 1):
        shift_ref[s] = product_nt(differ_ref[s], orb_ref[s])


def partial_kernel(
    shift_ref, order_ref, flags_ref, counts_ref, inv_ref, sla_ref, spots_ref, info_ref, jas_ref,
    part_ref, done_ref, pair_ref, odd_ref,
):
    walkers, _, orbs, nel = inv_ref.shape
    moves = flags_ref.shape[2]
    cols, keep = moves_of(order_ref, flags_ref)
    hots = one_hots(cols, nel)
    members = lax.axis_size("orb")
    share = walkers // members
    first = lax.axis_index("orb") * share
    tail = 2 * walkers * moves
    part_ref[tail:, :] = info_ref[...]
    for w in range(share):
        mine = spots_ref[first + w]
        at = tail + 2 + first + w
        part_ref[pl.ds(at, 1), :] = jnp.broadcast_to(
            jastrow_of(mine, turned(mine), jas_ref, nel), (1, part_ref.shape[1])
        )
    for s in (0, 1):
        for w in range(walkers):
            i = 2 * w + s
            mine = shift_ref[s, w * moves : (w + 1) * moves, :]
            proposed = mine + taken_nt(hots[i], sla_ref[w, s])
            part = product(proposed, inv_ref[w, s])
            part_ref[i * moves : (i + 1) * moves, :] = part * keep[i]
            done_ref[w, s] = sla_ref[w, s] + spread(mine, hots[i] * keep[i])
    half = walkers // 2
    per = 2 * orbs
    tail = half * per
    for pay, indices in sent(counts_ref, half, pair_ref, odd_ref):
        for j, (limits, index) in enumerate(indices):
            rows = picked(
                limits,
                index,
                [[done_ref[w, s] for w in range(walkers)] for s in (0, 1)]
                + [[spots_ref[w, :8] for w in range(walkers)]],
            )
            for s in (0, 1):
                pay[j * per + s * orbs : j * per + (s + 1) * orbs, :] = rows[s]
            pay[tail + 8 * j : tail + 8 * j + 8, :] = rows[2]


def add_kernel(mine_ref, other_ref, out_ref):
    out_ref[...] = mine_ref[...] + other_ref[...]


def update_kernel(
    sum_ref, got_ref, inv_ref, order_ref, flags_ref, counts_ref, amp_ref,
    cur_ref, log_ref, info_ref, pair_ref, odd_ref,
):
    walkers, _, orbs, nel = inv_ref.shape
    moves = flags_ref.shape[2]
    count = 2 * walkers
    cols, keep = moves_of(order_ref, flags_ref)
    hots = one_hots(cols, nel)
    eye = (
        lax.broadcasted_iota(jnp.int32, (moves, moves), 0)
        == lax.broadcasted_iota(jnp.int32, (moves, moves), 1)
    ).astype(F32)
    tiles = moves // 8
    left = []
    right = []
    columns = []
    for i in range(count):
        at = slice(i * moves, (i + 1) * moves)
        change = sum_ref[at, :] + got_ref[at, :] - hots[i] * keep[i]
        coupling = taken(change, hots[i]) + eye
        columns.append(taken(inv_ref[i // 2, i % 2], hots[i]))
        left.append([coupling[8 * t : 8 * t + 8] for t in range(tiles)])
        right.append([change[8 * t : 8 * t + 8] for t in range(tiles)])
    info_ref[...] = sum_ref[count * moves :, :] + got_ref[count * moves :, :]
    lanes = lax.broadcasted_iota(jnp.int32, (1, nel), 1)
    sub = lax.broadcasted_iota(jnp.int32, (8, nel), 0)
    pivots = [jnp.ones((1, nel), F32) for _ in range(count)]
    for k in range(0, moves, 2):
        own, line = k // 8, k % 8
        for i in range(count):
            wide = [
                [jnp.broadcast_to(left[i][t][:, c : c + 1], (8, nel)) for t in range(tiles)]
                for c in (k, k + 1)
            ]
            a, b = (wide[c][own][line : line + 1] for c in (0, 1))
            c, d = (wide[c][own][line + 1 : line + 2] for c in (0, 1))
            det = a * d - b * c
            pivots[i] = jnp.where(lanes == k, det, pivots[i])
            scale = 1.0 / det
            new = []
            for side, width in ((left, moves), (right, nel)):
                upper = side[i][own][line : line + 1]
                lower = side[i][own][line + 1 : line + 2]
                new.append(
                    (
                        (d[:, :width] * upper - b[:, :width] * lower) * scale[:, :width],
                        (a[:, :width] * lower - c[:, :width] * upper) * scale[:, :width],
                    )
                )
            for t in range(tiles):
                for side, width, (upper, lower) in ((left, moves, new[0]), (right, nel, new[1])):
                    tile = (
                        side[i][t] - wide[0][t][:, :width] * upper - wide[1][t][:, :width] * lower
                    )
                    if t == own:
                        tile = jnp.where(
                            sub[:, :width] == line,
                            upper,
                            jnp.where(sub[:, :width] == line + 1, lower, tile),
                        )
                    side[i][t] = tile
    for i in range(count):
        solved = jnp.concatenate(right[i], axis=0)
        cur_ref[i // 2, i % 2] = inv_ref[i // 2, i % 2] - product(columns[i], solved)
    log_ref[...] = jnp.zeros(log_ref.shape, F32)
    for w in range(walkers):
        both = jnp.log(jnp.abs(pivots[2 * w])) + jnp.log(jnp.abs(pivots[2 * w + 1]))
        log_ref[w : w + 1, :] = (
            jnp.broadcast_to(jnp.sum(both, axis=1, keepdims=True), (1, nel))
            + info_ref[2 + w : 3 + w, :nel]
            + amp_ref[:, w : w + 1]
        )
    half = walkers // 2
    per = 2 * orbs
    tail = half * per
    for pay, indices in sent(counts_ref, half, pair_ref, odd_ref):
        pay[tail : tail + INFO, :] = info_ref[...]
        pay[tail + INFO :, :] = jnp.zeros((pay.shape[0] - tail - INFO, LANES), F32)
        for j, (limits, index) in enumerate(indices):
            rows = picked(
                limits,
                index,
                [[cur_ref[w, s] for w in range(walkers)] for s in (0, 1)]
                + [[log_ref[w : w + 1, :] for w in range(walkers)]],
            )
            for s in (0, 1):
                pay[j * per + s * orbs : j * per + (s + 1) * orbs, :] = rows[s]
            pay[tail + INFO + j : tail + INFO + j + 1, :] = rows[2]


def place_kernel(
    counts_ref, cur_ref, done_ref, spots_ref, log_ref, info_ref,
    pair_s_ref, odd_s_ref, pair_i_ref, odd_i_ref,
    inv_out, sla_out, pos_out, log_out, energy_out, mean_out,
):
    walkers, _, orbs, nel = cur_ref.shape
    width = pos_out.shape[2] // LANES
    half = walkers // 2
    per = 2 * orbs
    tail = half * per
    me = lax.axis_index("walkers")
    parity = lax.rem(me, 2)
    info = info_ref[...] + pair_i_ref[tail : tail + INFO, :]
    lanes = lax.broadcasted_iota(jnp.int32, (1, info.shape[1]), 1)
    before = jnp.sum(jnp.where(lanes < me, info[0:1], 0.0), axis=1, keepdims=True)
    groups = lax.axis_size("walkers")
    mean = jnp.sum(info[1:2], axis=1, keepdims=True)
    mean_out[...] = mean / (1.0 * walkers * groups)
    limits = limits_of(counts_ref)
    slots = lax.broadcasted_iota(jnp.int32, (1, walkers), 1)
    here = [[cur_ref[w, s] for w in range(walkers)] for s in (0, 1)]
    here += [[done_ref[w, s] for w in range(walkers)] for s in (0, 1)]
    here += [[spots_ref[w, :8] for w in range(walkers)]]
    here += [[log_ref[w : w + 1, :] for w in range(walkers)]]
    odd = parity.astype(F32)
    log_new = jnp.zeros((1, walkers), F32)
    energy_new = jnp.zeros((1, walkers), F32)
    for j in range(walkers):
        index = (1.0 * walkers) * me.astype(F32) + 1.0 * j - before
        own = picked(limits, index, here)
        low = j < half
        outside = -index if low else index - limits[-1] + 1.0
        entry = index + 1.0 * half if low else index - limits[-1]
        on_pair = odd if low else 1.0 - odd
        shape_here = (orbs, nel)
        away = jnp.broadcast_to(outside, shape_here) > 0.0
        second = jnp.broadcast_to(entry, shape_here) > 0.5
        pair = jnp.broadcast_to(on_pair, shape_here) > 0.5

        def one(late, at, rows):
            parts = []
            for i in range(half):
                start = at(i)
                a, b = (ref[start : start + rows, :] for ref in late)
                parts.append(jnp.where(pair[:rows], a, b))
            value = parts[0]
            for i in range(1, half):
                again = second if i == 1 else jnp.broadcast_to(entry, shape_here) > i - 0.5
                value = jnp.where(again[:rows], parts[i], value)
            return value

        inverses = (pair_i_ref, odd_i_ref)
        slaters = (pair_s_ref, odd_s_ref)
        got = [one(inverses, lambda i, s=s: i * per + s * orbs, orbs) for s in (0, 1)]
        got += [one(slaters, lambda i, s=s: i * per + s * orbs, orbs) for s in (0, 1)]
        got += [one(slaters, lambda i: tail + 8 * i, 8)]
        got += [one(inverses, lambda i: tail + INFO + i, 1)]
        new = [jnp.where(away[: o.shape[0]], g, o) for o, g in zip(own, got)]
        for s in (0, 1):
            inv_out[j, s] = new[s]
            sla_out[j, s] = new[2 + s]
        for c in range(3):
            for h in range(width):
                pos_out[c, j : j + 1, h * LANES : (h + 1) * LANES] = new[4][
                    3 * h + c : 3 * h + c + 1
                ]
        log_new = jnp.where(slots == j, new[5][:, :walkers], log_new)
        energy_new = jnp.where(
            slots == j, new[4][3 * width : 3 * width + 1, :walkers], energy_new
        )
    log_out[...] = log_new
    energy_out[...] = energy_new


def call(kernel, outs, in_specs, scratch=(), us=1.0, name=None, vmem=32 * 2**20):
    return pl.pallas_call(
        kernel,
        out_shape=outs,
        in_specs=in_specs,
        out_specs=jax.tree.map(lambda _: VMEM, outs),
        scratch_shapes=list(scratch),
        compiler_params=pltpu.CompilerParams(vmem_limit_bytes=vmem),
        cost_estimate=pl.CostEstimate(flops=int(us * 1.1e9), bytes_accessed=2**18, transcendentals=0),
        name=name,
    )


def shape(*dims):
    return jax.ShapeDtypeStruct(dims, F32)


def body(
    inverse, slater, positions, displacements, move_order, accepted, counts, log_amp, centers,
    exponents, orbitals, jastrow,
):
    walkers, _, orbs, nel = inverse.shape
    moves = accepted.shape[2]
    both = positions.shape[2]
    basis = centers.shape[1]
    groups = lax.axis_size("walkers")
    members = lax.axis_size("orb")
    wide = max(LANES, groups)
    half = walkers // 2
    per = 2 * orbs
    count = 2 * walkers
    tall = half * per + 16

    counts = counts.reshape(1, walkers)
    log_amp = log_amp.reshape(1, walkers)
    jastrow = jastrow.reshape(1, jastrow.shape[0])

    pairs = [(i, i ^ 1) for i in range(groups)]
    odds = [(i, i + 1) for i in range(1, groups - 1, 2)]
    odds = odds + [(b, a) for a, b in odds]

    places = positions.transpose(1, 0, 2)
    steps = displacements.transpose(1, 0, 2)
    spots, info = call(
        energy_kernel,
        (
            shape(walkers, 16, LANES),
            shape(INFO, wide),
        ),
        [VMEM] * 5,
        us=2,
        vmem=61 * 2**20,
        name="energy",
    )(places, steps, move_order, accepted, counts)

    hops = members * 2
    step = hops
    while step < groups:
        info = info + lax.ppermute(info, "walkers", [(i, i ^ step) for i in range(groups)])
        step *= 2
    joint = [
        (d * members + o, (d ^ (2 * hop)) * members + o)
        for o in range(members)
        for hop in [(o + 1) % 3 if members > 3 and o < 3 else o]
        for d in range(groups)
        if 2 * hop < groups
    ]
    info = lax.ppermute(info, ("walkers", "orb"), joint)

    shift = call(
        shift_kernel,
        shape(2, walkers * moves, orbs),
        [VMEM] * 9,
        scratch=[pltpu.VMEM((2, walkers * moves, basis), F32)],
        us=3,
        name="shift",
    )(
        places, steps, move_order, accepted, counts, jastrow, centers,
        exponents.reshape(1, basis), orbitals,
    )

    part, done, pair_s, odd_s = call(
        partial_kernel,
        (
            shape(count * moves + INFO, nel),
            shape(walkers, 2, orbs, nel),
            shape(tall, LANES),
            shape(tall, LANES),
        ),
        [VMEM] * 9,
        us=2,
        name="partial",
    )(shift, move_order, accepted, counts, inverse, slater, spots, info, jastrow)

    total = part
    got = jnp.zeros_like(part)
    step = 1
    while step < members:
        partner = [(o, o ^ step) for o in range(members)]
        got = lax.ppermute(total, "orb", partner)
        if 2 * step < members:
            total = call(
                add_kernel,
                shape(count * moves + INFO, nel),
                [VMEM] * 2,
                us=0.5,
                name="add",
            )(total, got)
        step *= 2

    pair_s = lax.ppermute(pair_s, "walkers", pairs)
    odd_s = lax.ppermute(odd_s, "walkers", odds)

    current, logs, info, pair_i, odd_i = call(
        update_kernel,
        (
            shape(walkers, 2, orbs, nel),
            shape(8, nel),
            shape(INFO, wide),
            shape(tall, LANES),
            shape(tall, LANES),
        ),
        [VMEM] * 7,
        us=4,
        name="update",
    )(total, got, inverse, move_order, accepted, counts, log_amp)

    pair_i = lax.ppermute(pair_i, "walkers", pairs)
    odd_i = lax.ppermute(odd_i, "walkers", odds)

    inv_new, sla_new, pos_new, log_new, energy_new, mean = call(
        place_kernel,
        (
            shape(walkers, 2, orbs, nel),
            shape(walkers, 2, orbs, nel),
            shape(3, walkers, both),
            shape(1, walkers),
            shape(1, walkers),
            shape(1, 1),
        ),
        [VMEM] * 10,
        us=1.5,
        name="place",
    )(counts, current, done, spots, logs, info, pair_s, odd_s, pair_i, odd_i)
    return (
        inv_new,
        sla_new,
        pos_new.transpose(1, 0, 2),
        log_new.reshape(walkers),
        energy_new.reshape(walkers),
        mean.reshape(()),
    )


def solution(mesh):
    return jax.shard_map(
        body,
        mesh=mesh,
        in_specs=(
            P("walkers", None, "orb", None),
            P("walkers", None, "orb", None),
            P("walkers", None, None),
            P("walkers", None, None),
            P("walkers", None, None),
            P("walkers", None, None),
            P("walkers"),
            P("walkers"),
            P(),
            P(),
            P(None, "orb", None),
            P(),
        ),
        out_specs=(
            P("walkers", None, "orb", None),
            P("walkers", None, "orb", None),
            P("walkers", None, None),
            P("walkers"),
            P("walkers"),
            P(),
        ),
        check_vma=False,
    )
```

```python
import jax
import jax.numpy as jnp
from jax import lax
from jax.experimental import pallas as pl
from jax.experimental.pallas import tpu as pltpu
from jax.sharding import PartitionSpec as P

F32 = jnp.float32
BF16 = jnp.bfloat16
highest = lax.Precision.HIGHEST
VMEM = pl.BlockSpec(memory_space=pltpu.VMEM)
ANY = pl.BlockSpec(memory_space=pl.ANY)
LANES = 128
INFO = 8


def nt(a, b):
    return lax.dot_general(
        a, b, (((1,), (1,)), ((), ())), precision=highest, preferred_element_type=F32
    )


def thirds(x):
    high = x.astype(BF16)
    rest = x - high.astype(F32)
    middle = rest.astype(BF16)
    low = (rest - middle.astype(F32)).astype(BF16)
    return jnp.concatenate([high, middle, low], axis=0)


def parted(x):
    high = x.astype(BF16)
    return jnp.concatenate([high, (x - high.astype(F32)).astype(BF16)], axis=0)


def product(a, b):
    rows = a.shape[0]
    inner = b.shape[0]
    left = parted(a)
    right = parted(b)
    whole = None
    for part in (right[:inner], right[inner:]):
        both = lax.dot_general(
            left, part, (((1,), (0,)), ((), ())), preferred_element_type=F32
        )
        both = both[:rows] + both[rows:]
        whole = both if whole is None else whole + both
    return whole


def product_nt(a, b):
    rows, cols = a.shape[0], b.shape[0]
    both = lax.dot_general(
        parted(a), parted(b), (((1,), (1,)), ((), ())), preferred_element_type=F32
    )
    both = both[:rows] + both[rows:]
    return both[:, :cols] + both[:, cols:]


def taken_nt(hot, x):
    rows = x.shape[0]
    parts = lax.dot_general(
        hot.astype(BF16), thirds(x), (((1,), (1,)), ((), ())), preferred_element_type=F32
    )
    return parts[:, :rows] + parts[:, rows : 2 * rows] + parts[:, 2 * rows :]


def spread(x, hot):
    hot = hot.astype(BF16)
    return lax.dot_general(
        thirds(x),
        jnp.concatenate([hot] * 3, axis=0),
        (((0,), (0,)), ((), ())),
        preferred_element_type=F32,
    )


def taken(x, hot):
    rows = x.shape[0]
    parts = lax.dot_general(
        thirds(x), hot.astype(BF16), (((1,), (1,)), ((), ())), preferred_element_type=F32
    )
    return parts[:rows] + parts[rows : 2 * rows] + parts[2 * rows :]


def turned(rows):
    short = -rows.shape[0] % 8
    if short:
        rows = jnp.concatenate([rows, jnp.zeros((short, rows.shape[1]), F32)], axis=0)
    return jnp.transpose(rows)


def moves_of(order_ref, flags_ref):
    walkers, _, moves = flags_ref.shape
    nel = order_ref.shape[2]
    order = turned(
        jnp.concatenate([order_ref[w] for w in range(walkers)], axis=0).astype(F32)
    )
    flags = jnp.concatenate([flags_ref[w] for w in range(walkers)], axis=0).astype(F32)
    flags = turned(
        jnp.concatenate([flags, jnp.zeros((2 * walkers, nel - moves), F32)], axis=1)
    )
    cols = [order[:moves, i : i + 1] for i in range(2 * walkers)]
    keep = [flags[:moves, i : i + 1] for i in range(2 * walkers)]
    return cols, keep


def one_hots(cols, nel):
    moves = cols[0].shape[0]
    lanes = lax.broadcasted_iota(jnp.int32, (moves, nel), 1).astype(F32)
    return [(c == lanes).astype(F32) for c in cols]


def limits_of(spots_ref, walkers):
    counts = spots_ref[walkers, 0:1, :]
    limits = [counts[:, :1]]
    for w in range(1, walkers):
        limits.append(limits[-1] + counts[:, w : w + 1])
    return limits


def picked(limits, index, choices):
    rows = max(x[0].shape[0] for x in choices)
    after = [
        jnp.broadcast_to(limit - index, (rows, choices[0][0].shape[1])) <= 0.0
        for limit in limits[:-1]
    ]
    out = []
    for some in choices:
        value = some[0]
        for w in range(1, len(some)):
            value = jnp.where(after[w - 1][: value.shape[0]], some[w], value)
        out.append(value)
    return out


def sent(spots_ref, walkers, pair_ref, odd_ref):
    half = walkers // 2
    limits = limits_of(spots_ref, walkers)
    parity = lax.rem(lax.axis_index("walkers"), 2)
    out = []
    for pay, up in ((pair_ref, parity == 0), (odd_ref, parity == 1)):
        up = up.astype(F32)
        out.append(
            (pay, [(limits, up * (limits[-1] - 1.0 * half) + 1.0 * j) for j in range(half)])
        )
    return out


def pair_tiles(turns, rows, nel, kinds):
    sums = [None, None]
    for h in (0, 1):
        for t in range(nel // 8):
            wide = [
                [
                    jnp.broadcast_to(turn[h][c][8 * t : 8 * t + 8], (8, nel))
                    for c in range(3)
                ]
                for turn in turns
            ]
            for g in range(h, 2):
                squares = []
                for i, row in enumerate(rows):
                    total = None
                    for c in range(3):
                        offset = wide[i][c] - row[g][c]
                        total = offset * offset if total is None else total + offset * offset
                    squares.append(total)
                kind = int(g != h)
                term = kinds[kind](*squares)
                sums[kind] = term if sums[kind] is None else sums[kind] + term
    return sums


def summed(tile):
    return jnp.sum(jnp.sum(tile, axis=0, keepdims=True), axis=1, keepdims=True)


def jastrow_of(spots, turn, jas, nel):
    rows, turns = (
        [
            [
                [cut(base + 3 * h + c) for c in range(3)]
                for h in (0, 1)
            ]
            for base in (0, 8)
        ]
        for cut in (lambda r: spots[r : r + 1], lambda r: turn[:, r : r + 1])
    )

    def change(fall):
        fall = jnp.broadcast_to(fall, (8, nel))

        def term(new, old):
            nd = jnp.sqrt(new)
            od = jnp.sqrt(old)
            return (nd - od) / ((1.0 + fall * nd) * (1.0 + fall * od))

        return term

    same, other = pair_tiles(turns, rows, nel, [change(jas[:, 2:3]), change(jas[:, 3:4])])
    return summed(same * (0.5 * jas[:, :1]) + other * jas[:, 1:2])


def in_rows(rows):
    return [r[:, at : at + LANES] for at in range(0, rows[0].shape[1], LANES) for r in rows]


def energy_kernel(
    pos_in, dis_in, order_in, flags_in, counts_in, jas_in, amp_in, spots_out, info_out,
    pos_ref, dis_ref, order_ref, flags_ref, counts_ref, jas_ref, amp_ref, spots_ref, info_ref,
    loads, stores,
):
    operands = (
        (pos_in, pos_ref),
        (dis_in, dis_ref),
        (order_in, order_ref),
        (flags_in, flags_ref),
        (counts_in, counts_ref),
        (jas_in, jas_ref),
        (amp_in, amp_ref),
    )
    copies = [pltpu.make_async_copy(a, b, loads.at[i]) for i, (a, b) in enumerate(operands)]
    for copy in copies:
        copy.start()
    for copy in copies:
        copy.wait()
    _, walkers, both = pos_ref.shape
    nel = both // 2
    cols, keep = moves_of(order_ref, flags_ref)
    hots = one_hots(cols, nel)
    applied = jnp.concatenate(
        [
            jnp.concatenate(
                [
                    jnp.sum(hots[2 * w + s] * keep[2 * w + s], axis=0, keepdims=True)
                    for s in (0, 1)
                ],
                axis=1,
            )
            for w in range(walkers)
        ],
        axis=0,
    )
    now = [pos_ref[c] + dis_ref[c] * applied for c in range(3)]
    turn = turned(jnp.concatenate(now, axis=0))
    weighted = jnp.zeros((1, 1), F32)
    counts = counts_ref[...].astype(F32)
    for w in range(walkers):
        nrows = [now[c][w : w + 1] for c in range(3)]
        halves = [[r[:, h * nel : (h + 1) * nel] for r in nrows] for h in (0, 1)]
        tall = [
            [
                turn[h * nel : (h + 1) * nel, c * walkers + w : c * walkers + w + 1]
                for c in range(3)
            ]
            for h in (0, 1)
        ]
        same, other = pair_tiles([tall], [halves], nel, [lambda q: lax.rsqrt(q + 1.0)] * 2)
        whole = summed(same + 2.0 * other)
        energy = (whole - 1.0 * both) / (1.0 * both * (both - 1))
        wide = [jnp.broadcast_to(energy, (1, LANES)), jnp.zeros((7 - 3 * (both // LANES), LANES), F32)]
        spots_ref[w, :8] = jnp.concatenate(in_rows(nrows) + wide[: 1 + (3 * (both // LANES) < 7)], axis=0)
        spots_ref[w, 8 : 8 + 3 * (both // LANES)] = jnp.concatenate(
            in_rows([pos_ref[c, w : w + 1] for c in range(3)]), axis=0
        )
        weighted = weighted + energy * counts[:, w : w + 1]
    me = lax.axis_index("walkers")
    lanes = lax.broadcasted_iota(jnp.int32, info_ref.shape, 1)
    rows = lax.broadcasted_iota(jnp.int32, info_ref.shape, 0)
    spots_ref[walkers] = jnp.zeros(spots_ref.shape[1:], F32)
    for row, some in enumerate((counts, jas_ref[...], amp_ref[...])):
        spots_ref[walkers, row : row + 1, : some.shape[1]] = some
    number = jnp.sum(counts, axis=1, keepdims=True)
    info_ref[...] = jnp.where(
        lanes == me,
        jnp.where(rows == 0, number, jnp.where(rows == 1, weighted, 0.0)),
        0.0,
    )
    copies = [
        pltpu.make_async_copy(info_ref, info_out, stores.at[0]),
        pltpu.make_async_copy(spots_ref, spots_out, stores.at[1]),
    ]
    for copy in copies:
        copy.start()
    for copy in copies:
        copy.wait()


def shift_kernel(
    pos_ref, dis_ref, order_ref, flags_ref, cen_ref, exp_ref, orb_ref, shift_ref, differ_ref,
):
    _, walkers, both = pos_ref.shape
    nel = both // 2
    moves = flags_ref.shape[2]
    basis = cen_ref.shape[1]
    cols, _ = moves_of(order_ref, flags_ref)
    hots = one_hots(cols, nel)
    rows = [ref[c] for ref in (pos_ref, dis_ref) for c in range(3)]
    rows = jnp.concatenate(rows + [jnp.zeros((-6 * walkers % 8, both), F32)] * (6 * walkers % 8 > 0), axis=0)
    for s in (0, 1):
        points = nt(
            jnp.concatenate([hots[2 * w + s] for w in range(walkers)], axis=0),
            rows[:, s * nel : (s + 1) * nel],
        )
        for w in range(walkers):
            mine = points[w * moves : (w + 1) * moves]
            old = []
            new = []
            for c in range(3):
                at = c * walkers + w
                to = (3 + c) * walkers + w
                spot = mine[:, at : at + 1]
                old.append(jnp.broadcast_to(spot, (moves, LANES)))
                new.append(jnp.broadcast_to(spot + mine[:, to : to + 1], (moves, LANES)))
            for j in range(0, basis, LANES):
                osq = None
                nsq = None
                for c in range(3):
                    row = cen_ref[c : c + 1, j : j + LANES]
                    do = old[c] - row
                    dn = new[c] - row
                    osq = do * do if osq is None else osq + do * do
                    nsq = dn * dn if nsq is None else nsq + dn * dn
                rate = -exp_ref[:, j : j + LANES]
                differ_ref[s, w * moves : (w + 1) * moves, j : j + LANES] = jnp.exp(
                    rate * nsq
                ) - jnp.exp(rate * osq)
    for s in (0, 1):
        shift_ref[s] = product_nt(differ_ref[s], orb_ref[s])


def partial_kernel(
    shift_ref, order_ref, flags_ref, inv_ref, sla_ref, spots_ref, info_ref,
    part_ref, done_ref, pair_ref, odd_ref,
):
    walkers, _, orbs, nel = inv_ref.shape
    moves = flags_ref.shape[2]
    cols, keep = moves_of(order_ref, flags_ref)
    hots = one_hots(cols, nel)
    members = lax.axis_size("orb")
    share = walkers // members
    first = lax.axis_index("orb") * share
    tail = 2 * walkers * moves
    part_ref[tail:, :] = info_ref[...]
    jas = spots_ref[walkers, 1:2, :]
    for w in range(share):
        mine = spots_ref[first + w]
        at = tail + 2 + first + w
        part_ref[pl.ds(at, 1), :] = jnp.broadcast_to(
            jastrow_of(mine, turned(mine), jas, nel), (1, part_ref.shape[1])
        )
    for s in (0, 1):
        for w in range(walkers):
            i = 2 * w + s
            mine = shift_ref[s, w * moves : (w + 1) * moves, :]
            proposed = mine + taken_nt(hots[i], sla_ref[w, s])
            part = product(proposed, inv_ref[w, s])
            part_ref[i * moves : (i + 1) * moves, :] = part * keep[i]
            done_ref[w, s] = sla_ref[w, s] + spread(mine, hots[i] * keep[i])
    half = walkers // 2
    per = 2 * orbs
    tail = half * per
    for pay, indices in sent(spots_ref, walkers, pair_ref, odd_ref):
        for j, (limits, index) in enumerate(indices):
            rows = picked(
                limits,
                index,
                [[done_ref[w, s] for w in range(walkers)] for s in (0, 1)]
                + [[spots_ref[w, :8] for w in range(walkers)]],
            )
            for s in (0, 1):
                pay[j * per + s * orbs : j * per + (s + 1) * orbs, :] = rows[s]
            pay[tail + 8 * j : tail + 8 * j + 8, :] = rows[2]


def add_kernel(mine_ref, other_ref, out_ref):
    out_ref[...] = mine_ref[...] + other_ref[...]


def update_kernel(
    sum_ref, got_ref, inv_ref, order_ref, flags_ref, spots_ref,
    cur_ref, log_ref, info_ref, pair_ref, odd_ref,
):
    walkers, _, orbs, nel = inv_ref.shape
    moves = flags_ref.shape[2]
    count = 2 * walkers
    cols, keep = moves_of(order_ref, flags_ref)
    hots = one_hots(cols, nel)
    eye = (
        lax.broadcasted_iota(jnp.int32, (moves, moves), 0)
        == lax.broadcasted_iota(jnp.int32, (moves, moves), 1)
    ).astype(F32)
    tiles = moves // 8
    left = []
    right = []
    columns = []
    for i in range(count):
        at = slice(i * moves, (i + 1) * moves)
        change = sum_ref[at, :] + got_ref[at, :] - hots[i] * keep[i]
        coupling = taken(change, hots[i]) + eye
        columns.append(taken(inv_ref[i // 2, i % 2], hots[i]))
        left.append([coupling[8 * t : 8 * t + 8] for t in range(tiles)])
        right.append([change[8 * t : 8 * t + 8] for t in range(tiles)])
    info_ref[...] = sum_ref[count * moves :, :] + got_ref[count * moves :, :]
    lanes = lax.broadcasted_iota(jnp.int32, (1, nel), 1)
    sub = lax.broadcasted_iota(jnp.int32, (8, nel), 0)
    pivots = [jnp.ones((1, nel), F32) for _ in range(count)]
    for k in range(0, moves, 2):
        own, line = k // 8, k % 8
        for i in range(count):
            wide = [
                [jnp.broadcast_to(left[i][t][:, c : c + 1], (8, nel)) for t in range(tiles)]
                for c in (k, k + 1)
            ]
            a, b = (wide[c][own][line : line + 1] for c in (0, 1))
            c, d = (wide[c][own][line + 1 : line + 2] for c in (0, 1))
            det = a * d - b * c
            pivots[i] = jnp.where(lanes == k, det, pivots[i])
            scale = 1.0 / det
            new = []
            for side, width in ((left, moves), (right, nel)):
                upper = side[i][own][line : line + 1]
                lower = side[i][own][line + 1 : line + 2]
                new.append(
                    (
                        (d[:, :width] * upper - b[:, :width] * lower) * scale[:, :width],
                        (a[:, :width] * lower - c[:, :width] * upper) * scale[:, :width],
                    )
                )
            for t in range(tiles):
                for side, width, (upper, lower) in ((left, moves, new[0]), (right, nel, new[1])):
                    tile = (
                        side[i][t] - wide[0][t][:, :width] * upper - wide[1][t][:, :width] * lower
                    )
                    if t == own:
                        tile = jnp.where(
                            sub[:, :width] == line,
                            upper,
                            jnp.where(sub[:, :width] == line + 1, lower, tile),
                        )
                    side[i][t] = tile
    for i in range(count):
        solved = jnp.concatenate(right[i], axis=0)
        cur_ref[i // 2, i % 2] = inv_ref[i // 2, i % 2] - product(columns[i], solved)
    log_ref[...] = jnp.zeros(log_ref.shape, F32)
    for w in range(walkers):
        both = jnp.log(jnp.abs(pivots[2 * w])) + jnp.log(jnp.abs(pivots[2 * w + 1]))
        log_ref[w : w + 1, :] = (
            jnp.broadcast_to(jnp.sum(both, axis=1, keepdims=True), (1, nel))
            + info_ref[2 + w : 3 + w, :nel]
            + spots_ref[walkers, 2:3, w : w + 1]
        )
    half = walkers // 2
    per = 2 * orbs
    tail = half * per
    for pay, indices in sent(spots_ref, walkers, pair_ref, odd_ref):
        pay[tail : tail + INFO, :] = info_ref[...]
        pay[tail + INFO :, :] = jnp.zeros((pay.shape[0] - tail - INFO, LANES), F32)
        for j, (limits, index) in enumerate(indices):
            rows = picked(
                limits,
                index,
                [[cur_ref[w, s] for w in range(walkers)] for s in (0, 1)]
                + [[log_ref[w : w + 1, :] for w in range(walkers)]],
            )
            for s in (0, 1):
                pay[j * per + s * orbs : j * per + (s + 1) * orbs, :] = rows[s]
            pay[tail + INFO + j : tail + INFO + j + 1, :] = rows[2]


def place_kernel(
    cur_ref, done_ref, spots_ref, log_ref, info_ref,
    pair_s_ref, odd_s_ref, pair_i_ref, odd_i_ref,
    inv_out, sla_out, pos_out, log_out, energy_out, mean_out,
):
    walkers, _, orbs, nel = cur_ref.shape
    width = pos_out.shape[2] // LANES
    half = walkers // 2
    per = 2 * orbs
    tail = half * per
    me = lax.axis_index("walkers")
    parity = lax.rem(me, 2)
    info = info_ref[...] + pair_i_ref[tail : tail + INFO, :]
    lanes = lax.broadcasted_iota(jnp.int32, (1, info.shape[1]), 1)
    before = jnp.sum(jnp.where(lanes < me, info[0:1], 0.0), axis=1, keepdims=True)
    groups = lax.axis_size("walkers")
    mean = jnp.sum(info[1:2], axis=1, keepdims=True)
    mean_out[...] = mean / (1.0 * walkers * groups)
    limits = limits_of(spots_ref, walkers)
    slots = lax.broadcasted_iota(jnp.int32, (1, walkers), 1)
    here = [[cur_ref[w, s] for w in range(walkers)] for s in (0, 1)]
    here += [[done_ref[w, s] for w in range(walkers)] for s in (0, 1)]
    here += [[spots_ref[w, :8] for w in range(walkers)]]
    here += [[log_ref[w : w + 1, :] for w in range(walkers)]]
    odd = parity.astype(F32)
    log_new = jnp.zeros((1, walkers), F32)
    energy_new = jnp.zeros((1, walkers), F32)
    for j in range(walkers):
        index = (1.0 * walkers) * me.astype(F32) + 1.0 * j - before
        own = picked(limits, index, here)
        low = j < half
        outside = -index if low else index - limits[-1] + 1.0
        entry = index + 1.0 * half if low else index - limits[-1]
        on_pair = odd if low else 1.0 - odd
        shape_here = (orbs, nel)
        away = jnp.broadcast_to(outside, shape_here) > 0.0
        second = jnp.broadcast_to(entry, shape_here) > 0.5
        pair = jnp.broadcast_to(on_pair, shape_here) > 0.5

        def one(late, at, rows):
            parts = []
            for i in range(half):
                start = at(i)
                a, b = (ref[start : start + rows, :] for ref in late)
                parts.append(jnp.where(pair[:rows], a, b))
            value = parts[0]
            for i in range(1, half):
                again = second if i == 1 else jnp.broadcast_to(entry, shape_here) > i - 0.5
                value = jnp.where(again[:rows], parts[i], value)
            return value

        inverses = (pair_i_ref, odd_i_ref)
        slaters = (pair_s_ref, odd_s_ref)
        got = [one(inverses, lambda i, s=s: i * per + s * orbs, orbs) for s in (0, 1)]
        got += [one(slaters, lambda i, s=s: i * per + s * orbs, orbs) for s in (0, 1)]
        got += [one(slaters, lambda i: tail + 8 * i, 8)]
        got += [one(inverses, lambda i: tail + INFO + i, 1)]
        new = [jnp.where(away[: o.shape[0]], g, o) for o, g in zip(own, got)]
        for s in (0, 1):
            inv_out[j, s] = new[s]
            sla_out[j, s] = new[2 + s]
        for c in range(3):
            for h in range(width):
                pos_out[c, j : j + 1, h * LANES : (h + 1) * LANES] = new[4][
                    3 * h + c : 3 * h + c + 1
                ]
        log_new = jnp.where(slots == j, new[5][:, :walkers], log_new)
        energy_new = jnp.where(
            slots == j, new[4][3 * width : 3 * width + 1, :walkers], energy_new
        )
    log_out[...] = log_new
    energy_out[...] = energy_new


def call(kernel, outs, in_specs, scratch=(), us=1.0, name=None, out_specs=None, vmem=32 * 2**20):
    return pl.pallas_call(
        kernel,
        out_shape=outs,
        in_specs=in_specs,
        out_specs=out_specs or jax.tree.map(lambda _: VMEM, outs),
        scratch_shapes=list(scratch),
        compiler_params=pltpu.CompilerParams(vmem_limit_bytes=vmem),
        cost_estimate=pl.CostEstimate(flops=int(us * 1.1e9), bytes_accessed=2**18, transcendentals=0),
        name=name,
    )


def shape(*dims):
    return jax.ShapeDtypeStruct(dims, F32)


def body(
    inverse, slater, positions, displacements, move_order, accepted, counts, log_amp, centers,
    exponents, orbitals, jastrow,
):
    walkers, _, orbs, nel = inverse.shape
    moves = accepted.shape[2]
    both = positions.shape[2]
    basis = centers.shape[1]
    groups = lax.axis_size("walkers")
    members = lax.axis_size("orb")
    wide = max(LANES, groups)
    half = walkers // 2
    per = 2 * orbs
    count = 2 * walkers
    tall = half * per + 16

    counts = counts.reshape(1, walkers)
    log_amp = log_amp.reshape(1, walkers)
    jastrow = jastrow.reshape(1, jastrow.shape[0])

    pairs = [(i, i ^ 1) for i in range(groups)]
    odds = [(i, i + 1) for i in range(1, groups - 1, 2)]
    odds = odds + [(b, a) for a, b in odds]

    places = positions.transpose(1, 0, 2)
    steps = displacements.transpose(1, 0, 2)
    operands = (places, steps, move_order, accepted, counts, jastrow, log_amp)
    made = (shape(walkers + 1, 16, LANES), shape(INFO, wide))
    spots, info = call(
        energy_kernel,
        made,
        [ANY] * len(operands),
        out_specs=(ANY, ANY),
        scratch=[pltpu.VMEM(x.shape, x.dtype) for x in operands + made]
        + [pltpu.SemaphoreType.DMA((len(operands),)), pltpu.SemaphoreType.DMA((len(made),))],
        us=2,
        vmem=61 * 2**20,
        name="energy",
    )(*operands)

    hops = members * 2
    step = hops
    while step < groups:
        info = info + lax.ppermute(info, "walkers", [(i, i ^ step) for i in range(groups)])
        step *= 2
    joint = [
        (d * members + o, (d ^ (2 * hop)) * members + o)
        for o in range(members)
        for hop in [(1, 3, 0, 2)[o] if members == 4 else o]
        for d in range(groups)
        if 2 * hop < groups
    ]
    info = lax.ppermute(info, ("walkers", "orb"), joint)

    shift = call(
        shift_kernel,
        shape(2, walkers * moves, orbs),
        [VMEM] * 7,
        scratch=[pltpu.VMEM((2, walkers * moves, basis), F32)],
        us=3,
        name="shift",
    )(
        places, steps, move_order, accepted, centers, exponents.reshape(1, basis), orbitals,
    )

    part, done, pair_s, odd_s = call(
        partial_kernel,
        (
            shape(count * moves + INFO, nel),
            shape(walkers, 2, orbs, nel),
            shape(tall, LANES),
            shape(tall, LANES),
        ),
        [VMEM] * 7,
        us=2,
        name="partial",
    )(shift, move_order, accepted, inverse, slater, spots, info)

    total = part
    got = jnp.zeros_like(part)
    step = 1
    while step < members:
        partner = [(o, o ^ step) for o in range(members)]
        got = lax.ppermute(total, "orb", partner)
        if 2 * step < members:
            total = call(
                add_kernel,
                shape(count * moves + INFO, nel),
                [VMEM] * 2,
                us=0.5,
                name="add",
            )(total, got)
        step *= 2

    pair_s = lax.ppermute(pair_s, "walkers", pairs)
    odd_s = lax.ppermute(odd_s, "walkers", odds)

    current, logs, info, pair_i, odd_i = call(
        update_kernel,
        (
            shape(walkers, 2, orbs, nel),
            shape(8, nel),
            shape(INFO, wide),
            shape(tall, LANES),
            shape(tall, LANES),
        ),
        [VMEM] * 6,
        us=4,
        name="update",
    )(total, got, inverse, move_order, accepted, spots)

    pair_i = lax.ppermute(pair_i, "walkers", pairs)
    odd_i = lax.ppermute(odd_i, "walkers", odds)

    inv_new, sla_new, pos_new, log_new, energy_new, mean = call(
        place_kernel,
        (
            shape(walkers, 2, orbs, nel),
            shape(walkers, 2, orbs, nel),
            shape(3, walkers, both),
            shape(1, walkers),
            shape(1, walkers),
            shape(1, 1),
        ),
        [VMEM] * 9,
        us=1.5,
        name="place",
    )(current, done, spots, logs, info, pair_s, odd_s, pair_i, odd_i)
    return (
        inv_new,
        sla_new,
        pos_new.transpose(1, 0, 2),
        log_new.reshape(walkers),
        energy_new.reshape(walkers),
        mean.reshape(()),
    )


def solution(mesh):
    return jax.shard_map(
        body,
        mesh=mesh,
        in_specs=(
            P("walkers", None, "orb", None),
            P("walkers", None, "orb", None),
            P("walkers", None, None),
            P("walkers", None, None),
            P("walkers", None, None),
            P("walkers", None, None),
            P("walkers"),
            P("walkers"),
            P(),
            P(),
            P(None, "orb", None),
            P(),
        ),
        out_specs=(
            P("walkers", None, "orb", None),
            P("walkers", None, "orb", None),
            P("walkers", None, None),
            P("walkers"),
            P("walkers"),
            P(),
        ),
        check_vma=False,
    )
```

```python
import jax
import jax.numpy as jnp
from jax import lax
from jax.experimental import pallas as pl
from jax.experimental.pallas import tpu as pltpu
from jax.sharding import PartitionSpec as P

F32 = jnp.float32
BF16 = jnp.bfloat16
highest = lax.Precision.HIGHEST
VMEM = pl.BlockSpec(memory_space=pltpu.VMEM)
ANY = pl.BlockSpec(memory_space=pl.ANY)
LANES = 128
INFO = 8


def nt(a, b):
    return lax.dot_general(
        a, b, (((1,), (1,)), ((), ())), precision=highest, preferred_element_type=F32
    )


def thirds(x):
    high = x.astype(BF16)
    rest = x - high.astype(F32)
    middle = rest.astype(BF16)
    low = (rest - middle.astype(F32)).astype(BF16)
    return jnp.concatenate([high, middle, low], axis=0)


def parted(x):
    high = x.astype(BF16)
    return jnp.concatenate([high, (x - high.astype(F32)).astype(BF16)], axis=0)


def product(a, b):
    rows = a.shape[0]
    inner = b.shape[0]
    left = parted(a)
    right = parted(b)
    whole = None
    for part in (right[:inner], right[inner:]):
        both = lax.dot_general(
            left, part, (((1,), (0,)), ((), ())), preferred_element_type=F32
        )
        both = both[:rows] + both[rows:]
        whole = both if whole is None else whole + both
    return whole


def product_nt(a, b):
    rows, cols = a.shape[0], b.shape[0]
    both = lax.dot_general(
        parted(a), parted(b), (((1,), (1,)), ((), ())), preferred_element_type=F32
    )
    both = both[:rows] + both[rows:]
    return both[:, :cols] + both[:, cols:]


def taken_nt(hot, x):
    rows = x.shape[0]
    parts = lax.dot_general(
        hot.astype(BF16), thirds(x), (((1,), (1,)), ((), ())), preferred_element_type=F32
    )
    return parts[:, :rows] + parts[:, rows : 2 * rows] + parts[:, 2 * rows :]


def spread(x, hot):
    hot = hot.astype(BF16)
    return lax.dot_general(
        thirds(x),
        jnp.concatenate([hot] * 3, axis=0),
        (((0,), (0,)), ((), ())),
        preferred_element_type=F32,
    )


def taken(x, hot):
    rows = x.shape[0]
    parts = lax.dot_general(
        thirds(x), hot.astype(BF16), (((1,), (1,)), ((), ())), preferred_element_type=F32
    )
    return parts[:rows] + parts[rows : 2 * rows] + parts[2 * rows :]


def turned(rows):
    short = -rows.shape[0] % 8
    if short:
        rows = jnp.concatenate([rows, jnp.zeros((short, rows.shape[1]), F32)], axis=0)
    return jnp.transpose(rows)


def moves_of(order_ref, flags_ref):
    walkers, _, moves = flags_ref.shape
    nel = order_ref.shape[2]
    order = turned(
        jnp.concatenate([order_ref[w] for w in range(walkers)], axis=0).astype(F32)
    )
    flags = jnp.concatenate([flags_ref[w] for w in range(walkers)], axis=0).astype(F32)
    flags = turned(
        jnp.concatenate([flags, jnp.zeros((2 * walkers, nel - moves), F32)], axis=1)
    )
    cols = [order[:moves, i : i + 1] for i in range(2 * walkers)]
    keep = [flags[:moves, i : i + 1] for i in range(2 * walkers)]
    return cols, keep


def one_hots(cols, nel):
    moves = cols[0].shape[0]
    lanes = lax.broadcasted_iota(jnp.int32, (moves, nel), 1).astype(F32)
    return [(c == lanes).astype(F32) for c in cols]


def limits_of(spots_ref, walkers):
    counts = spots_ref[walkers, 0:1, :]
    limits = [counts[:, :1]]
    for w in range(1, walkers):
        limits.append(limits[-1] + counts[:, w : w + 1])
    return limits


def picked(limits, index, choices):
    rows = max(x[0].shape[0] for x in choices)
    after = [
        jnp.broadcast_to(limit - index, (rows, choices[0][0].shape[1])) <= 0.0
        for limit in limits[:-1]
    ]
    out = []
    for some in choices:
        value = some[0]
        for w in range(1, len(some)):
            value = jnp.where(after[w - 1][: value.shape[0]], some[w], value)
        out.append(value)
    return out


def sent(spots_ref, walkers, pair_ref, odd_ref):
    half = walkers // 2
    limits = limits_of(spots_ref, walkers)
    parity = lax.rem(lax.axis_index("walkers"), 2)
    out = []
    for pay, up in ((pair_ref, parity == 0), (odd_ref, parity == 1)):
        up = up.astype(F32)
        out.append(
            (pay, [(limits, up * (limits[-1] - 1.0 * half) + 1.0 * j) for j in range(half)])
        )
    return out


def pair_tiles(turns, rows, nel, kinds):
    sums = [None, None]
    for h in (0, 1):
        for t in range(nel // 8):
            wide = [
                [
                    jnp.broadcast_to(turn[h][c][8 * t : 8 * t + 8], (8, nel))
                    for c in range(3)
                ]
                for turn in turns
            ]
            for g in range(h, 2):
                squares = []
                for i, row in enumerate(rows):
                    total = None
                    for c in range(3):
                        offset = wide[i][c] - row[g][c]
                        total = offset * offset if total is None else total + offset * offset
                    squares.append(total)
                kind = int(g != h)
                term = kinds[kind](*squares)
                sums[kind] = term if sums[kind] is None else sums[kind] + term
    return sums


def summed(tile):
    return jnp.sum(jnp.sum(tile, axis=0, keepdims=True), axis=1, keepdims=True)


def jastrow_of(spots, turn, jas, nel):
    rows, turns = (
        [
            [
                [cut(base + 3 * h + c) for c in range(3)]
                for h in (0, 1)
            ]
            for base in (0, 8)
        ]
        for cut in (lambda r: spots[r : r + 1], lambda r: turn[:, r : r + 1])
    )

    def change(fall):
        fall = jnp.broadcast_to(fall, (8, nel))

        def term(new, old):
            nd = jnp.sqrt(new)
            od = jnp.sqrt(old)
            return (nd - od) / ((1.0 + fall * nd) * (1.0 + fall * od))

        return term

    same, other = pair_tiles(turns, rows, nel, [change(jas[:, 2:3]), change(jas[:, 3:4])])
    return summed(same * (0.5 * jas[:, :1]) + other * jas[:, 1:2])


def in_rows(rows):
    return [r[:, at : at + LANES] for at in range(0, rows[0].shape[1], LANES) for r in rows]


def energy_kernel(
    pos_in, dis_in, order_in, flags_in, counts_in, jas_in, amp_in, spots_out, info_out,
    pos_ref, dis_ref, order_ref, flags_ref, counts_ref, jas_ref, amp_ref, spots_ref, info_ref,
    loads, stores,
):
    operands = (
        (pos_in, pos_ref),
        (dis_in, dis_ref),
        (order_in, order_ref),
        (flags_in, flags_ref),
        (counts_in, counts_ref),
        (jas_in, jas_ref),
        (amp_in, amp_ref),
    )
    copies = [pltpu.make_async_copy(a, b, loads.at[i]) for i, (a, b) in enumerate(operands)]
    for copy in copies:
        copy.start()
    for copy in copies:
        copy.wait()
    _, walkers, both = pos_ref.shape
    nel = both // 2
    cols, keep = moves_of(order_ref, flags_ref)
    hots = one_hots(cols, nel)
    applied = jnp.concatenate(
        [
            jnp.concatenate(
                [
                    jnp.sum(hots[2 * w + s] * keep[2 * w + s], axis=0, keepdims=True)
                    for s in (0, 1)
                ],
                axis=1,
            )
            for w in range(walkers)
        ],
        axis=0,
    )
    now = [pos_ref[c] + dis_ref[c] * applied for c in range(3)]
    turn = turned(jnp.concatenate(now, axis=0))
    weighted = jnp.zeros((1, nel), F32)
    counts = counts_ref[...].astype(F32)
    for w in range(walkers):
        nrows = [now[c][w : w + 1] for c in range(3)]
        halves = [[r[:, h * nel : (h + 1) * nel] for r in nrows] for h in (0, 1)]
        tall = [
            [
                turn[h * nel : (h + 1) * nel, c * walkers + w : c * walkers + w + 1]
                for c in range(3)
            ]
            for h in (0, 1)
        ]
        same, other = pair_tiles([tall], [halves], nel, [lambda q: lax.rsqrt(q + 1.0)] * 2)
        soft = jnp.sum(same + 2.0 * other, axis=0, keepdims=True)
        wide = [soft, jnp.zeros((7 - 3 * (both // LANES), LANES), F32)]
        spots_ref[w, :8] = jnp.concatenate(in_rows(nrows) + wide[: 1 + (3 * (both // LANES) < 7)], axis=0)
        spots_ref[w, 8 : 8 + 3 * (both // LANES)] = jnp.concatenate(
            in_rows([pos_ref[c, w : w + 1] for c in range(3)]), axis=0
        )
        weighted = weighted + soft * counts[:, w : w + 1]
    me = lax.axis_index("walkers")
    lanes = lax.broadcasted_iota(jnp.int32, info_ref.shape, 1)
    rows = lax.broadcasted_iota(jnp.int32, info_ref.shape, 0)
    spots_ref[walkers] = jnp.zeros(spots_ref.shape[1:], F32)
    for row, some in enumerate((counts, jas_ref[...], amp_ref[...])):
        spots_ref[walkers, row : row + 1, : some.shape[1]] = some
    number = jnp.sum(counts, axis=1, keepdims=True)
    info_ref[...] = jnp.where((lanes == me) & (rows == 0), number, 0.0)
    info_ref[1:2, :nel] = weighted
    copies = [
        pltpu.make_async_copy(info_ref, info_out, stores.at[0]),
        pltpu.make_async_copy(spots_ref, spots_out, stores.at[1]),
    ]
    for copy in copies:
        copy.start()
    for copy in copies:
        copy.wait()


def shift_kernel(
    pos_ref, dis_ref, order_ref, flags_ref, cen_ref, exp_ref, orb_ref, shift_ref, differ_ref,
):
    _, walkers, both = pos_ref.shape
    nel = both // 2
    moves = flags_ref.shape[2]
    basis = cen_ref.shape[1]
    cols, _ = moves_of(order_ref, flags_ref)
    hots = one_hots(cols, nel)
    rows = [ref[c] for ref in (pos_ref, dis_ref) for c in range(3)]
    rows = jnp.concatenate(rows + [jnp.zeros((-6 * walkers % 8, both), F32)] * (6 * walkers % 8 > 0), axis=0)
    for s in (0, 1):
        points = nt(
            jnp.concatenate([hots[2 * w + s] for w in range(walkers)], axis=0),
            rows[:, s * nel : (s + 1) * nel],
        )
        for w in range(walkers):
            mine = points[w * moves : (w + 1) * moves]
            old = []
            new = []
            for c in range(3):
                at = c * walkers + w
                to = (3 + c) * walkers + w
                spot = mine[:, at : at + 1]
                old.append(jnp.broadcast_to(spot, (moves, LANES)))
                new.append(jnp.broadcast_to(spot + mine[:, to : to + 1], (moves, LANES)))
            for j in range(0, basis, LANES):
                osq = None
                nsq = None
                for c in range(3):
                    row = cen_ref[c : c + 1, j : j + LANES]
                    do = old[c] - row
                    dn = new[c] - row
                    osq = do * do if osq is None else osq + do * do
                    nsq = dn * dn if nsq is None else nsq + dn * dn
                rate = -exp_ref[:, j : j + LANES]
                differ_ref[s, w * moves : (w + 1) * moves, j : j + LANES] = jnp.exp(
                    rate * nsq
                ) - jnp.exp(rate * osq)
    for s in (0, 1):
        shift_ref[s] = product_nt(differ_ref[s], orb_ref[s])


def partial_kernel(
    shift_ref, order_ref, flags_ref, inv_ref, sla_ref, spots_ref, info_ref,
    part_ref, done_ref, pair_ref, odd_ref,
):
    walkers, _, orbs, nel = inv_ref.shape
    moves = flags_ref.shape[2]
    cols, keep = moves_of(order_ref, flags_ref)
    hots = one_hots(cols, nel)
    members = lax.axis_size("orb")
    share = walkers // members
    first = lax.axis_index("orb") * share
    tail = 2 * walkers * moves
    part_ref[tail:, :] = info_ref[...]
    jas = spots_ref[walkers, 1:2, :]
    for w in range(share):
        mine = spots_ref[first + w]
        at = tail + 2 + first + w
        part_ref[pl.ds(at, 1), :] = jnp.broadcast_to(
            jastrow_of(mine, turned(mine), jas, nel), (1, part_ref.shape[1])
        )
    for s in (0, 1):
        for w in range(walkers):
            i = 2 * w + s
            mine = shift_ref[s, w * moves : (w + 1) * moves, :]
            proposed = mine + taken_nt(hots[i], sla_ref[w, s])
            part = product(proposed, inv_ref[w, s])
            part_ref[i * moves : (i + 1) * moves, :] = part * keep[i]
            done_ref[w, s] = sla_ref[w, s] + spread(mine, hots[i] * keep[i])
    half = walkers // 2
    per = 2 * orbs
    tail = half * per
    for pay, indices in sent(spots_ref, walkers, pair_ref, odd_ref):
        for j, (limits, index) in enumerate(indices):
            rows = picked(
                limits,
                index,
                [[done_ref[w, s] for w in range(walkers)] for s in (0, 1)]
                + [[spots_ref[w, :8] for w in range(walkers)]],
            )
            for s in (0, 1):
                pay[j * per + s * orbs : j * per + (s + 1) * orbs, :] = rows[s]
            pay[tail + 8 * j : tail + 8 * j + 8, :] = rows[2]


def add_kernel(mine_ref, other_ref, out_ref):
    out_ref[...] = mine_ref[...] + other_ref[...]


def update_kernel(
    sum_ref, got_ref, inv_ref, order_ref, flags_ref, spots_ref,
    cur_ref, log_ref, info_ref, pair_ref, odd_ref,
):
    walkers, _, orbs, nel = inv_ref.shape
    moves = flags_ref.shape[2]
    count = 2 * walkers
    cols, keep = moves_of(order_ref, flags_ref)
    hots = one_hots(cols, nel)
    eye = (
        lax.broadcasted_iota(jnp.int32, (moves, moves), 0)
        == lax.broadcasted_iota(jnp.int32, (moves, moves), 1)
    ).astype(F32)
    tiles = moves // 8
    left = []
    right = []
    columns = []
    for i in range(count):
        at = slice(i * moves, (i + 1) * moves)
        change = sum_ref[at, :] + got_ref[at, :] - hots[i] * keep[i]
        coupling = taken(change, hots[i]) + eye
        columns.append(taken(inv_ref[i // 2, i % 2], hots[i]))
        left.append([coupling[8 * t : 8 * t + 8] for t in range(tiles)])
        right.append([change[8 * t : 8 * t + 8] for t in range(tiles)])
    info_ref[...] = sum_ref[count * moves :, :] + got_ref[count * moves :, :]
    lanes = lax.broadcasted_iota(jnp.int32, (1, nel), 1)
    sub = lax.broadcasted_iota(jnp.int32, (8, nel), 0)
    pivots = [jnp.ones((1, nel), F32) for _ in range(count)]
    for k in range(0, moves, 2):
        own, line = k // 8, k % 8
        for i in range(count):
            wide = [
                [jnp.broadcast_to(left[i][t][:, c : c + 1], (8, nel)) for t in range(tiles)]
                for c in (k, k + 1)
            ]
            a, b = (wide[c][own][line : line + 1] for c in (0, 1))
            c, d = (wide[c][own][line + 1 : line + 2] for c in (0, 1))
            det = a * d - b * c
            pivots[i] = jnp.where(lanes == k, det, pivots[i])
            scale = 1.0 / det
            new = []
            for side, width in ((left, moves), (right, nel)):
                upper = side[i][own][line : line + 1]
                lower = side[i][own][line + 1 : line + 2]
                new.append(
                    (
                        (d[:, :width] * upper - b[:, :width] * lower) * scale[:, :width],
                        (a[:, :width] * lower - c[:, :width] * upper) * scale[:, :width],
                    )
                )
            for t in range(tiles):
                for side, width, (upper, lower) in ((left, moves, new[0]), (right, nel, new[1])):
                    tile = (
                        side[i][t] - wide[0][t][:, :width] * upper - wide[1][t][:, :width] * lower
                    )
                    if t == own:
                        tile = jnp.where(
                            sub[:, :width] == line,
                            upper,
                            jnp.where(sub[:, :width] == line + 1, lower, tile),
                        )
                    side[i][t] = tile
    for i in range(count):
        solved = jnp.concatenate(right[i], axis=0)
        cur_ref[i // 2, i % 2] = inv_ref[i // 2, i % 2] - product(columns[i], solved)
    log_ref[...] = jnp.zeros(log_ref.shape, F32)
    for w in range(walkers):
        both = jnp.log(jnp.abs(pivots[2 * w])) + jnp.log(jnp.abs(pivots[2 * w + 1]))
        log_ref[w : w + 1, :] = (
            jnp.broadcast_to(jnp.sum(both, axis=1, keepdims=True), (1, nel))
            + info_ref[2 + w : 3 + w, :nel]
            + spots_ref[walkers, 2:3, w : w + 1]
        )
    half = walkers // 2
    per = 2 * orbs
    tail = half * per
    for pay, indices in sent(spots_ref, walkers, pair_ref, odd_ref):
        pay[tail : tail + INFO, :] = info_ref[...]
        pay[tail + INFO :, :] = jnp.zeros((pay.shape[0] - tail - INFO, LANES), F32)
        for j, (limits, index) in enumerate(indices):
            rows = picked(
                limits,
                index,
                [[cur_ref[w, s] for w in range(walkers)] for s in (0, 1)]
                + [[log_ref[w : w + 1, :] for w in range(walkers)]],
            )
            for s in (0, 1):
                pay[j * per + s * orbs : j * per + (s + 1) * orbs, :] = rows[s]
            pay[tail + INFO + j : tail + INFO + j + 1, :] = rows[2]


def place_kernel(
    cur_ref, done_ref, spots_ref, log_ref, info_ref,
    pair_s_ref, odd_s_ref, pair_i_ref, odd_i_ref,
    inv_out, sla_out, pos_out, log_out, energy_out, mean_out,
):
    walkers, _, orbs, nel = cur_ref.shape
    width = pos_out.shape[2] // LANES
    half = walkers // 2
    per = 2 * orbs
    tail = half * per
    me = lax.axis_index("walkers")
    parity = lax.rem(me, 2)
    info = info_ref[...] + pair_i_ref[tail : tail + INFO, :]
    lanes = lax.broadcasted_iota(jnp.int32, (1, info.shape[1]), 1)
    before = jnp.sum(jnp.where(lanes < me, info[0:1], 0.0), axis=1, keepdims=True)
    groups = lax.axis_size("walkers")
    both = pos_out.shape[2]

    def energy_of(row, copies):
        soft = jnp.sum(row, axis=1, keepdims=True)
        return (soft - 1.0 * both * copies) / (1.0 * both * (both - 1))

    copies = jnp.sum(info[0:1], axis=1, keepdims=True)
    mean_out[...] = energy_of(info[1:2], copies) / (1.0 * walkers * groups)
    limits = limits_of(spots_ref, walkers)
    slots = lax.broadcasted_iota(jnp.int32, (1, walkers), 1)
    here = [[cur_ref[w, s] for w in range(walkers)] for s in (0, 1)]
    here += [[done_ref[w, s] for w in range(walkers)] for s in (0, 1)]
    here += [[spots_ref[w, :8] for w in range(walkers)]]
    here += [[log_ref[w : w + 1, :] for w in range(walkers)]]
    odd = parity.astype(F32)
    log_new = jnp.zeros((1, walkers), F32)
    energy_new = jnp.zeros((1, walkers), F32)
    for j in range(walkers):
        index = (1.0 * walkers) * me.astype(F32) + 1.0 * j - before
        own = picked(limits, index, here)
        low = j < half
        outside = -index if low else index - limits[-1] + 1.0
        entry = index + 1.0 * half if low else index - limits[-1]
        on_pair = odd if low else 1.0 - odd
        shape_here = (orbs, nel)
        away = jnp.broadcast_to(outside, shape_here) > 0.0
        second = jnp.broadcast_to(entry, shape_here) > 0.5
        pair = jnp.broadcast_to(on_pair, shape_here) > 0.5

        def one(late, at, rows):
            parts = []
            for i in range(half):
                start = at(i)
                a, b = (ref[start : start + rows, :] for ref in late)
                parts.append(jnp.where(pair[:rows], a, b))
            value = parts[0]
            for i in range(1, half):
                again = second if i == 1 else jnp.broadcast_to(entry, shape_here) > i - 0.5
                value = jnp.where(again[:rows], parts[i], value)
            return value

        inverses = (pair_i_ref, odd_i_ref)
        slaters = (pair_s_ref, odd_s_ref)
        got = [one(inverses, lambda i, s=s: i * per + s * orbs, orbs) for s in (0, 1)]
        got += [one(slaters, lambda i, s=s: i * per + s * orbs, orbs) for s in (0, 1)]
        got += [one(slaters, lambda i: tail + 8 * i, 8)]
        got += [one(inverses, lambda i: tail + INFO + i, 1)]
        new = [jnp.where(away[: o.shape[0]], g, o) for o, g in zip(own, got)]
        for s in (0, 1):
            inv_out[j, s] = new[s]
            sla_out[j, s] = new[2 + s]
        for c in range(3):
            for h in range(width):
                pos_out[c, j : j + 1, h * LANES : (h + 1) * LANES] = new[4][
                    3 * h + c : 3 * h + c + 1
                ]
        log_new = jnp.where(slots == j, new[5][:, :walkers], log_new)
        energy_new = jnp.where(
            slots == j, energy_of(new[4][3 * width : 3 * width + 1], 1.0), energy_new
        )
    log_out[...] = log_new
    energy_out[...] = energy_new


def call(kernel, outs, in_specs, scratch=(), us=1.0, name=None, out_specs=None, vmem=32 * 2**20):
    return pl.pallas_call(
        kernel,
        out_shape=outs,
        in_specs=in_specs,
        out_specs=out_specs or jax.tree.map(lambda _: VMEM, outs),
        scratch_shapes=list(scratch),
        compiler_params=pltpu.CompilerParams(vmem_limit_bytes=vmem),
        cost_estimate=pl.CostEstimate(flops=int(us * 1.1e9), bytes_accessed=2**18, transcendentals=0),
        name=name,
    )


def shape(*dims):
    return jax.ShapeDtypeStruct(dims, F32)


def body(
    inverse, slater, positions, displacements, move_order, accepted, counts, log_amp, centers,
    exponents, orbitals, jastrow,
):
    walkers, _, orbs, nel = inverse.shape
    moves = accepted.shape[2]
    both = positions.shape[2]
    basis = centers.shape[1]
    groups = lax.axis_size("walkers")
    members = lax.axis_size("orb")
    wide = max(LANES, groups)
    half = walkers // 2
    per = 2 * orbs
    count = 2 * walkers
    tall = half * per + 16

    counts = counts.reshape(1, walkers)
    log_amp = log_amp.reshape(1, walkers)
    jastrow = jastrow.reshape(1, jastrow.shape[0])

    pairs = [(i, i ^ 1) for i in range(groups)]
    odds = [(i, i + 1) for i in range(1, groups - 1, 2)]
    odds = odds + [(b, a) for a, b in odds]

    places = positions.transpose(1, 0, 2)
    steps = displacements.transpose(1, 0, 2)
    operands = (places, steps, move_order, accepted, counts, jastrow, log_amp)
    made = (shape(walkers + 1, 16, LANES), shape(INFO, wide))
    spots, info = call(
        energy_kernel,
        made,
        [ANY] * len(operands),
        out_specs=(ANY, ANY),
        scratch=[pltpu.VMEM(x.shape, x.dtype) for x in operands + made]
        + [pltpu.SemaphoreType.DMA((len(operands),)), pltpu.SemaphoreType.DMA((len(made),))],
        us=2,
        vmem=61 * 2**20,
        name="energy",
    )(*operands)

    hops = members * 2
    step = hops
    while step < groups:
        info = info + lax.ppermute(info, "walkers", [(i, i ^ step) for i in range(groups)])
        step *= 2
    joint = [
        (d * members + o, (d ^ (2 * hop)) * members + o)
        for o in range(members)
        for hop in [(1, 3, 0, 2)[o] if members == 4 else o]
        for d in range(groups)
        if 2 * hop < groups
    ]
    info = lax.ppermute(info, ("walkers", "orb"), joint)

    shift = call(
        shift_kernel,
        shape(2, walkers * moves, orbs),
        [VMEM] * 7,
        scratch=[pltpu.VMEM((2, walkers * moves, basis), F32)],
        us=3,
        name="shift",
    )(
        places, steps, move_order, accepted, centers, exponents.reshape(1, basis), orbitals,
    )

    part, done, pair_s, odd_s = call(
        partial_kernel,
        (
            shape(count * moves + INFO, nel),
            shape(walkers, 2, orbs, nel),
            shape(tall, LANES),
            shape(tall, LANES),
        ),
        [VMEM] * 7,
        us=2,
        name="partial",
    )(shift, move_order, accepted, inverse, slater, spots, info)

    total = part
    got = jnp.zeros_like(part)
    step = 1
    while step < members:
        partner = [(o, o ^ step) for o in range(members)]
        got = lax.ppermute(total, "orb", partner)
        if 2 * step < members:
            total = call(
                add_kernel,
                shape(count * moves + INFO, nel),
                [VMEM] * 2,
                us=0.5,
                name="add",
            )(total, got)
        step *= 2

    pair_s = lax.ppermute(pair_s, "walkers", pairs)
    odd_s = lax.ppermute(odd_s, "walkers", odds)

    current, logs, info, pair_i, odd_i = call(
        update_kernel,
        (
            shape(walkers, 2, orbs, nel),
            shape(8, nel),
            shape(INFO, wide),
            shape(tall, LANES),
            shape(tall, LANES),
        ),
        [VMEM] * 6,
        us=4,
        name="update",
    )(total, got, inverse, move_order, accepted, spots)

    pair_i = lax.ppermute(pair_i, "walkers", pairs)
    odd_i = lax.ppermute(odd_i, "walkers", odds)

    inv_new, sla_new, pos_new, log_new, energy_new, mean = call(
        place_kernel,
        (
            shape(walkers, 2, orbs, nel),
            shape(walkers, 2, orbs, nel),
            shape(3, walkers, both),
            shape(1, walkers),
            shape(1, walkers),
            shape(1, 1),
        ),
        [VMEM] * 9,
        us=1.5,
        name="place",
    )(current, done, spots, logs, info, pair_s, odd_s, pair_i, odd_i)
    return (
        inv_new,
        sla_new,
        pos_new.transpose(1, 0, 2),
        log_new.reshape(walkers),
        energy_new.reshape(walkers),
        mean.reshape(()),
    )


def solution(mesh):
    return jax.shard_map(
        body,
        mesh=mesh,
        in_specs=(
            P("walkers", None, "orb", None),
            P("walkers", None, "orb", None),
            P("walkers", None, None),
            P("walkers", None, None),
            P("walkers", None, None),
            P("walkers", None, None),
            P("walkers"),
            P("walkers"),
            P(),
            P(),
            P(None, "orb", None),
            P(),
        ),
        out_specs=(
            P("walkers", None, "orb", None),
            P("walkers", None, "orb", None),
            P("walkers", None, None),
            P("walkers"),
            P("walkers"),
            P(),
        ),
        check_vma=False,
    )
```

```python
import jax
import jax.numpy as jnp
from jax import lax
from jax.experimental import pallas as pl
from jax.experimental.pallas import tpu as pltpu
from jax.sharding import PartitionSpec as P

F32 = jnp.float32
BF16 = jnp.bfloat16
highest = lax.Precision.HIGHEST
VMEM = pl.BlockSpec(memory_space=pltpu.VMEM)
ANY = pl.BlockSpec(memory_space=pl.ANY)
LANES = 128
INFO = 8


def nt(a, b):
    return lax.dot_general(
        a, b, (((1,), (1,)), ((), ())), precision=highest, preferred_element_type=F32
    )


def thirds(x):
    high = x.astype(BF16)
    rest = x - high.astype(F32)
    middle = rest.astype(BF16)
    low = (rest - middle.astype(F32)).astype(BF16)
    return jnp.concatenate([high, middle, low], axis=0)


def parted(x):
    high = x.astype(BF16)
    return jnp.concatenate([high, (x - high.astype(F32)).astype(BF16)], axis=0)


def product(a, b):
    rows = a.shape[0]
    inner = b.shape[0]
    left = parted(a)
    right = parted(b)
    whole = None
    for part in (right[:inner], right[inner:]):
        both = lax.dot_general(
            left, part, (((1,), (0,)), ((), ())), preferred_element_type=F32
        )
        both = both[:rows] + both[rows:]
        whole = both if whole is None else whole + both
    return whole


def product_nt(a, b):
    rows, cols = a.shape[0], b.shape[0]
    both = lax.dot_general(
        parted(a), parted(b), (((1,), (1,)), ((), ())), preferred_element_type=F32
    )
    both = both[:rows] + both[rows:]
    return both[:, :cols] + both[:, cols:]


def taken_nt(hot, x):
    rows = x.shape[0]
    parts = lax.dot_general(
        hot.astype(BF16), thirds(x), (((1,), (1,)), ((), ())), preferred_element_type=F32
    )
    return parts[:, :rows] + parts[:, rows : 2 * rows] + parts[:, 2 * rows :]


def spread(x, hot):
    hot = hot.astype(BF16)
    return lax.dot_general(
        thirds(x),
        jnp.concatenate([hot] * 3, axis=0),
        (((0,), (0,)), ((), ())),
        preferred_element_type=F32,
    )


def taken(x, hot):
    rows = x.shape[0]
    parts = lax.dot_general(
        thirds(x), hot.astype(BF16), (((1,), (1,)), ((), ())), preferred_element_type=F32
    )
    return parts[:rows] + parts[rows : 2 * rows] + parts[2 * rows :]


def turned(rows):
    short = -rows.shape[0] % 8
    if short:
        rows = jnp.concatenate([rows, jnp.zeros((short, rows.shape[1]), F32)], axis=0)
    return jnp.transpose(rows)


def moves_of(order_ref, flags_ref):
    walkers, _, moves = flags_ref.shape
    nel = order_ref.shape[2]
    order = turned(
        jnp.concatenate([order_ref[w] for w in range(walkers)], axis=0).astype(F32)
    )
    flags = jnp.concatenate([flags_ref[w] for w in range(walkers)], axis=0).astype(F32)
    flags = turned(
        jnp.concatenate([flags, jnp.zeros((2 * walkers, nel - moves), F32)], axis=1)
    )
    cols = [order[:moves, i : i + 1] for i in range(2 * walkers)]
    keep = [flags[:moves, i : i + 1] for i in range(2 * walkers)]
    return cols, keep


def one_hots(cols, nel):
    moves = cols[0].shape[0]
    lanes = lax.broadcasted_iota(jnp.int32, (moves, nel), 1).astype(F32)
    return [(c == lanes).astype(F32) for c in cols]


def limits_of(spots_ref, walkers):
    counts = spots_ref[walkers, 0:1, :]
    limits = [counts[:, :1]]
    for w in range(1, walkers):
        limits.append(limits[-1] + counts[:, w : w + 1])
    return limits


def picked(limits, index, choices):
    rows = max(x[0].shape[0] for x in choices)
    after = [
        jnp.broadcast_to(limit - index, (rows, choices[0][0].shape[1])) <= 0.0
        for limit in limits[:-1]
    ]
    out = []
    for some in choices:
        value = some[0]
        for w in range(1, len(some)):
            value = jnp.where(after[w - 1][: value.shape[0]], some[w], value)
        out.append(value)
    return out


def sent(spots_ref, walkers, pair_ref, odd_ref):
    half = walkers // 2
    limits = limits_of(spots_ref, walkers)
    parity = lax.rem(lax.axis_index("walkers"), 2)
    out = []
    for pay, up in ((pair_ref, parity == 0), (odd_ref, parity == 1)):
        up = up.astype(F32)
        out.append(
            (pay, [(limits, up * (limits[-1] - 1.0 * half) + 1.0 * j) for j in range(half)])
        )
    return out


def pair_tiles(turns, rows, nel, kinds):
    sums = [None, None]
    for h in (0, 1):
        for t in range(nel // 8):
            wide = [
                [
                    jnp.broadcast_to(turn[h][c][8 * t : 8 * t + 8], (8, nel))
                    for c in range(3)
                ]
                for turn in turns
            ]
            for g in range(h, 2):
                squares = []
                for i, row in enumerate(rows):
                    total = None
                    for c in range(3):
                        offset = wide[i][c] - row[g][c]
                        total = offset * offset if total is None else total + offset * offset
                    squares.append(total)
                kind = int(g != h)
                term = kinds[kind](*squares)
                sums[kind] = term if sums[kind] is None else sums[kind] + term
    return sums


def summed(tile):
    return jnp.sum(jnp.sum(tile, axis=0, keepdims=True), axis=1, keepdims=True)


def jastrow_of(spots, turn, jas, nel):
    rows, turns = (
        [
            [
                [cut(base + 3 * h + c) for c in range(3)]
                for h in (0, 1)
            ]
            for base in (0, 8)
        ]
        for cut in (lambda r: spots[r : r + 1], lambda r: turn[:, r : r + 1])
    )

    def change(fall):
        fall = jnp.broadcast_to(fall, (8, nel))

        def term(new, old):
            nd = jnp.sqrt(new)
            od = jnp.sqrt(old)
            return (nd - od) / ((1.0 + fall * nd) * (1.0 + fall * od))

        return term

    same, other = pair_tiles(turns, rows, nel, [change(jas[:, 2:3]), change(jas[:, 3:4])])
    return summed(same * (0.5 * jas[:, :1]) + other * jas[:, 1:2])


def in_rows(rows):
    return [r[:, at : at + LANES] for at in range(0, rows[0].shape[1], LANES) for r in rows]


def energy_kernel(
    pos_in, dis_in, order_in, flags_in, counts_in, jas_in, amp_in, spots_out, info_out,
    pos_ref, dis_ref, order_ref, flags_ref, counts_ref, jas_ref, amp_ref, spots_ref, info_ref,
    loads, stores,
):
    operands = (
        (pos_in, pos_ref),
        (dis_in, dis_ref),
        (order_in, order_ref),
        (flags_in, flags_ref),
        (counts_in, counts_ref),
        (jas_in, jas_ref),
        (amp_in, amp_ref),
    )
    copies = [pltpu.make_async_copy(a, b, loads.at[i]) for i, (a, b) in enumerate(operands)]
    for copy in copies:
        copy.start()
    for copy in copies:
        copy.wait()
    _, walkers, both = pos_ref.shape
    nel = both // 2
    cols, keep = moves_of(order_ref, flags_ref)
    hots = one_hots(cols, nel)
    applied = jnp.concatenate(
        [
            jnp.concatenate(
                [
                    jnp.sum(hots[2 * w + s] * keep[2 * w + s], axis=0, keepdims=True)
                    for s in (0, 1)
                ],
                axis=1,
            )
            for w in range(walkers)
        ],
        axis=0,
    )
    now = [pos_ref[c] + dis_ref[c] * applied for c in range(3)]
    turn = turned(jnp.concatenate(now, axis=0))
    weighted = jnp.zeros((1, nel), F32)
    counts = counts_ref[...].astype(F32)
    for w in range(walkers):
        nrows = [now[c][w : w + 1] for c in range(3)]
        halves = [[r[:, h * nel : (h + 1) * nel] for r in nrows] for h in (0, 1)]
        tall = [
            [
                turn[h * nel : (h + 1) * nel, c * walkers + w : c * walkers + w + 1]
                for c in range(3)
            ]
            for h in (0, 1)
        ]
        same, other = pair_tiles([tall], [halves], nel, [lambda q: lax.rsqrt(q + 1.0)] * 2)
        soft = jnp.sum(same + 2.0 * other, axis=0, keepdims=True)
        wide = [soft, jnp.zeros((7 - 3 * (both // LANES), LANES), F32)]
        spots_ref[w, :8] = jnp.concatenate(in_rows(nrows) + wide[: 1 + (3 * (both // LANES) < 7)], axis=0)
        spots_ref[w, 8 : 8 + 3 * (both // LANES)] = jnp.concatenate(
            in_rows([pos_ref[c, w : w + 1] for c in range(3)]), axis=0
        )
        weighted = weighted + soft * counts[:, w : w + 1]
    me = lax.axis_index("walkers")
    lanes = lax.broadcasted_iota(jnp.int32, info_ref.shape, 1)
    rows = lax.broadcasted_iota(jnp.int32, info_ref.shape, 0)
    spots_ref[walkers] = jnp.zeros(spots_ref.shape[1:], F32)
    for row, some in enumerate((counts, jas_ref[...], amp_ref[...])):
        spots_ref[walkers, row : row + 1, : some.shape[1]] = some
    number = jnp.sum(counts, axis=1, keepdims=True)
    info_ref[...] = jnp.where((lanes == me) & (rows == 0), number, 0.0)
    info_ref[1:2, :nel] = weighted
    copies = [
        pltpu.make_async_copy(info_ref, info_out, stores.at[0]),
        pltpu.make_async_copy(spots_ref, spots_out, stores.at[1]),
    ]
    for copy in copies:
        copy.start()
    for copy in copies:
        copy.wait()


def shift_kernel(
    pos_ref, dis_ref, order_ref, flags_ref, cen_ref, exp_ref, orb_ref, shift_ref, differ_ref,
):
    _, walkers, both = pos_ref.shape
    nel = both // 2
    moves = flags_ref.shape[2]
    basis = cen_ref.shape[1]
    cols, _ = moves_of(order_ref, flags_ref)
    hots = one_hots(cols, nel)
    rows = [ref[c] for ref in (pos_ref, dis_ref) for c in range(3)]
    rows = jnp.concatenate(rows + [jnp.zeros((-6 * walkers % 8, both), F32)] * (6 * walkers % 8 > 0), axis=0)
    for s in (0, 1):
        points = nt(
            jnp.concatenate([hots[2 * w + s] for w in range(walkers)], axis=0),
            rows[:, s * nel : (s + 1) * nel],
        )
        for w in range(walkers):
            mine = points[w * moves : (w + 1) * moves]
            old = []
            new = []
            for c in range(3):
                at = c * walkers + w
                to = (3 + c) * walkers + w
                spot = mine[:, at : at + 1]
                old.append(jnp.broadcast_to(spot, (moves, LANES)))
                new.append(jnp.broadcast_to(spot + mine[:, to : to + 1], (moves, LANES)))
            for j in range(0, basis, LANES):
                osq = None
                nsq = None
                for c in range(3):
                    row = cen_ref[c : c + 1, j : j + LANES]
                    do = old[c] - row
                    dn = new[c] - row
                    osq = do * do if osq is None else osq + do * do
                    nsq = dn * dn if nsq is None else nsq + dn * dn
                rate = -exp_ref[:, j : j + LANES]
                differ_ref[s, w * moves : (w + 1) * moves, j : j + LANES] = jnp.exp(
                    rate * nsq
                ) - jnp.exp(rate * osq)
    for s in (0, 1):
        shift_ref[s] = product_nt(differ_ref[s], orb_ref[s])


def partial_kernel(
    shift_ref, order_ref, flags_ref, inv_ref, sla_ref, spots_ref,
    part_ref, done_ref, pair_ref, odd_ref,
):
    walkers, _, orbs, nel = inv_ref.shape
    moves = flags_ref.shape[2]
    cols, keep = moves_of(order_ref, flags_ref)
    hots = one_hots(cols, nel)
    members = lax.axis_size("orb")
    share = walkers // members
    first = lax.axis_index("orb") * share
    tail = 2 * walkers * moves
    part_ref[tail:, :] = jnp.zeros((part_ref.shape[0] - tail, part_ref.shape[1]), F32)
    jas = spots_ref[walkers, 1:2, :]
    for w in range(share):
        mine = spots_ref[first + w]
        at = tail + 2 + first + w
        part_ref[pl.ds(at, 1), :] = jnp.broadcast_to(
            jastrow_of(mine, turned(mine), jas, nel), (1, part_ref.shape[1])
        )
    for s in (0, 1):
        for w in range(walkers):
            i = 2 * w + s
            mine = shift_ref[s, w * moves : (w + 1) * moves, :]
            proposed = mine + taken_nt(hots[i], sla_ref[w, s])
            part = product(proposed, inv_ref[w, s])
            part_ref[i * moves : (i + 1) * moves, :] = part * keep[i]
            done_ref[w, s] = sla_ref[w, s] + spread(mine, hots[i] * keep[i])
    half = walkers // 2
    per = 2 * orbs
    tail = half * per
    for pay, indices in sent(spots_ref, walkers, pair_ref, odd_ref):
        for j, (limits, index) in enumerate(indices):
            rows = picked(
                limits,
                index,
                [[done_ref[w, s] for w in range(walkers)] for s in (0, 1)]
                + [[spots_ref[w, :8] for w in range(walkers)]],
            )
            for s in (0, 1):
                pay[j * per + s * orbs : j * per + (s + 1) * orbs, :] = rows[s]
            pay[tail + 8 * j : tail + 8 * j + 8, :] = rows[2]


def join_kernel(part_ref, info_ref, out_ref):
    rows = part_ref.shape[0] - info_ref.shape[0]
    out_ref[:rows, :] = part_ref[:rows, :]
    out_ref[rows:, :] = part_ref[rows:, :] + info_ref[...]


def add_kernel(mine_ref, other_ref, out_ref):
    out_ref[...] = mine_ref[...] + other_ref[...]


def update_kernel(
    sum_ref, got_ref, inv_ref, order_ref, flags_ref, spots_ref,
    cur_ref, log_ref, info_ref, pair_ref, odd_ref,
):
    walkers, _, orbs, nel = inv_ref.shape
    moves = flags_ref.shape[2]
    count = 2 * walkers
    cols, keep = moves_of(order_ref, flags_ref)
    hots = one_hots(cols, nel)
    eye = (
        lax.broadcasted_iota(jnp.int32, (moves, moves), 0)
        == lax.broadcasted_iota(jnp.int32, (moves, moves), 1)
    ).astype(F32)
    tiles = moves // 8
    left = []
    right = []
    columns = []
    for i in range(count):
        at = slice(i * moves, (i + 1) * moves)
        change = sum_ref[at, :] + got_ref[at, :] - hots[i] * keep[i]
        coupling = taken(change, hots[i]) + eye
        columns.append(taken(inv_ref[i // 2, i % 2], hots[i]))
        left.append([coupling[8 * t : 8 * t + 8] for t in range(tiles)])
        right.append([change[8 * t : 8 * t + 8] for t in range(tiles)])
    info_ref[...] = sum_ref[count * moves :, :] + got_ref[count * moves :, :]
    lanes = lax.broadcasted_iota(jnp.int32, (1, nel), 1)
    sub = lax.broadcasted_iota(jnp.int32, (8, nel), 0)
    pivots = [jnp.ones((1, nel), F32) for _ in range(count)]
    for k in range(0, moves, 2):
        own, line = k // 8, k % 8
        for i in range(count):
            wide = [
                [jnp.broadcast_to(left[i][t][:, c : c + 1], (8, nel)) for t in range(tiles)]
                for c in (k, k + 1)
            ]
            a, b = (wide[c][own][line : line + 1] for c in (0, 1))
            c, d = (wide[c][own][line + 1 : line + 2] for c in (0, 1))
            det = a * d - b * c
            pivots[i] = jnp.where(lanes == k, det, pivots[i])
            scale = 1.0 / det
            new = []
            for side, width in ((left, moves), (right, nel)):
                upper = side[i][own][line : line + 1]
                lower = side[i][own][line + 1 : line + 2]
                new.append(
                    (
                        (d[:, :width] * upper - b[:, :width] * lower) * scale[:, :width],
                        (a[:, :width] * lower - c[:, :width] * upper) * scale[:, :width],
                    )
                )
            for t in range(tiles):
                for side, width, (upper, lower) in ((left, moves, new[0]), (right, nel, new[1])):
                    tile = (
                        side[i][t] - wide[0][t][:, :width] * upper - wide[1][t][:, :width] * lower
                    )
                    if t == own:
                        tile = jnp.where(
                            sub[:, :width] == line,
                            upper,
                            jnp.where(sub[:, :width] == line + 1, lower, tile),
                        )
                    side[i][t] = tile
    for i in range(count):
        solved = jnp.concatenate(right[i], axis=0)
        cur_ref[i // 2, i % 2] = inv_ref[i // 2, i % 2] - product(columns[i], solved)
    log_ref[...] = jnp.zeros(log_ref.shape, F32)
    for w in range(walkers):
        both = jnp.log(jnp.abs(pivots[2 * w])) + jnp.log(jnp.abs(pivots[2 * w + 1]))
        log_ref[w : w + 1, :] = (
            jnp.broadcast_to(jnp.sum(both, axis=1, keepdims=True), (1, nel))
            + info_ref[2 + w : 3 + w, :nel]
            + spots_ref[walkers, 2:3, w : w + 1]
        )
    half = walkers // 2
    per = 2 * orbs
    tail = half * per
    for pay, indices in sent(spots_ref, walkers, pair_ref, odd_ref):
        pay[tail : tail + INFO, :] = info_ref[...]
        pay[tail + INFO :, :] = jnp.zeros((pay.shape[0] - tail - INFO, LANES), F32)
        for j, (limits, index) in enumerate(indices):
            rows = picked(
                limits,
                index,
                [[cur_ref[w, s] for w in range(walkers)] for s in (0, 1)]
                + [[log_ref[w : w + 1, :] for w in range(walkers)]],
            )
            for s in (0, 1):
                pay[j * per + s * orbs : j * per + (s + 1) * orbs, :] = rows[s]
            pay[tail + INFO + j : tail + INFO + j + 1, :] = rows[2]


def place_kernel(
    cur_ref, done_ref, spots_ref, log_ref, info_ref,
    pair_s_ref, odd_s_ref, pair_i_ref, odd_i_ref,
    inv_out, sla_out, pos_out, log_out, energy_out, mean_out,
):
    walkers, _, orbs, nel = cur_ref.shape
    width = pos_out.shape[2] // LANES
    half = walkers // 2
    per = 2 * orbs
    tail = half * per
    me = lax.axis_index("walkers")
    parity = lax.rem(me, 2)
    info = info_ref[...] + pair_i_ref[tail : tail + INFO, :]
    lanes = lax.broadcasted_iota(jnp.int32, (1, info.shape[1]), 1)
    before = jnp.sum(jnp.where(lanes < me, info[0:1], 0.0), axis=1, keepdims=True)
    groups = lax.axis_size("walkers")
    both = pos_out.shape[2]

    def energy_of(row, copies):
        soft = jnp.sum(row, axis=1, keepdims=True)
        return (soft - 1.0 * both * copies) / (1.0 * both * (both - 1))

    copies = jnp.sum(info[0:1], axis=1, keepdims=True)
    mean_out[...] = energy_of(info[1:2], copies) / (1.0 * walkers * groups)
    limits = limits_of(spots_ref, walkers)
    slots = lax.broadcasted_iota(jnp.int32, (1, walkers), 1)
    here = [[cur_ref[w, s] for w in range(walkers)] for s in (0, 1)]
    here += [[done_ref[w, s] for w in range(walkers)] for s in (0, 1)]
    here += [[spots_ref[w, :8] for w in range(walkers)]]
    here += [[log_ref[w : w + 1, :] for w in range(walkers)]]
    odd = parity.astype(F32)
    log_new = jnp.zeros((1, walkers), F32)
    energy_new = jnp.zeros((1, walkers), F32)
    for j in range(walkers):
        index = (1.0 * walkers) * me.astype(F32) + 1.0 * j - before
        own = picked(limits, index, here)
        low = j < half
        outside = -index if low else index - limits[-1] + 1.0
        entry = index + 1.0 * half if low else index - limits[-1]
        on_pair = odd if low else 1.0 - odd
        shape_here = (orbs, nel)
        away = jnp.broadcast_to(outside, shape_here) > 0.0
        second = jnp.broadcast_to(entry, shape_here) > 0.5
        pair = jnp.broadcast_to(on_pair, shape_here) > 0.5

        def one(late, at, rows):
            parts = []
            for i in range(half):
                start = at(i)
                a, b = (ref[start : start + rows, :] for ref in late)
                parts.append(jnp.where(pair[:rows], a, b))
            value = parts[0]
            for i in range(1, half):
                again = second if i == 1 else jnp.broadcast_to(entry, shape_here) > i - 0.5
                value = jnp.where(again[:rows], parts[i], value)
            return value

        inverses = (pair_i_ref, odd_i_ref)
        slaters = (pair_s_ref, odd_s_ref)
        got = [one(inverses, lambda i, s=s: i * per + s * orbs, orbs) for s in (0, 1)]
        got += [one(slaters, lambda i, s=s: i * per + s * orbs, orbs) for s in (0, 1)]
        got += [one(slaters, lambda i: tail + 8 * i, 8)]
        got += [one(inverses, lambda i: tail + INFO + i, 1)]
        new = [jnp.where(away[: o.shape[0]], g, o) for o, g in zip(own, got)]
        for s in (0, 1):
            inv_out[j, s] = new[s]
            sla_out[j, s] = new[2 + s]
        for c in range(3):
            for h in range(width):
                pos_out[c, j : j + 1, h * LANES : (h + 1) * LANES] = new[4][
                    3 * h + c : 3 * h + c + 1
                ]
        log_new = jnp.where(slots == j, new[5][:, :walkers], log_new)
        energy_new = jnp.where(
            slots == j, energy_of(new[4][3 * width : 3 * width + 1], 1.0), energy_new
        )
    log_out[...] = log_new
    energy_out[...] = energy_new


def call(kernel, outs, in_specs, scratch=(), us=1.0, name=None, out_specs=None, vmem=32 * 2**20):
    return pl.pallas_call(
        kernel,
        out_shape=outs,
        in_specs=in_specs,
        out_specs=out_specs or jax.tree.map(lambda _: VMEM, outs),
        scratch_shapes=list(scratch),
        compiler_params=pltpu.CompilerParams(vmem_limit_bytes=vmem),
        cost_estimate=pl.CostEstimate(flops=int(us * 1.1e9), bytes_accessed=2**18, transcendentals=0),
        name=name,
    )


def shape(*dims):
    return jax.ShapeDtypeStruct(dims, F32)


def body(
    inverse, slater, positions, displacements, move_order, accepted, counts, log_amp, centers,
    exponents, orbitals, jastrow,
):
    walkers, _, orbs, nel = inverse.shape
    moves = accepted.shape[2]
    both = positions.shape[2]
    basis = centers.shape[1]
    groups = lax.axis_size("walkers")
    members = lax.axis_size("orb")
    wide = max(LANES, groups)
    half = walkers // 2
    per = 2 * orbs
    count = 2 * walkers
    tall = half * per + 16

    counts = counts.reshape(1, walkers)
    log_amp = log_amp.reshape(1, walkers)
    jastrow = jastrow.reshape(1, jastrow.shape[0])

    pairs = [(i, i ^ 1) for i in range(groups)]
    odds = [(i, i + 1) for i in range(1, groups - 1, 2)]
    odds = odds + [(b, a) for a, b in odds]

    places = positions.transpose(1, 0, 2)
    steps = displacements.transpose(1, 0, 2)
    operands = (places, steps, move_order, accepted, counts, jastrow, log_amp)
    made = (shape(walkers + 1, 16, LANES), shape(INFO, wide))
    spots, info = call(
        energy_kernel,
        made,
        [ANY] * len(operands),
        out_specs=(ANY, ANY),
        scratch=[pltpu.VMEM(x.shape, x.dtype) for x in operands + made]
        + [pltpu.SemaphoreType.DMA((len(operands),)), pltpu.SemaphoreType.DMA((len(made),))],
        us=2,
        vmem=61 * 2**20,
        name="energy",
    )(*operands)

    hops = members * 2
    step = hops
    while step < groups:
        info = info + lax.ppermute(info, "walkers", [(i, i ^ step) for i in range(groups)])
        step *= 2
    joint = [
        (d * members + o, (d ^ (2 * hop)) * members + o)
        for o in range(members)
        for hop in [(1, 3, 0, 2)[o] if members == 4 else o]
        for d in range(groups)
        if 2 * hop < groups
    ]
    info = lax.ppermute(info, ("walkers", "orb"), joint)

    shift = call(
        shift_kernel,
        shape(2, walkers * moves, orbs),
        [VMEM] * 7,
        scratch=[pltpu.VMEM((2, walkers * moves, basis), F32)],
        us=3,
        name="shift",
    )(
        places, steps, move_order, accepted, centers, exponents.reshape(1, basis), orbitals,
    )

    part, done, pair_s, odd_s = call(
        partial_kernel,
        (
            shape(count * moves + INFO, nel),
            shape(walkers, 2, orbs, nel),
            shape(tall, LANES),
            shape(tall, LANES),
        ),
        [VMEM] * 6,
        us=2,
        name="partial",
    )(shift, move_order, accepted, inverse, slater, spots)

    part = call(
        join_kernel, shape(count * moves + INFO, nel), [VMEM] * 2, us=0.2, name="join"
    )(part, info)

    total = part
    got = jnp.zeros_like(part)
    step = 1
    while step < members:
        partner = [(o, o ^ step) for o in range(members)]
        got = lax.ppermute(total, "orb", partner)
        if 2 * step < members:
            total = call(
                add_kernel,
                shape(count * moves + INFO, nel),
                [VMEM] * 2,
                us=0.5,
                name="add",
            )(total, got)
        step *= 2

    pair_s = lax.ppermute(pair_s, "walkers", pairs)
    odd_s = lax.ppermute(odd_s, "walkers", odds)

    current, logs, info, pair_i, odd_i = call(
        update_kernel,
        (
            shape(walkers, 2, orbs, nel),
            shape(8, nel),
            shape(INFO, wide),
            shape(tall, LANES),
            shape(tall, LANES),
        ),
        [VMEM] * 6,
        us=4,
        name="update",
    )(total, got, inverse, move_order, accepted, spots)

    pair_i = lax.ppermute(pair_i, "walkers", pairs)
    odd_i = lax.ppermute(odd_i, "walkers", odds)

    inv_new, sla_new, pos_new, log_new, energy_new, mean = call(
        place_kernel,
        (
            shape(walkers, 2, orbs, nel),
            shape(walkers, 2, orbs, nel),
            shape(3, walkers, both),
            shape(1, walkers),
            shape(1, walkers),
            shape(1, 1),
        ),
        [VMEM] * 9,
        us=1.5,
        name="place",
    )(current, done, spots, logs, info, pair_s, odd_s, pair_i, odd_i)
    return (
        inv_new,
        sla_new,
        pos_new.transpose(1, 0, 2),
        log_new.reshape(walkers),
        energy_new.reshape(walkers),
        mean.reshape(()),
    )


def solution(mesh):
    return jax.shard_map(
        body,
        mesh=mesh,
        in_specs=(
            P("walkers", None, "orb", None),
            P("walkers", None, "orb", None),
            P("walkers", None, None),
            P("walkers", None, None),
            P("walkers", None, None),
            P("walkers", None, None),
            P("walkers"),
            P("walkers"),
            P(),
            P(),
            P(None, "orb", None),
            P(),
        ),
        out_specs=(
            P("walkers", None, "orb", None),
            P("walkers", None, "orb", None),
            P("walkers", None, None),
            P("walkers"),
            P("walkers"),
            P(),
        ),
        check_vma=False,
    )
```

```python
import jax
import jax.numpy as jnp
from jax import lax
from jax.experimental import pallas as pl
from jax.experimental.pallas import tpu as pltpu
from jax.sharding import PartitionSpec as P

F32 = jnp.float32
BF16 = jnp.bfloat16
highest = lax.Precision.HIGHEST
VMEM = pl.BlockSpec(memory_space=pltpu.VMEM)
ANY = pl.BlockSpec(memory_space=pl.ANY)
LANES = 128
INFO = 8


def nt(a, b):
    return lax.dot_general(
        a, b, (((1,), (1,)), ((), ())), precision=highest, preferred_element_type=F32
    )


def thirds(x):
    high = x.astype(BF16)
    rest = x - high.astype(F32)
    middle = rest.astype(BF16)
    low = (rest - middle.astype(F32)).astype(BF16)
    return jnp.concatenate([high, middle, low], axis=0)


def parted(x):
    high = x.astype(BF16)
    return jnp.concatenate([high, (x - high.astype(F32)).astype(BF16)], axis=0)


def product(a, b):
    rows = a.shape[0]
    inner = b.shape[0]
    left = parted(a)
    right = parted(b)
    whole = None
    for part in (right[:inner], right[inner:]):
        both = lax.dot_general(
            left, part, (((1,), (0,)), ((), ())), preferred_element_type=F32
        )
        both = both[:rows] + both[rows:]
        whole = both if whole is None else whole + both
    return whole


def product_nt(a, b):
    rows, cols = a.shape[0], b.shape[0]
    both = lax.dot_general(
        parted(a), parted(b), (((1,), (1,)), ((), ())), preferred_element_type=F32
    )
    both = both[:rows] + both[rows:]
    return both[:, :cols] + both[:, cols:]


def taken_nt(hot, x):
    rows = x.shape[0]
    parts = lax.dot_general(
        hot.astype(BF16), thirds(x), (((1,), (1,)), ((), ())), preferred_element_type=F32
    )
    return parts[:, :rows] + parts[:, rows : 2 * rows] + parts[:, 2 * rows :]


def spread(x, hot):
    hot = hot.astype(BF16)
    return lax.dot_general(
        thirds(x),
        jnp.concatenate([hot] * 3, axis=0),
        (((0,), (0,)), ((), ())),
        preferred_element_type=F32,
    )


def taken(x, hot):
    rows = x.shape[0]
    parts = lax.dot_general(
        thirds(x), hot.astype(BF16), (((1,), (1,)), ((), ())), preferred_element_type=F32
    )
    return parts[:rows] + parts[rows : 2 * rows] + parts[2 * rows :]


def turned(rows):
    short = -rows.shape[0] % 8
    if short:
        rows = jnp.concatenate([rows, jnp.zeros((short, rows.shape[1]), F32)], axis=0)
    return jnp.transpose(rows)


def moves_of(order_ref, flags_ref):
    walkers, _, moves = flags_ref.shape
    nel = order_ref.shape[2]
    order = turned(
        jnp.concatenate([order_ref[w] for w in range(walkers)], axis=0).astype(F32)
    )
    flags = jnp.concatenate([flags_ref[w] for w in range(walkers)], axis=0).astype(F32)
    flags = turned(
        jnp.concatenate([flags, jnp.zeros((2 * walkers, nel - moves), F32)], axis=1)
    )
    cols = [order[:moves, i : i + 1] for i in range(2 * walkers)]
    keep = [flags[:moves, i : i + 1] for i in range(2 * walkers)]
    return cols, keep


def one_hots(cols, nel):
    moves = cols[0].shape[0]
    lanes = lax.broadcasted_iota(jnp.int32, (moves, nel), 1).astype(F32)
    return [(c == lanes).astype(F32) for c in cols]


def limits_of(spots_ref, walkers):
    counts = spots_ref[walkers, 0:1, :]
    limits = [counts[:, :1]]
    for w in range(1, walkers):
        limits.append(limits[-1] + counts[:, w : w + 1])
    return limits


def picked(limits, index, choices):
    rows = max(x[0].shape[0] for x in choices)
    after = [
        jnp.broadcast_to(limit - index, (rows, choices[0][0].shape[1])) <= 0.0
        for limit in limits[:-1]
    ]
    out = []
    for some in choices:
        value = some[0]
        for w in range(1, len(some)):
            value = jnp.where(after[w - 1][: value.shape[0]], some[w], value)
        out.append(value)
    return out


def sent(spots_ref, walkers, pair_ref, odd_ref):
    half = walkers // 2
    limits = limits_of(spots_ref, walkers)
    parity = lax.rem(lax.axis_index("walkers"), 2)
    out = []
    for pay, up in ((pair_ref, parity == 0), (odd_ref, parity == 1)):
        up = up.astype(F32)
        out.append(
            (pay, [(limits, up * (limits[-1] - 1.0 * half) + 1.0 * j) for j in range(half)])
        )
    return out


def pair_tiles(turns, rows, nel, kinds):
    sums = [None, None]
    for h in (0, 1):
        for t in range(nel // 8):
            wide = [
                [
                    jnp.broadcast_to(turn[h][c][8 * t : 8 * t + 8], (8, nel))
                    for c in range(3)
                ]
                for turn in turns
            ]
            for g in range(h, 2):
                squares = []
                for i, row in enumerate(rows):
                    total = None
                    for c in range(3):
                        offset = wide[i][c] - row[g][c]
                        total = offset * offset if total is None else total + offset * offset
                    squares.append(total)
                kind = int(g != h)
                term = kinds[kind](*squares)
                sums[kind] = term if sums[kind] is None else sums[kind] + term
    return sums


def summed(tile):
    return jnp.sum(jnp.sum(tile, axis=0, keepdims=True), axis=1, keepdims=True)


def jastrow_of(spots, turn, jas, nel):
    rows, turns = (
        [
            [
                [cut(base + 3 * h + c) for c in range(3)]
                for h in (0, 1)
            ]
            for base in (0, 8)
        ]
        for cut in (lambda r: spots[r : r + 1], lambda r: turn[:, r : r + 1])
    )

    def change(fall):
        fall = jnp.broadcast_to(fall, (8, nel))

        def term(new, old):
            nd = jnp.sqrt(new)
            od = jnp.sqrt(old)
            return (nd - od) / ((1.0 + fall * nd) * (1.0 + fall * od))

        return term

    same, other = pair_tiles(turns, rows, nel, [change(jas[:, 2:3]), change(jas[:, 3:4])])
    return summed(same * (0.5 * jas[:, :1]) + other * jas[:, 1:2])


def in_rows(rows):
    return [r[:, at : at + LANES] for at in range(0, rows[0].shape[1], LANES) for r in rows]


def energy_kernel(
    pos_in, dis_in, order_in, flags_in, counts_in, jas_in, amp_in, spots_out, info_out,
    pos_ref, dis_ref, order_ref, flags_ref, counts_ref, jas_ref, amp_ref, spots_ref, info_ref,
    loads, stores,
):
    operands = (
        (pos_in, pos_ref),
        (dis_in, dis_ref),
        (order_in, order_ref),
        (flags_in, flags_ref),
        (counts_in, counts_ref),
        (jas_in, jas_ref),
        (amp_in, amp_ref),
    )
    copies = [pltpu.make_async_copy(a, b, loads.at[i]) for i, (a, b) in enumerate(operands)]
    for copy in copies:
        copy.start()
    for copy in copies:
        copy.wait()
    _, walkers, both = pos_ref.shape
    nel = both // 2
    cols, keep = moves_of(order_ref, flags_ref)
    hots = one_hots(cols, nel)
    applied = jnp.concatenate(
        [
            jnp.concatenate(
                [
                    jnp.sum(hots[2 * w + s] * keep[2 * w + s], axis=0, keepdims=True)
                    for s in (0, 1)
                ],
                axis=1,
            )
            for w in range(walkers)
        ],
        axis=0,
    )
    now = [pos_ref[c] + dis_ref[c] * applied for c in range(3)]
    turn = turned(jnp.concatenate(now, axis=0))
    weighted = jnp.zeros((1, nel), F32)
    counts = counts_ref[...].astype(F32)
    for w in range(walkers):
        nrows = [now[c][w : w + 1] for c in range(3)]
        halves = [[r[:, h * nel : (h + 1) * nel] for r in nrows] for h in (0, 1)]
        tall = [
            [
                turn[h * nel : (h + 1) * nel, c * walkers + w : c * walkers + w + 1]
                for c in range(3)
            ]
            for h in (0, 1)
        ]
        same, other = pair_tiles([tall], [halves], nel, [lambda q: lax.rsqrt(q + 1.0)] * 2)
        soft = jnp.sum(same + 2.0 * other, axis=0, keepdims=True)
        wide = [soft, jnp.zeros((7 - 3 * (both // LANES), LANES), F32)]
        spots_ref[w, :8] = jnp.concatenate(in_rows(nrows) + wide[: 1 + (3 * (both // LANES) < 7)], axis=0)
        spots_ref[w, 8 : 8 + 3 * (both // LANES)] = jnp.concatenate(
            in_rows([pos_ref[c, w : w + 1] for c in range(3)]), axis=0
        )
        weighted = weighted + soft * counts[:, w : w + 1]
    me = lax.axis_index("walkers")
    lanes = lax.broadcasted_iota(jnp.int32, info_ref.shape, 1)
    rows = lax.broadcasted_iota(jnp.int32, info_ref.shape, 0)
    spots_ref[walkers] = jnp.zeros(spots_ref.shape[1:], F32)
    for row, some in enumerate((counts, jas_ref[...], amp_ref[...])):
        spots_ref[walkers, row : row + 1, : some.shape[1]] = some
    number = jnp.sum(counts, axis=1, keepdims=True)
    info_ref[...] = jnp.where((lanes == me) & (rows == 0), number, 0.0)
    info_ref[1:2, :nel] = weighted
    copies = [
        pltpu.make_async_copy(info_ref, info_out, stores.at[0]),
        pltpu.make_async_copy(spots_ref, spots_out, stores.at[1]),
    ]
    for copy in copies:
        copy.start()
    for copy in copies:
        copy.wait()


def shift_kernel(
    pos_ref, dis_ref, order_ref, flags_ref, cen_ref, exp_ref, orb_ref, shift_ref, differ_ref,
):
    _, walkers, both = pos_ref.shape
    nel = both // 2
    moves = flags_ref.shape[2]
    basis = cen_ref.shape[1]
    cols, _ = moves_of(order_ref, flags_ref)
    hots = one_hots(cols, nel)
    rows = [ref[c] for ref in (pos_ref, dis_ref) for c in range(3)]
    rows = jnp.concatenate(rows + [jnp.zeros((-6 * walkers % 8, both), F32)] * (6 * walkers % 8 > 0), axis=0)
    for s in (0, 1):
        points = nt(
            jnp.concatenate([hots[2 * w + s] for w in range(walkers)], axis=0),
            rows[:, s * nel : (s + 1) * nel],
        )
        for w in range(walkers):
            mine = points[w * moves : (w + 1) * moves]
            old = []
            new = []
            for c in range(3):
                at = c * walkers + w
                to = (3 + c) * walkers + w
                spot = mine[:, at : at + 1]
                old.append(jnp.broadcast_to(spot, (moves, LANES)))
                new.append(jnp.broadcast_to(spot + mine[:, to : to + 1], (moves, LANES)))
            for j in range(0, basis, LANES):
                osq = None
                nsq = None
                for c in range(3):
                    row = cen_ref[c : c + 1, j : j + LANES]
                    do = old[c] - row
                    dn = new[c] - row
                    osq = do * do if osq is None else osq + do * do
                    nsq = dn * dn if nsq is None else nsq + dn * dn
                rate = -exp_ref[:, j : j + LANES]
                differ_ref[s, w * moves : (w + 1) * moves, j : j + LANES] = jnp.exp(
                    rate * nsq
                ) - jnp.exp(rate * osq)
    for s in (0, 1):
        shift_ref[s] = product_nt(differ_ref[s], orb_ref[s])


def partial_kernel(
    shift_ref, order_ref, flags_ref, inv_ref, sla_ref, spots_ref,
    part_ref, done_ref, pair_ref, odd_ref,
):
    walkers, _, orbs, nel = inv_ref.shape
    moves = flags_ref.shape[2]
    cols, keep = moves_of(order_ref, flags_ref)
    hots = one_hots(cols, nel)
    members = lax.axis_size("orb")
    share = walkers // members
    first = lax.axis_index("orb") * share
    tail = 2 * walkers * moves
    part_ref[tail:, :] = jnp.zeros((part_ref.shape[0] - tail, part_ref.shape[1]), F32)
    jas = spots_ref[walkers, 1:2, :]
    for w in range(share):
        mine = spots_ref[first + w]
        at = tail + 2 + first + w
        part_ref[pl.ds(at, 1), :] = jnp.broadcast_to(
            jastrow_of(mine, turned(mine), jas, nel), (1, part_ref.shape[1])
        )
    for s in (0, 1):
        for w in range(walkers):
            i = 2 * w + s
            mine = shift_ref[s, w * moves : (w + 1) * moves, :]
            proposed = mine + taken_nt(hots[i], sla_ref[w, s])
            part = product(proposed, inv_ref[w, s])
            part_ref[i * moves : (i + 1) * moves, :] = part * keep[i]
            done_ref[w, s] = sla_ref[w, s] + spread(mine, hots[i] * keep[i])
    half = walkers // 2
    per = 2 * orbs
    tail = half * per
    for pay, indices in sent(spots_ref, walkers, pair_ref, odd_ref):
        for j, (limits, index) in enumerate(indices):
            rows = picked(
                limits,
                index,
                [[done_ref[w, s] for w in range(walkers)] for s in (0, 1)]
                + [[spots_ref[w, :8] for w in range(walkers)]],
            )
            for s in (0, 1):
                pay[j * per + s * orbs : j * per + (s + 1) * orbs, :] = rows[s]
            pay[tail + 8 * j : tail + 8 * j + 8, :] = rows[2]


def moved_kernel(
    pos_ref, dis_ref, order_ref, flags_ref, cen_ref, exp_ref, orb_ref, inv_ref, sla_ref, spots_ref,
    part_ref, done_ref, pair_ref, odd_ref, differ_ref, shift_ref,
):
    shift_kernel(
        pos_ref, dis_ref, order_ref, flags_ref, cen_ref, exp_ref, orb_ref, shift_ref, differ_ref
    )
    partial_kernel(
        shift_ref, order_ref, flags_ref, inv_ref, sla_ref, spots_ref,
        part_ref, done_ref, pair_ref, odd_ref,
    )


def join_kernel(part_ref, info_ref, out_ref):
    rows = part_ref.shape[0] - info_ref.shape[0]
    out_ref[:rows, :] = part_ref[:rows, :]
    out_ref[rows:, :] = part_ref[rows:, :] + info_ref[...]


def add_kernel(mine_ref, other_ref, out_ref):
    out_ref[...] = mine_ref[...] + other_ref[...]


def update_kernel(
    sum_ref, got_ref, inv_ref, order_ref, flags_ref, spots_ref,
    cur_ref, log_ref, info_ref, pair_ref, odd_ref,
):
    walkers, _, orbs, nel = inv_ref.shape
    moves = flags_ref.shape[2]
    count = 2 * walkers
    cols, keep = moves_of(order_ref, flags_ref)
    hots = one_hots(cols, nel)
    eye = (
        lax.broadcasted_iota(jnp.int32, (moves, moves), 0)
        == lax.broadcasted_iota(jnp.int32, (moves, moves), 1)
    ).astype(F32)
    tiles = moves // 8
    left = []
    right = []
    columns = []
    for i in range(count):
        at = slice(i * moves, (i + 1) * moves)
        change = sum_ref[at, :] + got_ref[at, :] - hots[i] * keep[i]
        coupling = taken(change, hots[i]) + eye
        columns.append(taken(inv_ref[i // 2, i % 2], hots[i]))
        left.append([coupling[8 * t : 8 * t + 8] for t in range(tiles)])
        right.append([change[8 * t : 8 * t + 8] for t in range(tiles)])
    info_ref[...] = sum_ref[count * moves :, :] + got_ref[count * moves :, :]
    lanes = lax.broadcasted_iota(jnp.int32, (1, nel), 1)
    sub = lax.broadcasted_iota(jnp.int32, (8, nel), 0)
    pivots = [jnp.ones((1, nel), F32) for _ in range(count)]
    for k in range(0, moves, 2):
        own, line = k // 8, k % 8
        for i in range(count):
            wide = [
                [jnp.broadcast_to(left[i][t][:, c : c + 1], (8, nel)) for t in range(tiles)]
                for c in (k, k + 1)
            ]
            a, b = (wide[c][own][line : line + 1] for c in (0, 1))
            c, d = (wide[c][own][line + 1 : line + 2] for c in (0, 1))
            det = a * d - b * c
            pivots[i] = jnp.where(lanes == k, det, pivots[i])
            scale = 1.0 / det
            new = []
            for side, width in ((left, moves), (right, nel)):
                upper = side[i][own][line : line + 1]
                lower = side[i][own][line + 1 : line + 2]
                new.append(
                    (
                        (d[:, :width] * upper - b[:, :width] * lower) * scale[:, :width],
                        (a[:, :width] * lower - c[:, :width] * upper) * scale[:, :width],
                    )
                )
            for t in range(tiles):
                for side, width, (upper, lower) in ((left, moves, new[0]), (right, nel, new[1])):
                    tile = (
                        side[i][t] - wide[0][t][:, :width] * upper - wide[1][t][:, :width] * lower
                    )
                    if t == own:
                        tile = jnp.where(
                            sub[:, :width] == line,
                            upper,
                            jnp.where(sub[:, :width] == line + 1, lower, tile),
                        )
                    side[i][t] = tile
    for i in range(count):
        solved = jnp.concatenate(right[i], axis=0)
        cur_ref[i // 2, i % 2] = inv_ref[i // 2, i % 2] - product(columns[i], solved)
    log_ref[...] = jnp.zeros(log_ref.shape, F32)
    for w in range(walkers):
        both = jnp.log(jnp.abs(pivots[2 * w])) + jnp.log(jnp.abs(pivots[2 * w + 1]))
        log_ref[w : w + 1, :] = (
            jnp.broadcast_to(jnp.sum(both, axis=1, keepdims=True), (1, nel))
            + info_ref[2 + w : 3 + w, :nel]
            + spots_ref[walkers, 2:3, w : w + 1]
        )
    half = walkers // 2
    per = 2 * orbs
    tail = half * per
    for pay, indices in sent(spots_ref, walkers, pair_ref, odd_ref):
        pay[tail : tail + INFO, :] = info_ref[...]
        pay[tail + INFO :, :] = jnp.zeros((pay.shape[0] - tail - INFO, LANES), F32)
        for j, (limits, index) in enumerate(indices):
            rows = picked(
                limits,
                index,
                [[cur_ref[w, s] for w in range(walkers)] for s in (0, 1)]
                + [[log_ref[w : w + 1, :] for w in range(walkers)]],
            )
            for s in (0, 1):
                pay[j * per + s * orbs : j * per + (s + 1) * orbs, :] = rows[s]
            pay[tail + INFO + j : tail + INFO + j + 1, :] = rows[2]


def place_kernel(
    cur_ref, done_ref, spots_ref, log_ref, info_ref,
    pair_s_ref, odd_s_ref, pair_i_ref, odd_i_ref,
    inv_out, sla_out, pos_out, log_out, energy_out, mean_out,
):
    walkers, _, orbs, nel = cur_ref.shape
    width = pos_out.shape[2] // LANES
    half = walkers // 2
    per = 2 * orbs
    tail = half * per
    me = lax.axis_index("walkers")
    parity = lax.rem(me, 2)
    info = info_ref[...] + pair_i_ref[tail : tail + INFO, :]
    lanes = lax.broadcasted_iota(jnp.int32, (1, info.shape[1]), 1)
    before = jnp.sum(jnp.where(lanes < me, info[0:1], 0.0), axis=1, keepdims=True)
    groups = lax.axis_size("walkers")
    both = pos_out.shape[2]

    def energy_of(row, copies):
        soft = jnp.sum(row, axis=1, keepdims=True)
        return (soft - 1.0 * both * copies) / (1.0 * both * (both - 1))

    copies = jnp.sum(info[0:1], axis=1, keepdims=True)
    mean_out[...] = energy_of(info[1:2], copies) / (1.0 * walkers * groups)
    limits = limits_of(spots_ref, walkers)
    slots = lax.broadcasted_iota(jnp.int32, (1, walkers), 1)
    here = [[cur_ref[w, s] for w in range(walkers)] for s in (0, 1)]
    here += [[done_ref[w, s] for w in range(walkers)] for s in (0, 1)]
    here += [[spots_ref[w, :8] for w in range(walkers)]]
    here += [[log_ref[w : w + 1, :] for w in range(walkers)]]
    odd = parity.astype(F32)
    log_new = jnp.zeros((1, walkers), F32)
    energy_new = jnp.zeros((1, walkers), F32)
    for j in range(walkers):
        index = (1.0 * walkers) * me.astype(F32) + 1.0 * j - before
        own = picked(limits, index, here)
        low = j < half
        outside = -index if low else index - limits[-1] + 1.0
        entry = index + 1.0 * half if low else index - limits[-1]
        on_pair = odd if low else 1.0 - odd
        shape_here = (orbs, nel)
        away = jnp.broadcast_to(outside, shape_here) > 0.0
        second = jnp.broadcast_to(entry, shape_here) > 0.5
        pair = jnp.broadcast_to(on_pair, shape_here) > 0.5

        def one(late, at, rows):
            parts = []
            for i in range(half):
                start = at(i)
                a, b = (ref[start : start + rows, :] for ref in late)
                parts.append(jnp.where(pair[:rows], a, b))
            value = parts[0]
            for i in range(1, half):
                again = second if i == 1 else jnp.broadcast_to(entry, shape_here) > i - 0.5
                value = jnp.where(again[:rows], parts[i], value)
            return value

        inverses = (pair_i_ref, odd_i_ref)
        slaters = (pair_s_ref, odd_s_ref)
        got = [one(inverses, lambda i, s=s: i * per + s * orbs, orbs) for s in (0, 1)]
        got += [one(slaters, lambda i, s=s: i * per + s * orbs, orbs) for s in (0, 1)]
        got += [one(slaters, lambda i: tail + 8 * i, 8)]
        got += [one(inverses, lambda i: tail + INFO + i, 1)]
        new = [jnp.where(away[: o.shape[0]], g, o) for o, g in zip(own, got)]
        for s in (0, 1):
            inv_out[j, s] = new[s]
            sla_out[j, s] = new[2 + s]
        for c in range(3):
            for h in range(width):
                pos_out[c, j : j + 1, h * LANES : (h + 1) * LANES] = new[4][
                    3 * h + c : 3 * h + c + 1
                ]
        log_new = jnp.where(slots == j, new[5][:, :walkers], log_new)
        energy_new = jnp.where(
            slots == j, energy_of(new[4][3 * width : 3 * width + 1], 1.0), energy_new
        )
    log_out[...] = log_new
    energy_out[...] = energy_new


def call(kernel, outs, in_specs, scratch=(), us=1.0, name=None, out_specs=None, vmem=32 * 2**20):
    return pl.pallas_call(
        kernel,
        out_shape=outs,
        in_specs=in_specs,
        out_specs=out_specs or jax.tree.map(lambda _: VMEM, outs),
        scratch_shapes=list(scratch),
        compiler_params=pltpu.CompilerParams(vmem_limit_bytes=vmem),
        cost_estimate=pl.CostEstimate(flops=int(us * 1.1e9), bytes_accessed=2**18, transcendentals=0),
        name=name,
    )


def shape(*dims):
    return jax.ShapeDtypeStruct(dims, F32)


def body(
    inverse, slater, positions, displacements, move_order, accepted, counts, log_amp, centers,
    exponents, orbitals, jastrow,
):
    walkers, _, orbs, nel = inverse.shape
    moves = accepted.shape[2]
    both = positions.shape[2]
    basis = centers.shape[1]
    groups = lax.axis_size("walkers")
    members = lax.axis_size("orb")
    wide = max(LANES, groups)
    half = walkers // 2
    per = 2 * orbs
    count = 2 * walkers
    tall = half * per + 16

    counts = counts.reshape(1, walkers)
    log_amp = log_amp.reshape(1, walkers)
    jastrow = jastrow.reshape(1, jastrow.shape[0])

    pairs = [(i, i ^ 1) for i in range(groups)]
    odds = [(i, i + 1) for i in range(1, groups - 1, 2)]
    odds = odds + [(b, a) for a, b in odds]

    places = positions.transpose(1, 0, 2)
    steps = displacements.transpose(1, 0, 2)
    operands = (places, steps, move_order, accepted, counts, jastrow, log_amp)
    made = (shape(walkers + 1, 16, LANES), shape(INFO, wide))
    spots, info = call(
        energy_kernel,
        made,
        [ANY] * len(operands),
        out_specs=(ANY, ANY),
        scratch=[pltpu.VMEM(x.shape, x.dtype) for x in operands + made]
        + [pltpu.SemaphoreType.DMA((len(operands),)), pltpu.SemaphoreType.DMA((len(made),))],
        us=2,
        vmem=61 * 2**20,
        name="energy",
    )(*operands)

    hops = members * 2
    step = hops
    while step < groups:
        info = info + lax.ppermute(info, "walkers", [(i, i ^ step) for i in range(groups)])
        step *= 2
    joint = [
        (d * members + o, (d ^ (2 * hop)) * members + o)
        for o in range(members)
        for hop in [(1, 3, 0, 2)[o] if members == 4 else o]
        for d in range(groups)
        if 2 * hop < groups
    ]
    info = lax.ppermute(info, ("walkers", "orb"), joint)

    part, done, pair_s, odd_s = call(
        moved_kernel,
        (
            shape(count * moves + INFO, nel),
            shape(walkers, 2, orbs, nel),
            shape(tall, LANES),
            shape(tall, LANES),
        ),
        [VMEM] * 10,
        scratch=[
            pltpu.VMEM((2, walkers * moves, basis), F32),
            pltpu.VMEM((2, walkers * moves, orbs), F32),
        ],
        us=4,
        name="moved",
    )(
        places, steps, move_order, accepted, centers, exponents.reshape(1, basis), orbitals,
        inverse, slater, spots,
    )

    part = call(
        join_kernel, shape(count * moves + INFO, nel), [VMEM] * 2, us=0.2, name="join"
    )(part, info)

    total = part
    got = jnp.zeros_like(part)
    step = 1
    while step < members:
        partner = [(o, o ^ step) for o in range(members)]
        got = lax.ppermute(total, "orb", partner)
        if 2 * step < members:
            total = call(
                add_kernel,
                shape(count * moves + INFO, nel),
                [VMEM] * 2,
                us=0.5,
                name="add",
            )(total, got)
        step *= 2

    pair_s = lax.ppermute(pair_s, "walkers", pairs)
    odd_s = lax.ppermute(odd_s, "walkers", odds)

    current, logs, info, pair_i, odd_i = call(
        update_kernel,
        (
            shape(walkers, 2, orbs, nel),
            shape(8, nel),
            shape(INFO, wide),
            shape(tall, LANES),
            shape(tall, LANES),
        ),
        [VMEM] * 6,
        us=4,
        name="update",
    )(total, got, inverse, move_order, accepted, spots)

    pair_i = lax.ppermute(pair_i, "walkers", pairs)
    odd_i = lax.ppermute(odd_i, "walkers", odds)

    inv_new, sla_new, pos_new, log_new, energy_new, mean = call(
        place_kernel,
        (
            shape(walkers, 2, orbs, nel),
            shape(walkers, 2, orbs, nel),
            shape(3, walkers, both),
            shape(1, walkers),
            shape(1, walkers),
            shape(1, 1),
        ),
        [VMEM] * 9,
        us=1.5,
        name="place",
    )(current, done, spots, logs, info, pair_s, odd_s, pair_i, odd_i)
    return (
        inv_new,
        sla_new,
        pos_new.transpose(1, 0, 2),
        log_new.reshape(walkers),
        energy_new.reshape(walkers),
        mean.reshape(()),
    )


def solution(mesh):
    return jax.shard_map(
        body,
        mesh=mesh,
        in_specs=(
            P("walkers", None, "orb", None),
            P("walkers", None, "orb", None),
            P("walkers", None, None),
            P("walkers", None, None),
            P("walkers", None, None),
            P("walkers", None, None),
            P("walkers"),
            P("walkers"),
            P(),
            P(),
            P(None, "orb", None),
            P(),
        ),
        out_specs=(
            P("walkers", None, "orb", None),
            P("walkers", None, "orb", None),
            P("walkers", None, None),
            P("walkers"),
            P("walkers"),
            P(),
        ),
        check_vma=False,
    )
```

```python
import jax
import jax.numpy as jnp
from jax import lax
from jax.experimental import pallas as pl
from jax.experimental.pallas import tpu as pltpu
from jax.sharding import PartitionSpec as P

F32 = jnp.float32
BF16 = jnp.bfloat16
VMEM = pl.BlockSpec(memory_space=pltpu.VMEM)
ANY = pl.BlockSpec(memory_space=pl.ANY)
LANES = 128
INFO = 8


def thirds(x):
    high = x.astype(BF16)
    rest = x - high.astype(F32)
    middle = rest.astype(BF16)
    low = (rest - middle.astype(F32)).astype(BF16)
    return jnp.concatenate([high, middle, low], axis=0)


def parted(x):
    high = x.astype(BF16)
    return jnp.concatenate([high, (x - high.astype(F32)).astype(BF16)], axis=0)


def product(a, b):
    rows = a.shape[0]
    inner = b.shape[0]
    left = parted(a)
    right = parted(b)
    whole = None
    for part in (right[:inner], right[inner:]):
        both = lax.dot_general(
            left, part, (((1,), (0,)), ((), ())), preferred_element_type=F32
        )
        both = both[:rows] + both[rows:]
        whole = both if whole is None else whole + both
    return whole


def product_nt(a, b):
    rows, cols = a.shape[0], b.shape[0]
    both = lax.dot_general(
        parted(a), parted(b), (((1,), (1,)), ((), ())), preferred_element_type=F32
    )
    both = both[:rows] + both[rows:]
    return both[:, :cols] + both[:, cols:]


def taken_nt(hot, x):
    rows = x.shape[0]
    parts = lax.dot_general(
        hot.astype(BF16), thirds(x), (((1,), (1,)), ((), ())), preferred_element_type=F32
    )
    return parts[:, :rows] + parts[:, rows : 2 * rows] + parts[:, 2 * rows :]


def spread(x, hot):
    hot = hot.astype(BF16)
    return lax.dot_general(
        thirds(x),
        jnp.concatenate([hot] * 3, axis=0),
        (((0,), (0,)), ((), ())),
        preferred_element_type=F32,
    )


def taken(x, hot):
    rows = x.shape[0]
    parts = lax.dot_general(
        thirds(x), hot.astype(BF16), (((1,), (1,)), ((), ())), preferred_element_type=F32
    )
    return parts[:rows] + parts[rows : 2 * rows] + parts[2 * rows :]


def turned(rows):
    short = -rows.shape[0] % 8
    if short:
        rows = jnp.concatenate([rows, jnp.zeros((short, rows.shape[1]), F32)], axis=0)
    return jnp.transpose(rows)


def moves_of(order_ref, flags_ref):
    walkers, _, moves = flags_ref.shape
    nel = order_ref.shape[2]
    order = turned(
        jnp.concatenate([order_ref[w] for w in range(walkers)], axis=0).astype(F32)
    )
    flags = jnp.concatenate([flags_ref[w] for w in range(walkers)], axis=0).astype(F32)
    flags = turned(
        jnp.concatenate([flags, jnp.zeros((2 * walkers, nel - moves), F32)], axis=1)
    )
    cols = [order[:moves, i : i + 1] for i in range(2 * walkers)]
    keep = [flags[:moves, i : i + 1] for i in range(2 * walkers)]
    return cols, keep


def one_hots(cols, nel):
    moves = cols[0].shape[0]
    lanes = lax.broadcasted_iota(jnp.int32, (moves, nel), 1).astype(F32)
    return [(c == lanes).astype(F32) for c in cols]


def limits_of(spots_ref, walkers):
    counts = spots_ref[walkers, 0:1, :]
    limits = [counts[:, :1]]
    for w in range(1, walkers):
        limits.append(limits[-1] + counts[:, w : w + 1])
    return limits


def picked(limits, index, choices):
    rows = max(x[0].shape[0] for x in choices)
    after = [
        jnp.broadcast_to(limit - index, (rows, choices[0][0].shape[1])) <= 0.0
        for limit in limits[:-1]
    ]
    out = []
    for some in choices:
        value = some[0]
        for w in range(1, len(some)):
            value = jnp.where(after[w - 1][: value.shape[0]], some[w], value)
        out.append(value)
    return out


def sent(spots_ref, walkers, pair_ref, odd_ref):
    half = walkers // 2
    limits = limits_of(spots_ref, walkers)
    parity = lax.rem(lax.axis_index("walkers"), 2)
    out = []
    for pay, up in ((pair_ref, parity == 0), (odd_ref, parity == 1)):
        up = up.astype(F32)
        out.append(
            (pay, [(limits, up * (limits[-1] - 1.0 * half) + 1.0 * j) for j in range(half)])
        )
    return out


def pair_tiles(turns, rows, nel, kinds):
    sums = [None, None]
    for h in (0, 1):
        for t in range(nel // 8):
            wide = [
                [
                    jnp.broadcast_to(turn[h][c][8 * t : 8 * t + 8], (8, nel))
                    for c in range(3)
                ]
                for turn in turns
            ]
            for g in range(h, 2):
                squares = []
                for i, row in enumerate(rows):
                    total = None
                    for c in range(3):
                        offset = wide[i][c] - row[g][c]
                        total = offset * offset if total is None else total + offset * offset
                    squares.append(total)
                kind = int(g != h)
                term = kinds[kind](*squares)
                sums[kind] = term if sums[kind] is None else sums[kind] + term
    return sums


def summed(tile):
    return jnp.sum(jnp.sum(tile, axis=0, keepdims=True), axis=1, keepdims=True)


def jastrow_of(spots, turn, jas, nel):
    rows, turns = (
        [
            [
                [cut(base + 3 * h + c) for c in range(3)]
                for h in (0, 1)
            ]
            for base in (0, 8)
        ]
        for cut in (lambda r: spots[r : r + 1], lambda r: turn[:, r : r + 1])
    )

    def change(fall):
        fall = jnp.broadcast_to(fall, (8, nel))

        def term(new, old):
            nd = jnp.sqrt(new)
            od = jnp.sqrt(old)
            return (nd - od) / ((1.0 + fall * nd) * (1.0 + fall * od))

        return term

    same, other = pair_tiles(turns, rows, nel, [change(jas[:, 2:3]), change(jas[:, 3:4])])
    return summed(same * (0.5 * jas[:, :1]) + other * jas[:, 1:2])


def in_rows(rows):
    return [r[:, at : at + LANES] for at in range(0, rows[0].shape[1], LANES) for r in rows]


def energy_kernel(
    pos_in, dis_in, order_in, flags_in, counts_in, jas_in, amp_in, spots_out, info_out,
    pos_ref, dis_ref, order_ref, flags_ref, counts_ref, jas_ref, amp_ref, spots_ref, info_ref,
    loads, stores,
):
    operands = (
        (pos_in, pos_ref),
        (dis_in, dis_ref),
        (order_in, order_ref),
        (flags_in, flags_ref),
        (counts_in, counts_ref),
        (jas_in, jas_ref),
        (amp_in, amp_ref),
    )
    copies = [pltpu.make_async_copy(a, b, loads.at[i]) for i, (a, b) in enumerate(operands)]
    for copy in copies:
        copy.start()
    for copy in copies:
        copy.wait()
    _, walkers, both = pos_ref.shape
    nel = both // 2
    cols, keep = moves_of(order_ref, flags_ref)
    hots = one_hots(cols, nel)
    applied = jnp.concatenate(
        [
            jnp.concatenate(
                [
                    jnp.sum(hots[2 * w + s] * keep[2 * w + s], axis=0, keepdims=True)
                    for s in (0, 1)
                ],
                axis=1,
            )
            for w in range(walkers)
        ],
        axis=0,
    )
    now = [pos_ref[c] + dis_ref[c] * applied for c in range(3)]
    turn = turned(jnp.concatenate(now, axis=0))
    weighted = jnp.zeros((1, nel), F32)
    counts = counts_ref[...].astype(F32)
    for w in range(walkers):
        nrows = [now[c][w : w + 1] for c in range(3)]
        halves = [[r[:, h * nel : (h + 1) * nel] for r in nrows] for h in (0, 1)]
        tall = [
            [
                turn[h * nel : (h + 1) * nel, c * walkers + w : c * walkers + w + 1]
                for c in range(3)
            ]
            for h in (0, 1)
        ]
        same, other = pair_tiles([tall], [halves], nel, [lambda q: lax.rsqrt(q + 1.0)] * 2)
        soft = jnp.sum(same + 2.0 * other, axis=0, keepdims=True)
        wide = [soft, jnp.zeros((7 - 3 * (both // LANES), LANES), F32)]
        spots_ref[w, :8] = jnp.concatenate(in_rows(nrows) + wide[: 1 + (3 * (both // LANES) < 7)], axis=0)
        spots_ref[w, 8 : 8 + 3 * (both // LANES)] = jnp.concatenate(
            in_rows([pos_ref[c, w : w + 1] for c in range(3)]), axis=0
        )
        weighted = weighted + soft * counts[:, w : w + 1]
    me = lax.axis_index("walkers")
    lanes = lax.broadcasted_iota(jnp.int32, info_ref.shape, 1)
    rows = lax.broadcasted_iota(jnp.int32, info_ref.shape, 0)
    spots_ref[walkers] = jnp.zeros(spots_ref.shape[1:], F32)
    for row, some in enumerate((counts, jas_ref[...], amp_ref[...])):
        spots_ref[walkers, row : row + 1, : some.shape[1]] = some
    number = jnp.sum(counts, axis=1, keepdims=True)
    info_ref[...] = jnp.where((lanes == me) & (rows == 0), number, 0.0)
    info_ref[1:2, :nel] = weighted
    copies = [
        pltpu.make_async_copy(info_ref, info_out, stores.at[0]),
        pltpu.make_async_copy(spots_ref, spots_out, stores.at[1]),
    ]
    for copy in copies:
        copy.start()
    for copy in copies:
        copy.wait()


def shift_kernel(
    pos_ref, dis_ref, order_ref, flags_ref, cen_ref, exp_ref, orb_ref, shift_ref, differ_ref,
):
    _, walkers, both = pos_ref.shape
    nel = both // 2
    moves = flags_ref.shape[2]
    basis = cen_ref.shape[1]
    cols, _ = moves_of(order_ref, flags_ref)
    hots = one_hots(cols, nel)
    rows = [ref[c] for ref in (pos_ref, dis_ref) for c in range(3)]
    rows = jnp.concatenate(rows + [jnp.zeros((-6 * walkers % 16, both), F32)] * (6 * walkers % 16 > 0), axis=0)
    for s in (0, 1):
        points = taken_nt(
            jnp.concatenate([hots[2 * w + s] for w in range(walkers)], axis=0),
            rows[:, s * nel : (s + 1) * nel],
        )
        for w in range(walkers):
            mine = points[w * moves : (w + 1) * moves]
            old = []
            new = []
            for c in range(3):
                at = c * walkers + w
                to = (3 + c) * walkers + w
                spot = mine[:, at : at + 1]
                old.append(jnp.broadcast_to(spot, (moves, LANES)))
                new.append(jnp.broadcast_to(spot + mine[:, to : to + 1], (moves, LANES)))
            for j in range(0, basis, LANES):
                osq = None
                nsq = None
                for c in range(3):
                    row = cen_ref[c : c + 1, j : j + LANES]
                    do = old[c] - row
                    dn = new[c] - row
                    osq = do * do if osq is None else osq + do * do
                    nsq = dn * dn if nsq is None else nsq + dn * dn
                rate = -exp_ref[:, j : j + LANES]
                differ_ref[s, w * moves : (w + 1) * moves, j : j + LANES] = jnp.exp(
                    rate * nsq
                ) - jnp.exp(rate * osq)
    for s in (0, 1):
        shift_ref[s] = product_nt(differ_ref[s], orb_ref[s])


def partial_kernel(
    shift_ref, order_ref, flags_ref, inv_ref, sla_ref, spots_ref,
    part_ref, done_ref, pair_ref, odd_ref,
):
    walkers, _, orbs, nel = inv_ref.shape
    moves = flags_ref.shape[2]
    cols, keep = moves_of(order_ref, flags_ref)
    hots = one_hots(cols, nel)
    members = lax.axis_size("orb")
    share = walkers // members
    first = lax.axis_index("orb") * share
    tail = 2 * walkers * moves
    part_ref[tail:, :] = jnp.zeros((part_ref.shape[0] - tail, part_ref.shape[1]), F32)
    jas = spots_ref[walkers, 1:2, :]
    for w in range(share):
        mine = spots_ref[first + w]
        at = tail + 2 + first + w
        part_ref[pl.ds(at, 1), :] = jnp.broadcast_to(
            jastrow_of(mine, turned(mine), jas, nel), (1, part_ref.shape[1])
        )
    for s in (0, 1):
        for w in range(walkers):
            i = 2 * w + s
            mine = shift_ref[s, w * moves : (w + 1) * moves, :]
            proposed = mine + taken_nt(hots[i], sla_ref[w, s])
            part = product(proposed, inv_ref[w, s])
            part_ref[i * moves : (i + 1) * moves, :] = part * keep[i]
            done_ref[w, s] = sla_ref[w, s] + spread(mine, hots[i] * keep[i])
    half = walkers // 2
    per = 2 * orbs
    tail = half * per
    for pay, indices in sent(spots_ref, walkers, pair_ref, odd_ref):
        for j, (limits, index) in enumerate(indices):
            rows = picked(
                limits,
                index,
                [[done_ref[w, s] for w in range(walkers)] for s in (0, 1)]
                + [[spots_ref[w, :8] for w in range(walkers)]],
            )
            for s in (0, 1):
                pay[j * per + s * orbs : j * per + (s + 1) * orbs, :] = rows[s]
            pay[tail + 8 * j : tail + 8 * j + 8, :] = rows[2]


def join_kernel(part_ref, info_ref, out_ref):
    rows = part_ref.shape[0] - info_ref.shape[0]
    out_ref[:rows, :] = part_ref[:rows, :]
    out_ref[rows:, :] = part_ref[rows:, :] + info_ref[...]


def add_kernel(mine_ref, other_ref, out_ref):
    out_ref[...] = mine_ref[...] + other_ref[...]


def update_kernel(
    sum_ref, got_ref, inv_ref, order_ref, flags_ref, spots_ref,
    cur_ref, log_ref, info_ref, pair_ref, odd_ref,
):
    walkers, _, orbs, nel = inv_ref.shape
    moves = flags_ref.shape[2]
    count = 2 * walkers
    cols, keep = moves_of(order_ref, flags_ref)
    hots = one_hots(cols, nel)
    eye = (
        lax.broadcasted_iota(jnp.int32, (moves, moves), 0)
        == lax.broadcasted_iota(jnp.int32, (moves, moves), 1)
    ).astype(F32)
    tiles = moves // 8
    left = []
    right = []
    columns = []
    for i in range(count):
        at = slice(i * moves, (i + 1) * moves)
        change = sum_ref[at, :] + got_ref[at, :] - hots[i] * keep[i]
        coupling = taken(change, hots[i]) + eye
        columns.append(taken(inv_ref[i // 2, i % 2], hots[i]))
        left.append([coupling[8 * t : 8 * t + 8] for t in range(tiles)])
        right.append([change[8 * t : 8 * t + 8] for t in range(tiles)])
    info_ref[...] = sum_ref[count * moves :, :] + got_ref[count * moves :, :]
    lanes = lax.broadcasted_iota(jnp.int32, (1, nel), 1)
    sub = lax.broadcasted_iota(jnp.int32, (8, nel), 0)
    pivots = [jnp.ones((1, nel), F32) for _ in range(count)]
    for k in range(0, moves, 2):
        own, line = k // 8, k % 8
        for i in range(count):
            wide = [
                [jnp.broadcast_to(left[i][t][:, c : c + 1], (8, nel)) for t in range(tiles)]
                for c in (k, k + 1)
            ]
            a, b = (wide[c][own][line : line + 1] for c in (0, 1))
            c, d = (wide[c][own][line + 1 : line + 2] for c in (0, 1))
            det = a * d - b * c
            pivots[i] = jnp.where(lanes == k, det, pivots[i])
            scale = 1.0 / det
            new = []
            for side, width in ((left, moves), (right, nel)):
                upper = side[i][own][line : line + 1]
                lower = side[i][own][line + 1 : line + 2]
                new.append(
                    (
                        (d[:, :width] * upper - b[:, :width] * lower) * scale[:, :width],
                        (a[:, :width] * lower - c[:, :width] * upper) * scale[:, :width],
                    )
                )
            for t in range(tiles):
                sides = ((right, nel, new[1]), (left, moves, new[0]))
                for side, width, (upper, lower) in sides[: 1 + (k + 2 < moves)]:
                    tile = (
                        side[i][t] - wide[0][t][:, :width] * upper - wide[1][t][:, :width] * lower
                    )
                    if t == own:
                        tile = jnp.where(
                            sub[:, :width] == line,
                            upper,
                            jnp.where(sub[:, :width] == line + 1, lower, tile),
                        )
                    side[i][t] = tile
    for i in range(count):
        solved = jnp.concatenate(right[i], axis=0)
        cur_ref[i // 2, i % 2] = inv_ref[i // 2, i % 2] - product(columns[i], solved)
    log_ref[...] = jnp.zeros(log_ref.shape, F32)
    for w in range(walkers):
        both = jnp.log(jnp.abs(pivots[2 * w])) + jnp.log(jnp.abs(pivots[2 * w + 1]))
        log_ref[w : w + 1, :] = (
            jnp.broadcast_to(jnp.sum(both, axis=1, keepdims=True), (1, nel))
            + info_ref[2 + w : 3 + w, :nel]
            + spots_ref[walkers, 2:3, w : w + 1]
        )
    half = walkers // 2
    per = 2 * orbs
    tail = half * per
    for pay, indices in sent(spots_ref, walkers, pair_ref, odd_ref):
        pay[tail : tail + INFO, :] = info_ref[...]
        pay[tail + INFO :, :] = jnp.zeros((pay.shape[0] - tail - INFO, LANES), F32)
        for j, (limits, index) in enumerate(indices):
            rows = picked(
                limits,
                index,
                [[cur_ref[w, s] for w in range(walkers)] for s in (0, 1)]
                + [[log_ref[w : w + 1, :] for w in range(walkers)]],
            )
            for s in (0, 1):
                pay[j * per + s * orbs : j * per + (s + 1) * orbs, :] = rows[s]
            pay[tail + INFO + j : tail + INFO + j + 1, :] = rows[2]


def place_kernel(
    cur_ref, done_ref, spots_ref, log_ref, info_ref,
    pair_s_ref, odd_s_ref, pair_i_ref, odd_i_ref,
    inv_out, sla_out, pos_out, log_out, energy_out, mean_out,
):
    walkers, _, orbs, nel = cur_ref.shape
    width = pos_out.shape[2] // LANES
    half = walkers // 2
    per = 2 * orbs
    tail = half * per
    me = lax.axis_index("walkers")
    parity = lax.rem(me, 2)
    info = info_ref[...] + pair_i_ref[tail : tail + INFO, :]
    lanes = lax.broadcasted_iota(jnp.int32, (1, info.shape[1]), 1)
    before = jnp.sum(jnp.where(lanes < me, info[0:1], 0.0), axis=1, keepdims=True)
    groups = lax.axis_size("walkers")
    both = pos_out.shape[2]

    def energy_of(row, copies):
        soft = jnp.sum(row, axis=1, keepdims=True)
        return (soft - 1.0 * both * copies) / (1.0 * both * (both - 1))

    copies = jnp.sum(info[0:1], axis=1, keepdims=True)
    mean_out[...] = energy_of(info[1:2], copies) / (1.0 * walkers * groups)
    limits = limits_of(spots_ref, walkers)
    slots = lax.broadcasted_iota(jnp.int32, (1, walkers), 1)
    here = [[cur_ref[w, s] for w in range(walkers)] for s in (0, 1)]
    here += [[done_ref[w, s] for w in range(walkers)] for s in (0, 1)]
    here += [[spots_ref[w, :8] for w in range(walkers)]]
    here += [[log_ref[w : w + 1, :] for w in range(walkers)]]
    odd = parity.astype(F32)
    log_new = jnp.zeros((1, walkers), F32)
    energy_new = jnp.zeros((1, walkers), F32)
    for j in range(walkers):
        index = (1.0 * walkers) * me.astype(F32) + 1.0 * j - before
        own = picked(limits, index, here)
        low = j < half
        outside = -index if low else index - limits[-1] + 1.0
        entry = index + 1.0 * half if low else index - limits[-1]
        on_pair = odd if low else 1.0 - odd
        shape_here = (orbs, nel)
        away = jnp.broadcast_to(outside, shape_here) > 0.0
        second = jnp.broadcast_to(entry, shape_here) > 0.5
        pair = jnp.broadcast_to(on_pair, shape_here) > 0.5

        def one(late, at, rows):
            parts = []
            for i in range(half):
                start = at(i)
                a, b = (ref[start : start + rows, :] for ref in late)
                parts.append(jnp.where(pair[:rows], a, b))
            value = parts[0]
            for i in range(1, half):
                again = second if i == 1 else jnp.broadcast_to(entry, shape_here) > i - 0.5
                value = jnp.where(again[:rows], parts[i], value)
            return value

        inverses = (pair_i_ref, odd_i_ref)
        slaters = (pair_s_ref, odd_s_ref)
        got = [one(inverses, lambda i, s=s: i * per + s * orbs, orbs) for s in (0, 1)]
        got += [one(slaters, lambda i, s=s: i * per + s * orbs, orbs) for s in (0, 1)]
        got += [one(slaters, lambda i: tail + 8 * i, 8)]
        got += [one(inverses, lambda i: tail + INFO + i, 1)]
        new = [jnp.where(away[: o.shape[0]], g, o) for o, g in zip(own, got)]
        for s in (0, 1):
            inv_out[j, s] = new[s]
            sla_out[j, s] = new[2 + s]
        for c in range(3):
            for h in range(width):
                pos_out[c, j : j + 1, h * LANES : (h + 1) * LANES] = new[4][
                    3 * h + c : 3 * h + c + 1
                ]
        log_new = jnp.where(slots == j, new[5][:, :walkers], log_new)
        energy_new = jnp.where(
            slots == j, energy_of(new[4][3 * width : 3 * width + 1], 1.0), energy_new
        )
    log_out[...] = log_new
    energy_out[...] = energy_new


def call(kernel, outs, in_specs, scratch=(), us=1.0, name=None, out_specs=None, vmem=32 * 2**20):
    return pl.pallas_call(
        kernel,
        out_shape=outs,
        in_specs=in_specs,
        out_specs=out_specs or jax.tree.map(lambda _: VMEM, outs),
        scratch_shapes=list(scratch),
        compiler_params=pltpu.CompilerParams(vmem_limit_bytes=vmem),
        cost_estimate=pl.CostEstimate(flops=int(us * 1.1e9), bytes_accessed=2**18, transcendentals=0),
        name=name,
    )


def shape(*dims):
    return jax.ShapeDtypeStruct(dims, F32)


def body(
    inverse, slater, positions, displacements, move_order, accepted, counts, log_amp, centers,
    exponents, orbitals, jastrow,
):
    walkers, _, orbs, nel = inverse.shape
    moves = accepted.shape[2]
    both = positions.shape[2]
    basis = centers.shape[1]
    groups = lax.axis_size("walkers")
    members = lax.axis_size("orb")
    wide = max(LANES, groups)
    half = walkers // 2
    per = 2 * orbs
    count = 2 * walkers
    tall = half * per + 16

    counts = counts.reshape(1, walkers)
    log_amp = log_amp.reshape(1, walkers)
    jastrow = jastrow.reshape(1, jastrow.shape[0])

    pairs = [(i, i ^ 1) for i in range(groups)]
    odds = [(i, i + 1) for i in range(1, groups - 1, 2)]
    odds = odds + [(b, a) for a, b in odds]

    places = positions.transpose(1, 0, 2)
    steps = displacements.transpose(1, 0, 2)
    operands = (places, steps, move_order, accepted, counts, jastrow, log_amp)
    made = (shape(walkers + 1, 16, LANES), shape(INFO, wide))
    spots, info = call(
        energy_kernel,
        made,
        [ANY] * len(operands),
        out_specs=(ANY, ANY),
        scratch=[pltpu.VMEM(x.shape, x.dtype) for x in operands + made]
        + [pltpu.SemaphoreType.DMA((len(operands),)), pltpu.SemaphoreType.DMA((len(made),))],
        us=2,
        vmem=61 * 2**20,
        name="energy",
    )(*operands)

    hops = members * 2
    step = hops
    while step < groups:
        info = info + lax.ppermute(info, "walkers", [(i, i ^ step) for i in range(groups)])
        step *= 2
    joint = [
        (d * members + o, (d ^ (2 * hop)) * members + o)
        for o in range(members)
        for hop in [(1, 3, 0, 2)[o] if members == 4 else o]
        for d in range(groups)
        if 2 * hop < groups
    ]
    info = lax.ppermute(info, ("walkers", "orb"), joint)

    shift = call(
        shift_kernel,
        shape(2, walkers * moves, orbs),
        [VMEM] * 7,
        scratch=[pltpu.VMEM((2, walkers * moves, basis), F32)],
        us=3,
        name="shift",
    )(
        places, steps, move_order, accepted, centers, exponents.reshape(1, basis), orbitals,
    )

    part, done, pair_s, odd_s = call(
        partial_kernel,
        (
            shape(count * moves + INFO, nel),
            shape(walkers, 2, orbs, nel),
            shape(tall, LANES),
            shape(tall, LANES),
        ),
        [VMEM] * 6,
        us=2,
        name="partial",
    )(shift, move_order, accepted, inverse, slater, spots)

    part = call(
        join_kernel, shape(count * moves + INFO, nel), [VMEM] * 2, us=0.2, name="join"
    )(part, info)

    total = part
    got = jnp.zeros_like(part)
    step = 1
    while step < members:
        partner = [(o, o ^ step) for o in range(members)]
        got = lax.ppermute(total, "orb", partner)
        if 2 * step < members:
            total = call(
                add_kernel,
                shape(count * moves + INFO, nel),
                [VMEM] * 2,
                us=0.5,
                name="add",
            )(total, got)
        step *= 2

    pair_s = lax.ppermute(pair_s, "walkers", pairs)
    odd_s = lax.ppermute(odd_s, "walkers", odds)

    current, logs, info, pair_i, odd_i = call(
        update_kernel,
        (
            shape(walkers, 2, orbs, nel),
            shape(8, nel),
            shape(INFO, wide),
            shape(tall, LANES),
            shape(tall, LANES),
        ),
        [VMEM] * 6,
        us=4,
        name="update",
    )(total, got, inverse, move_order, accepted, spots)

    pair_i = lax.ppermute(pair_i, "walkers", pairs)
    odd_i = lax.ppermute(odd_i, "walkers", odds)

    inv_new, sla_new, pos_new, log_new, energy_new, mean = call(
        place_kernel,
        (
            shape(walkers, 2, orbs, nel),
            shape(walkers, 2, orbs, nel),
            shape(3, walkers, both),
            shape(1, walkers),
            shape(1, walkers),
            shape(1, 1),
        ),
        [VMEM] * 9,
        us=1.5,
        name="place",
    )(current, done, spots, logs, info, pair_s, odd_s, pair_i, odd_i)
    return (
        inv_new,
        sla_new,
        pos_new.transpose(1, 0, 2),
        log_new.reshape(walkers),
        energy_new.reshape(walkers),
        mean.reshape(()),
    )


def solution(mesh):
    return jax.shard_map(
        body,
        mesh=mesh,
        in_specs=(
            P("walkers", None, "orb", None),
            P("walkers", None, "orb", None),
            P("walkers", None, None),
            P("walkers", None, None),
            P("walkers", None, None),
            P("walkers", None, None),
            P("walkers"),
            P("walkers"),
            P(),
            P(),
            P(None, "orb", None),
            P(),
        ),
        out_specs=(
            P("walkers", None, "orb", None),
            P("walkers", None, "orb", None),
            P("walkers", None, None),
            P("walkers"),
            P("walkers"),
            P(),
        ),
        check_vma=False,
    )
```
